32 devices in a mesh: lat: 4 (over z), lon: 8 (over y, x, core).
Axes of the slice: x: 2, y: 2, z: 4, core: 2. Of those that a mesh axis runs over, the one named last changes fastest.
Arguments:
- state: bfloat16 [32, 3072, 128], P('lat', 'lon'), may hold values from -6 to 6
- forcing: bfloat16 [32, 3072, 128], P('lat', 'lon'), may hold values from -4 to 4
- cotangent: bfloat16 [32, 3072, 128], P('lat', 'lon'), may hold values from -6 to 6
- land_mask: int32 [32, 3072], P('lat', 'lon'), may hold values 0 or 1
- dw_weight: bfloat16 [7, 7, 128], replicated, may hold values from -0.875 to 0.875
- dw_bias: float32 [128], replicated, may hold values from -3 to 3
- norm_gain: float32 [128], replicated, may hold values from 0.5 to 1.5
- norm_bias: float32 [128], replicated, may hold values from -3 to 3
- up_weight: bfloat16 [128, 512], replicated, may hold values from -0.5 to 0.5
- up_bias: float32 [512], replicated, may hold values from -3 to 3
- down_weight: bfloat16 [512, 128], replicated, may hold values from -0.25 to 0.25
- down_bias: float32 [128], replicated, may hold values from -3 to 3
- layer_scale: float32 [128], replicated, may hold values from 0.3 to 1
- owner: int32 [196608, 1], P(('lat', 'lon')), may hold values from 0 to 31; in each aligned block of 6144 rows (0 to 6143, 6144 to 12287, ...) at most 384 rows name the same one
- atmos_cell: int32 [196608], P(('lat', 'lon')), may hold values from 0 to 511
- weight_index: int32 [196608], P(('lat', 'lon')), may hold values from 0 to 15
- intersection_weights: float32 [16], replicated, may hold values from 0.1 to 1
Outputs:
- result: bfloat16 [32, 3072, 128], P('lat', 'lon')
- grad_dw: float32 [7, 7, 128], replicated
- grad_up: float32 [128, 512], replicated
- grad_down: float32 [512, 128], replicated
- forcing_grad: float32 [16384, 128], P(('lat', 'lon'))
The draws below stay inside these ranges and needn't reach their ends.
Inputs may be any that keep to these rules, and one draw needn't show every extreme that they name: At most 384 entries of one device name the same owner, and in every draw some device's entries name some owner exactly 384 times.
All inputs are finite; a program needn't handle non-finite values. No bound on the sum of `land_mask` on one device may be relied on, other than what follows from the above.
Results may differ from the reference program's by a relative error of at most 0.0071.
Values may be sent and summed in bfloat16 or wider, within the bound.
No kernel may reach another device: no remote copies, remote signals or barrier semaphores. Data moves between devices by JAX's collectives and lax.ppermute only.
A program may use at most 128 MiB of HBM per device.

```python
import math
import jax
import jax.numpy as jnp
import numpy as np
from jax import lax

C = 128
HID = 512
KS = 7
NW = 16
CLAT = 8
CLON = 384
A_DEV = 512
NLAT = 32
NLON = 3072
ENT_DEV = 6144
ENTRIES = 196608
ATMOS = 16384
CAP = 384
N_LAT = 4
N_LON = 8
DEVICES = 32


def touch_ends(array, stream_key, low, high):
    longest = array.shape.index(max(array.shape))
    spots = []
    for shift in (0, 1):
        where = [jax.random.randint(jax.random.fold_in(stream_key, axis), (), 0, length) for axis, length in enumerate(array.shape)]
        where[longest] = (where[longest] + shift) % array.shape[longest]
        spots.append(tuple(where))
    return array.at[spots[0]].set(low).at[spots[1]].set(high)


def block_levels(own_key, extent, split, low, largest):
    loudness = 1.0
    for axis_at, shards_of in split:
        heights = jax.random.uniform(jax.random.fold_in(jax.random.fold_in(own_key, 6), axis_at), (shards_of,), jnp.float32, low / len(split), largest / len(split))
        loudness = loudness * jnp.repeat(jnp.exp(heights), extent[axis_at] // shards_of).reshape((-1,) + (1,) * (len(extent) - 1 - axis_at))
    return loudness


def shared_out(key, own, number, rows, count, top, bound, skew):
    order = jax.random.permutation(key, count)
    packed, ordinary = load_shares(count, rows * top, bound, skew, True), load_shares(count, rows * top, bound, skew, False)
    places = jnp.arange(count)

    def named(tallies, offset_by):
        used = int((tallies > 0).sum())
        fixed = max(1, used // 4)
        passed = fixed + (places - fixed + offset_by * (used - fixed)) % max(1, count - fixed)
        return jnp.zeros((count,), jnp.int32).at[order[jnp.where(places < fixed, places, passed)]].set(jnp.asarray(tallies, jnp.int32))

    tallies = jnp.where(number % 4 == 0, named(packed, number // 4), named(ordinary, number - number // 4 - 1))
    mixed = jax.random.permutation(jax.random.fold_in(own, 3), count)
    donor, receiver = mixed[0:count // 2 * 2:2], mixed[1:count // 2 * 2:2]
    slack = jnp.minimum(tallies[donor] - 1, bound - tallies[receiver]) // 2
    slack = jnp.where((donor == order[0]) | (receiver == order[0]) | (tallies[receiver] == 0), 0, jnp.maximum(slack, 0))
    passed = jax.random.randint(jax.random.fold_in(own, 4), (count // 2,), 0, 1 << 20) % (slack + 1)
    tallies = tallies.at[donor].add(-passed).at[receiver].add(passed)
    items = jnp.searchsorted(jnp.cumsum(tallies), jnp.arange(rows * top), side="right").astype(jnp.int32)
    grid = items.reshape(top, rows).T
    grid = grid[jax.random.permutation(jax.random.fold_in(own, 1), rows)]
    offset_by = jax.random.randint(jax.random.fold_in(own, 2), (rows, 1), 0, top)
    return jnp.take_along_axis(grid, (jnp.arange(top)[None, :] + offset_by) % top, axis=1)


def load_shares(amount, total, limit, skew, full):
    portions = [(1 << 20) // math.isqrt(rank ** skew) + 1 for rank in range(1, amount + 1)]
    largest = limit if full else min(limit, max(-(-total // amount), total * portions[0] // sum(portions)))
    least = 1 if total - largest >= amount - 1 else 0
    counts, surplus = [largest] + [least] * (amount - 1), total - largest - least * (amount - 1)
    while surplus > 0:
        candidates = [i for i in range(1, amount) if counts[i] < largest] or [i for i in range(1, amount) if counts[i] < limit]
        whole, remaining = sum([portions[i] for i in candidates]), surplus
        for i in candidates:
            addition = min(limit - counts[i], max(1, remaining * portions[i] // whole), surplus)
            counts[i] = counts[i] + addition
            surplus = surplus - addition
    return np.array(counts)


def bell_draw(rng, extent, spread, bound, pieces=(), held_as=jnp.bfloat16):
    array = jax.random.normal(rng, extent, jnp.float32) * spread
    if len(pieces) > 0:
        array = block_levels(rng, extent, pieces, -0.22, 0.18) * array
    return jnp.clip(array, min=-bound, max=bound).astype(held_as)


def setup_inputs(seed: int = 0) -> dict:
    splits = jax.random.split(jax.random.key(seed), 18)
    state = bell_draw(splits[0], (NLAT, NLON, C), 1.0, 6.0, ((0, 4), (1, 8)))
    forcing = bell_draw(splits[1], (NLAT, NLON, C), 0.5, 4.0, ((0, 4), (1, 8)))
    cotangent = bell_draw(splits[2], (NLAT, NLON, C), 1.0, 6.0, ((0, 4), (1, 8)))
    land_mask = touch_ends((jax.random.randint(splits[3], (NLAT, NLON), 0, 10) < 7).astype(jnp.int32), jax.random.fold_in(splits[3], 1), 0, 1)
    dw_weight = bell_draw(splits[4], (KS, KS, C), (KS * KS) ** -0.5, 0.875)
    dw_bias = bell_draw(splits[5], (C,), 0.5, 3.0, (), jnp.float32)
    norm_gain = jnp.clip(jax.random.uniform(splits[6], (C,), jnp.float32, 0.5, 1.5), 0.5, 1.5)
    norm_bias = bell_draw(splits[7], (C,), 0.5, 3.0, (), jnp.float32)
    up_weight = bell_draw(splits[8], (C, HID), C ** -0.5, 0.5)
    up_bias = bell_draw(splits[9], (HID,), 0.5, 3.0, (), jnp.float32)
    down_weight = bell_draw(splits[10], (HID, C), HID ** -0.5, 0.25)
    down_bias = bell_draw(splits[11], (C,), 0.5, 3.0, (), jnp.float32)
    layer_scale = jnp.clip(jnp.exp(jax.random.uniform(splits[12], (C,), jnp.float32, math.log(0.3), math.log(1.0))), 0.3, 1.0)
    owner_keys = jax.random.split(jax.random.fold_in(splits[13], 1), ENTRIES // ENT_DEV)
    owner_turns = jax.random.permutation(jax.random.fold_in(splits[13], 3), ENTRIES // ENT_DEV)
    owner = jax.vmap(lambda own, number: shared_out(jax.random.fold_in(splits[13], 2), own, number, ENT_DEV, DEVICES, 1, CAP, 2))(owner_keys, owner_turns).reshape((ENTRIES, 1))
    atmos_cell = touch_ends(jax.random.randint(splits[14], (ENTRIES,), 0, A_DEV), jax.random.fold_in(splits[14], 1), 0, A_DEV - 1).astype(jnp.int32)
    weight_index = touch_ends(jax.random.randint(splits[15], (ENTRIES,), 0, NW), jax.random.fold_in(splits[15], 1), 0, NW - 1).astype(jnp.int32)
    intersection_weights = jnp.clip(jnp.exp(jax.random.uniform(splits[16], (NW,), jnp.float32, math.log(0.1), math.log(1.0))), 0.1, 1.0)
    return {"state": state, "forcing": forcing, "cotangent": cotangent, "land_mask": land_mask, "dw_weight": dw_weight, "dw_bias": dw_bias, "norm_gain": norm_gain, "norm_bias": norm_bias, "up_weight": up_weight, "up_bias": up_bias, "down_weight": down_weight, "down_bias": down_bias, "layer_scale": layer_scale, "owner": owner, "atmos_cell": atmos_cell, "weight_index": weight_index, "intersection_weights": intersection_weights}


gelu_scale = 0.7978845608028654
cubic_coef = 0.044715

def gelu_pair(pre):
    inner = gelu_scale * (pre + cubic_coef * pre * pre * pre)
    tanh_value = jnp.tanh(inner)
    value = 0.5 * pre * (1.0 + tanh_value)
    slope = 0.5 * (1.0 + tanh_value) + 0.5 * pre * (1.0 - tanh_value * tanh_value) * gelu_scale * (1.0 + 3.0 * cubic_coef * pre * pre)
    return (value, slope)

def depthwise(padded, kernel):
    channels = padded.shape[-1]
    convolved = lax.conv_general_dilated(padded[None], kernel[:, :, None, :], (1, 1), 'VALID', dimension_numbers=('NHWC', 'HWIO', 'NHWC'), feature_group_count=channels, preferred_element_type=jnp.float32)
    return convolved[0]

def block_pass(padded, state, forcing, cotangent, land, dw_weight, dw_bias, norm_gain, norm_bias, up_weight, up_bias, down_weight, down_bias, layer_scale):
    tile_rows, tile_cols, channels = state.shape
    conv = depthwise(padded, dw_weight) + dw_bias
    average = lax.optimization_barrier(jnp.mean(conv, axis=-1, keepdims=True))
    centred = conv - average
    variance = lax.optimization_barrier(jnp.mean(centred * centred, axis=-1, keepdims=True))
    inv_std = lax.rsqrt(variance + 1e-06)
    normed = centred * inv_std
    mixed = (normed * norm_gain + norm_bias + forcing.astype(jnp.float32)).astype(jnp.bfloat16)
    flat = mixed.reshape(-1, channels)
    pre = jnp.dot(flat, up_weight, preferred_element_type=jnp.float32) + up_bias
    activated, slope = gelu_pair(pre)
    hidden = activated.astype(jnp.bfloat16)
    projected = jnp.dot(hidden, down_weight, preferred_element_type=jnp.float32) + down_bias
    ocean = land.astype(jnp.float32).reshape(-1, 1)
    result = (ocean * (state.reshape(-1, channels).astype(jnp.float32) + layer_scale * projected)).astype(jnp.bfloat16)
    grad_out = (ocean * layer_scale * cotangent.reshape(-1, channels).astype(jnp.float32)).astype(jnp.bfloat16)
    down_term = jnp.dot(hidden.T, grad_out, preferred_element_type=jnp.float32)
    grad_hidden = jnp.dot(grad_out, down_weight.T, preferred_element_type=jnp.float32)
    grad_pre = (grad_hidden * slope).astype(jnp.bfloat16)
    up_term = jnp.dot(flat.T, grad_pre, preferred_element_type=jnp.float32)
    grad_mixed = jnp.dot(grad_pre, up_weight.T, preferred_element_type=jnp.float32).reshape(tile_rows, tile_cols, channels)
    gained = grad_mixed * norm_gain
    grad_conv = (inv_std * (gained - lax.optimization_barrier(jnp.mean(gained, axis=-1, keepdims=True)) - normed * lax.optimization_barrier(jnp.mean(gained * normed, axis=-1, keepdims=True)))).astype(jnp.bfloat16)
    conv_term = depthwise(padded, grad_conv)
    return (result.reshape(tile_rows, tile_cols, channels), grad_mixed, conv_term, up_term, down_term)

def pad_grid(state, margin):
    lon_padded = jnp.concatenate([state[:, -margin:], state, state[:, :margin]], axis=1)
    below = jnp.zeros((margin,) + lon_padded.shape[1:], state.dtype)
    above = lon_padded[-margin:][::-1, ::-1]
    return jnp.concatenate([below, lon_padded, above], axis=0)

def reference(state, forcing, cotangent, land_mask, dw_weight, dw_bias, norm_gain, norm_bias, up_weight, up_bias, down_weight, down_bias, layer_scale, owner, atmos_cell, weight_index, intersection_weights):
    margin = KS // 2
    padded = pad_grid(state, margin)
    band_rows = 4
    band_count = NLAT // band_rows

    def band_step(totals, block_id):
        start = block_id * band_rows
        pad_rows = lax.dynamic_slice_in_dim(padded, start, band_rows + 2 * margin, 0)
        state_rows = lax.dynamic_slice_in_dim(state, start, band_rows, 0)
        forcing_rows = lax.dynamic_slice_in_dim(forcing, start, band_rows, 0)
        cot_rows = lax.dynamic_slice_in_dim(cotangent, start, band_rows, 0)
        land_rows = lax.dynamic_slice_in_dim(land_mask, start, band_rows, 0)
        result, grad_mixed, conv_term, up_term, down_term = block_pass(pad_rows, state_rows, forcing_rows, cot_rows, land_rows, dw_weight, dw_bias, norm_gain, norm_bias, up_weight, up_bias, down_weight, down_bias, layer_scale)
        return ((totals[0] + conv_term, totals[1] + up_term, totals[2] + down_term), (result, grad_mixed))
    zeros_init = (jnp.zeros((KS, KS, C), jnp.float32), jnp.zeros((C, HID), jnp.float32), jnp.zeros((HID, C), jnp.float32))
    totals, (results, grad_bands) = lax.scan(band_step, zeros_init, jnp.arange(band_count, dtype=jnp.int32))
    scale = float(NLAT * NLON) ** (-0.5)
    grad_dw = totals[0] * scale
    grad_up = totals[1] * scale
    grad_down = totals[2] * scale
    result = results.reshape(NLAT, NLON, C)
    tiles = grad_bands.reshape(N_LAT, CLAT, N_LON, CLON, C)
    table_hit = weight_index[:, None] == jnp.arange(NW, dtype=jnp.int32)[None, :]
    entry_weights = lax.optimization_barrier(jnp.sum(jnp.where(table_hit, intersection_weights[None, :], 0.0), axis=1))
    owners = owner[:, 0]

    def regrid_step(total, device_id):
        band = lax.dynamic_index_in_dim(tiles, device_id // N_LON, 0, keepdims=False)
        device_tile = lax.dynamic_index_in_dim(band, device_id % N_LON, 1, keepdims=False)
        per_entry = jnp.repeat(device_tile.reshape(CLAT * CLON, C), 2, axis=0)
        offset = device_id * ENT_DEV
        weights_here = lax.dynamic_slice_in_dim(entry_weights, offset, ENT_DEV)
        rounded = (weights_here[:, None] * per_entry).astype(jnp.bfloat16)
        rounded = lax.optimization_barrier(rounded).astype(jnp.float32)
        targets = lax.dynamic_slice_in_dim(owners, offset, ENT_DEV) * A_DEV + lax.dynamic_slice_in_dim(atmos_cell, offset, ENT_DEV)
        return (total.at[targets].add(rounded), None)
    forcing_grad, _ = lax.scan(regrid_step, jnp.zeros((ATMOS, C), jnp.float32), jnp.arange(DEVICES, dtype=jnp.int32))
    return (result, grad_dw, grad_up, grad_down, forcing_grad)
```

```python
import functools

import jax
import jax.numpy as jnp
from jax import lax
from jax.experimental import pallas as pl
from jax.experimental.pallas import tpu as pltpu
from jax.sharding import PartitionSpec as P

A_DEV = 512
PAD = 8
BATCH = 16
gelu_scale = 0.7978845608028654
cubic_coef = 0.044715
f32 = jnp.float32
bf16 = jnp.bfloat16


def params(limit=56 << 20):
    return pltpu.CompilerParams(vmem_limit_bytes=limit)


def vmem():
    return pl.BlockSpec(memory_space=pltpu.VMEM)


def smem():
    return pl.BlockSpec(memory_space=pltpu.SMEM)


def gelu_pair(pre):
    square = pre * pre
    tanh_value = jnp.tanh(pre * (gelu_scale + gelu_scale * cubic_coef * square))
    half = 0.5 + 0.5 * tanh_value
    value = pre * half
    slope = half + pre * (1.0 - tanh_value * tanh_value) * (
        0.5 * gelu_scale + 1.5 * gelu_scale * cubic_coef * square
    )
    return (value, slope)


def main_kernel(
    state, left, right, south, north, forcing, cotangent, land, dw, dwb, gain, nbias,
    up, upb, down, downb, scale, up_t, down_t,
    result, grad_mixed, padded, grad_conv, grads, conv, acc_up, acc_down,
):
    rows, cols, channels = state.shape
    taps = 7
    margin = 3
    height = rows + 2 * margin
    padded[0:margin] = south[...].astype(f32)
    padded[height - margin : height] = north[...].astype(f32)
    for r in range(rows):
        padded[r + margin, PAD : PAD + cols, :] = state[r].astype(f32)
        padded[r + margin, PAD - margin : PAD, :] = left[r].astype(f32)
        padded[r + margin, PAD + cols : PAD + cols + margin, :] = right[r].astype(f32)

    def conv_step(step, _):
        base = pl.multiple_of(step * 8, 8)
        sums = [jnp.broadcast_to(dwb[...], (8, channels)) for _ in range(rows)]
        for b in range(taps):
            weights = [
                jnp.broadcast_to(dw[pl.ds(a * taps + b, 1), :], (8, channels)) for a in range(taps)
            ]
            for h in range(height):
                x = padded[h, pl.ds(base + (PAD - margin + b), 8), :]
                for a in range(taps):
                    if 0 <= h - a < rows:
                        sums[h - a] = sums[h - a] + weights[a] * x
        for r in range(rows):
            conv[r, pl.ds(base, 8), :] = sums[r]
        return 0

    lax.fori_loop(0, cols // 8, conv_step, 0)
    acc_up[...] = jnp.zeros_like(acc_up)
    acc_down[...] = jnp.zeros_like(acc_down)
    group = 2
    size = group * cols

    def mlp_step(step, _):
        first = step * group
        field = conv[pl.ds(first, group)].reshape(size, channels)
        average = jnp.mean(field, axis=-1, keepdims=True)
        centred = field - average
        variance = jnp.mean(centred * centred, axis=-1, keepdims=True)
        inv_std = lax.rsqrt(variance + 1e-06)
        normed = centred * inv_std
        force = forcing[pl.ds(first, group)].reshape(size, channels).astype(f32)
        mixed = (normed * gain[...] + nbias[...] + force).astype(bf16)
        pre = jnp.dot(mixed, up[...], preferred_element_type=f32) + upb[...]
        activated, slope = gelu_pair(pre)
        hidden = activated.astype(bf16)
        projected = jnp.dot(hidden, down[...], preferred_element_type=f32) + downb[...]
        ocean = jnp.concatenate(
            [
                jnp.broadcast_to(land[pl.ds(first + k, 1), :].astype(f32), (channels, cols)).T
                for k in range(group)
            ],
            axis=0,
        )
        own = state[pl.ds(first, group)].reshape(size, channels).astype(f32)
        out = ocean * (own + scale[...] * projected)
        result[pl.ds(first, group)] = out.astype(bf16).reshape(group, cols, channels)
        cot = cotangent[pl.ds(first, group)].reshape(size, channels).astype(f32)
        grad_out = (ocean * scale[...] * cot).astype(bf16)
        grad_hidden = jnp.dot(grad_out, down_t[...], preferred_element_type=f32)
        grad_pre = (grad_hidden * slope).astype(bf16)
        gmix = jnp.dot(grad_pre, up_t[...], preferred_element_type=f32)
        grad_mixed[pl.ds(pl.multiple_of(step * size, 8), size), :] = gmix
        gained = gmix * gain[...]
        gconv = inv_std * (
            gained
            - jnp.mean(gained, axis=-1, keepdims=True)
            - normed * jnp.mean(gained * normed, axis=-1, keepdims=True)
        )
        grad_conv[pl.ds(first, group)] = gconv.reshape(group, cols, channels)
        contract = (((0,), (0,)), ((), ()))
        acc_up[...] += lax.dot_general(mixed, grad_pre, contract, preferred_element_type=f32)
        acc_down[...] += lax.dot_general(grad_out, hidden, contract, preferred_element_type=f32)
        return 0

    lax.fori_loop(0, rows // group, mlp_step, 0)
    blocks = up.shape[1] // channels
    for k in range(blocks):
        part = slice(k * channels, (k + 1) * channels)
        grads[k] = acc_up[:, part]
        grads[blocks + k] = acc_down[:, part].T


def conv_grad_kernel(padded, grad_conv, out):
    rows, cols, channels = grad_conv.shape
    taps = 7
    margin = 3
    height = rows + 2 * margin
    out[...] = jnp.zeros_like(out)
    for b in range(taps):

        def step_of(step, sums):
            base = pl.multiple_of(step * 8, 8)
            sums = list(sums)
            gc = [grad_conv[r, pl.ds(base, 8), :] for r in range(rows)]
            for h in range(height):
                x = padded[h, pl.ds(base + (PAD - margin + b), 8), :]
                for a in range(taps):
                    if 0 <= h - a < rows:
                        sums[a] = sums[a] + gc[h - a] * x
            return tuple(sums)

        zero = jnp.zeros((8, channels), f32)
        sums = lax.fori_loop(0, cols // 8, step_of, (zero,) * taps)
        for a in range(taps):
            out[pl.ds(a * taps + b, 1), :] = jnp.sum(sums[a], axis=0, keepdims=True)


def regrid_kernel(target, weight, clash, terms, keep, send, table, sem):
    half = keep.shape[0]
    chunk = 512

    def clear(step, _):
        table[pl.ds(pl.multiple_of(step * chunk, chunk), chunk), :] = jnp.zeros((chunk, 128), f32)
        return 0

    lax.fori_loop(0, table.shape[0] // chunk, clear, 0)

    def add_batch(step, _):
        first = step * BATCH

        def one(k):
            e = first + k
            row = step * (BATCH // 2) + k // 2
            return target[e], weight[e] * terms[pl.ds(row, 1), :]

        @pl.when(clash[step] == 0)
        def _():
            entries = [one(k) for k in range(BATCH)]
            sums = [table[pl.ds(t, 1), :] + v for t, v in entries]
            for (t, _), s in zip(entries, sums):
                table[pl.ds(t, 1), :] = s

        @pl.when(clash[step] != 0)
        def _():
            for k in range(BATCH):
                t, v = one(k)
                table[pl.ds(t, 1), :] = table[pl.ds(t, 1), :] + v

        return 0

    lax.fori_loop(0, target.shape[0] // BATCH, add_batch, 0)

    copy = pltpu.make_async_copy(table.at[pl.ds(0, half)], keep, sem)
    copy.start()

    def give(step, _):
        at = pl.multiple_of(step * chunk, chunk)
        send[pl.ds(at, chunk), :] = table[pl.ds(half + at, chunk), :].astype(bf16)
        return 0

    lax.fori_loop(0, half // chunk, give, 0)
    copy.wait()


def swap_bit(array, bit, lon_bits):
    axis, distance = ("lon", bit) if bit < lon_bits else ("lat", bit - lon_bits)
    pairs = [(i, i ^ (1 << distance)) for i in range(lax.axis_size(axis))]
    return lax.ppermute(array, axis, pairs)


def on_device(
    state, forcing, cotangent, land_mask, dw_weight, dw_bias, norm_gain, norm_bias,
    up_weight, up_bias, down_weight, down_bias, layer_scale, owner, atmos_cell, weight_index,
    intersection_weights,
):
    margin = dw_weight.shape[0] // 2
    rows, cols, channels = state.shape
    hid = up_weight.shape[1]
    lat_count = lax.axis_size("lat")
    lon_count = lax.axis_size("lon")
    lat = lax.axis_index("lat")
    lon = lax.axis_index("lon")
    lon_bits = lon_count.bit_length() - 1
    lat_bits = lat_count.bit_length() - 1
    devices = lat_count * lon_count

    forward = [(i, (i + 1) % lon_count) for i in range(lon_count)]
    backward = [(t, s) for s, t in forward]
    left = lax.ppermute(state[:, cols - margin :], "lon", forward)
    right = lax.ppermute(state[:, :margin], "lon", backward)

    def widened(lo, hi):
        gap = jnp.zeros((margin, PAD - margin, channels), bf16)
        return jnp.concatenate([gap, left[lo:hi], state[lo:hi], right[lo:hi], gap], axis=1)

    low_rows = widened(0, margin)
    high_rows = widened(rows - margin, rows)
    folded = high_rows[::-1, ::-1]
    odd = lat % 2 == 1
    last = lat == lat_count - 1
    even_pairs, odd_pairs = [], []
    for l in range(lat_count):
        for j in range(lon_count):
            here = l * lon_count + j
            even_pairs.append((here, (l ^ 1) * lon_count + j))
            up_l = l + 1 if l % 2 else l - 1
            if l == lat_count - 1:
                odd_pairs.append((here, l * lon_count + lon_count - 1 - j))
            elif up_l >= 0:
                odd_pairs.append((here, up_l * lon_count + j))
    got_even = lax.ppermute(jnp.where(odd, low_rows, high_rows), ("lat", "lon"), even_pairs)
    got_odd = lax.ppermute(
        jnp.where(last, folded, jnp.where(odd, high_rows, low_rows)), ("lat", "lon"), odd_pairs
    )
    south = jnp.where(odd, got_even, got_odd)
    north = jnp.where(odd, got_odd, got_even)

    me = lat * lon_count + lon
    relative = owner[:, 0] ^ me
    lon_rest = list(range(1, lon_bits))
    lat_rest = list(range(lon_bits + lat_bits - 1, lon_bits - 1, -1))
    orders = [lon_rest + lat_rest, lon_rest[::-1] + lat_rest, lat_rest + lon_rest]
    widths = [160, 160, 192]
    blocks = devices // 2
    half_rows = blocks * A_DEV
    target = jnp.zeros_like(relative)
    start = 0
    for order, width in zip(orders, widths):
        number = jnp.zeros_like(relative)
        for bit in order:
            number = number * 2 + ((relative >> bit) & 1)
        place = blocks * start + number * width + (atmos_cell - start)
        target = jnp.where((atmos_cell >= start) & (atmos_cell < start + width), place, target)
        start += width
    target = target + (relative & 1) * half_rows
    table_hit = (
        weight_index[:, None] == jnp.arange(intersection_weights.shape[0], dtype=jnp.int32)[None, :]
    )
    entry_weights = jnp.sum(jnp.where(table_hit, intersection_weights[None, :], 0.0), axis=1)
    batches = target.reshape(-1, BATCH)
    clash = jnp.zeros((batches.shape[0],), jnp.int32)
    for shift in range(1, BATCH // 2 + 1):
        same = batches == jnp.roll(batches, shift, axis=1)
        clash = clash | jnp.max(same.astype(jnp.int32), axis=1)

    row = lambda v: v.reshape(1, -1)
    cells = rows * cols
    shape = jax.ShapeDtypeStruct
    result, grad_mixed, padded, grad_conv, grads = pl.pallas_call(
        main_kernel,
        out_shape=(
            shape((rows, cols, channels), bf16),
            shape((cells, channels), f32),
            shape((rows + 2 * margin, cols + 2 * PAD, channels), f32),
            shape((rows, cols, channels), f32),
            shape((2 * hid // channels, channels, channels), f32),
        ),
        in_specs=[vmem()] * 19,
        out_specs=[vmem()] * 5,
        scratch_shapes=[
            pltpu.VMEM((rows, cols, channels), f32),
            pltpu.VMEM((channels, hid), f32),
            pltpu.VMEM((channels, hid), f32),
        ],
        compiler_params=params(),
        name="block",
    )(
        state, left, right, south, north, forcing, cotangent, land_mask,
        dw_weight.reshape(-1, channels).astype(f32), row(dw_bias), row(norm_gain), row(norm_bias),
        up_weight, row(up_bias), down_weight, row(down_bias), row(layer_scale),
        up_weight.T, down_weight.T,
    )

    keep, send = pl.pallas_call(
        regrid_kernel,
        out_shape=(shape((half_rows, channels), f32), shape((half_rows, channels), bf16)),
        in_specs=[smem(), smem(), smem(), vmem()],
        out_specs=[pl.BlockSpec(memory_space=pl.ANY), vmem()],
        scratch_shapes=[pltpu.VMEM((2 * half_rows, channels), f32), pltpu.SemaphoreType.DMA],
        compiler_params=params(),
        name="regrid",
    )(target, entry_weights, clash, grad_mixed)

    dw_rows = -(-dw_weight.shape[0] * dw_weight.shape[1] // devices) * devices
    grad_dw = pl.pallas_call(
        conv_grad_kernel,
        out_shape=shape((dw_rows, channels), f32),
        in_specs=[vmem()] * 2,
        out_specs=vmem(),
        compiler_params=params(),
        name="conv_grad",
    )(padded, grad_conv)

    got = swap_bit(send, 0, lon_bits)
    parts = []
    start = 0
    for order, width in zip(orders, widths):
        lo, hi = blocks * start, blocks * (start + width)
        parts.append(keep[lo:hi] + got[lo:hi].astype(f32))
        start += width
    for stage in range(len(orders[0])):
        for q, order in enumerate(orders):
            middle = parts[q].shape[0] // 2
            arrived = swap_bit(parts[q][middle:].astype(bf16), order[stage], lon_bits)
            parts[q] = parts[q][:middle] + arrived.astype(f32)
    forcing_grad = jnp.concatenate(parts, axis=0)

    size_all = 2 * hid + dw_rows
    total = jnp.concatenate([grads.reshape(2 * hid, channels), grad_dw], axis=0)
    bits = list(range(lon_bits + lat_bits))
    for bit in bits:
        middle = total.shape[0] // 2
        mine = (me >> bit) & 1
        out = lax.dynamic_slice_in_dim(total, (1 - mine) * middle, middle, 0).astype(bf16)
        arrived = swap_bit(out, bit, lon_bits)
        total = lax.dynamic_slice_in_dim(total, mine * middle, middle, 0) + arrived.astype(f32)
    total = total.astype(bf16)
    for bit in bits[::-1]:
        arrived = swap_bit(total, bit, lon_bits)
        mine = ((me >> bit) & 1) == 1
        total = jnp.where(
            mine,
            jnp.concatenate([arrived, total], axis=0),
            jnp.concatenate([total, arrived], axis=0),
        )
    scale = float(cells * devices) ** (-0.5)
    total = total.astype(f32) * scale
    grad_up = total[:hid].reshape(hid // channels, channels, channels)
    grad_up = grad_up.transpose(1, 0, 2).reshape(channels, hid)
    grad_down = total[hid : 2 * hid]
    grad_dw = total[2 * hid : 2 * hid + dw_weight.shape[0] * dw_weight.shape[1]]
    return (result, grad_dw.reshape(dw_weight.shape), grad_up, grad_down, forcing_grad)


def solution(mesh):
    grid = P("lat", "lon", None)
    in_specs = (grid, grid, grid, P("lat", "lon")) + (P(),) * 9
    in_specs += (P(("lat", "lon"), None), P(("lat", "lon")), P(("lat", "lon")), P())
    out_specs = (grid, P(), P(), P(), P(("lat", "lon"), None))
    return jax.shard_map(
        on_device, mesh=mesh, in_specs=in_specs, out_specs=out_specs, check_vma=False
    )
```

```python
import jax
import jax.numpy as jnp
from jax import lax
from jax.experimental import pallas as pl
from jax.experimental.pallas import tpu as pltpu
from jax.sharding import PartitionSpec as P

A_DEV = 512
PAD = 8
TAPS = 7
MARGIN = 3
BATCH = 32
gelu_scale = 0.7978845608028654
cubic_coef = 0.044715
f32 = jnp.float32
bf16 = jnp.bfloat16
shape = jax.ShapeDtypeStruct


def params():
    return pltpu.CompilerParams(vmem_limit_bytes=56 << 20)


def vmem():
    return pl.BlockSpec(memory_space=pltpu.VMEM)


def smem():
    return pl.BlockSpec(memory_space=pltpu.SMEM)


def conv_block(field, base, dw, dwb, rows, channels):
    sums = [jnp.broadcast_to(dwb[...], (8, channels)) for _ in range(rows)]
    for b in range(TAPS):
        weights = [
            jnp.broadcast_to(dw[pl.ds(a * TAPS + b, 1), :], (8, channels)) for a in range(TAPS)
        ]
        for h in range(rows + TAPS - 1):
            x = field(h, base + (PAD - MARGIN + b))
            for a in range(TAPS):
                if 0 <= h - a < rows:
                    sums[h - a] = sums[h - a] + weights[a] * x
    return sums


def fill_rows(padded, state, south, north):
    rows, cols, _ = state.shape
    inner = slice(PAD, PAD + cols)
    padded[0:MARGIN, inner, :] = south[...].astype(f32)
    padded[rows + MARGIN : rows + 2 * MARGIN, inner, :] = north[...].astype(f32)
    for r in range(rows):
        padded[r + MARGIN, inner, :] = state[r].astype(f32)


def conv_kernel(state, south, north, dw, dwb, conv, padded):
    rows, cols, channels = state.shape
    fill_rows(padded, state, south, north)

    def step_of(step, _):
        base = pl.multiple_of(step * 8, 8)
        field = lambda h, at: padded[h, pl.ds(at, 8), :]
        sums = conv_block(field, base, dw, dwb, rows, channels)
        for r in range(rows):
            conv[r, pl.ds(base, 8), :] = sums[r]
        return 0

    lax.fori_loop(1, cols // 8 - 1, step_of, 0)


def block_kernel(
    state, south, north, left, right, conv, forcing, cotangent, land, entry_weights,
    dw, dwb, gain, nbias, up, upb, down, downb, scale, up_t, down_t,
    result, terms, grad_conv, grads, field, edge, acc_up, acc_down,
):
    rows, cols, channels = state.shape
    wide = 16
    for side in range(2):
        own = slice(0, wide) if side == 0 else slice(cols - wide, cols)
        at = PAD if side == 0 else 0
        edge[side, 0:MARGIN, at : at + wide, :] = south[:, own, :].astype(f32)
        edge[side, rows + MARGIN : rows + 2 * MARGIN, at : at + wide, :] = north[:, own, :].astype(f32)
        for r in range(rows):
            edge[side, r + MARGIN, at : at + wide, :] = state[r, own, :].astype(f32)
        for h in range(rows + 2 * MARGIN):
            if side == 0:
                edge[side, h, PAD - MARGIN : PAD, :] = left[h].astype(f32)
            else:
                edge[side, h, wide : wide + MARGIN, :] = right[h].astype(f32)
        sums = conv_block(
            lambda h, at: edge[side, h, pl.ds(at, 8), :], 0, dw, dwb, rows, channels
        )
        out = slice(0, 8) if side == 0 else slice(cols - 8, cols)
        for r in range(rows):
            field[r, out, :] = sums[r]
    for r in range(rows):
        field[r, 8 : cols - 8, :] = conv[r, 8 : cols - 8, :]

    acc_up[...] = jnp.zeros_like(acc_up)
    acc_down[...] = jnp.zeros_like(acc_down)
    group = 2
    size = group * cols

    def column(ref, first):
        return jnp.concatenate(
            [
                jnp.broadcast_to(ref[pl.ds(first + k, 1), :].astype(f32), (channels, cols)).T
                for k in range(group)
            ],
            axis=0,
        )

    def mlp_step(step, _):
        first = step * group
        here = field[pl.ds(first, group)].reshape(size, channels)
        average = jnp.mean(here, axis=-1, keepdims=True)
        centred = here - average
        variance = jnp.mean(centred * centred, axis=-1, keepdims=True)
        inv_std = lax.rsqrt(variance + 1e-06)
        normed = centred * inv_std
        force = forcing[pl.ds(first, group)].reshape(size, channels).astype(f32)
        mixed = (normed * gain[...] + nbias[...] + force).astype(bf16)
        pre = jnp.dot(mixed, up[...], preferred_element_type=f32) + upb[...]
        square = pre * pre
        tanh_value = jnp.tanh(pre * (gelu_scale + gelu_scale * cubic_coef * square))
        half = 0.5 + 0.5 * tanh_value
        hidden = (pre * half).astype(bf16)
        slope = half + pre * (1.0 - tanh_value * tanh_value) * (
            0.5 * gelu_scale + 1.5 * gelu_scale * cubic_coef * square
        )
        projected = jnp.dot(hidden, down[...], preferred_element_type=f32) + downb[...]
        ocean = column(land, first)
        own = state[pl.ds(first, group)].reshape(size, channels).astype(f32)
        out = ocean * (own + scale[...] * projected)
        result[pl.ds(first, group)] = out.astype(bf16).reshape(group, cols, channels)
        cot = cotangent[pl.ds(first, group)].reshape(size, channels).astype(f32)
        grad_out = (ocean * scale[...] * cot).astype(bf16)
        grad_hidden = jnp.dot(grad_out, down_t[...], preferred_element_type=f32)
        grad_pre = (grad_hidden * slope).astype(bf16)
        gmix = jnp.dot(grad_pre, up_t[...], preferred_element_type=f32)
        at = pl.multiple_of(step * size, 8)
        for k in range(2):
            terms[pl.ds(k * rows * cols + at, size), :] = column(entry_weights.at[k], first) * gmix
        gained = gmix * gain[...]
        gconv = inv_std * (
            gained
            - jnp.mean(gained, axis=-1, keepdims=True)
            - normed * jnp.mean(gained * normed, axis=-1, keepdims=True)
        )
        grad_conv[pl.ds(first, group)] = gconv.reshape(group, cols, channels)
        contract = (((0,), (0,)), ((), ()))
        acc_up[...] += lax.dot_general(mixed, grad_pre, contract, preferred_element_type=f32)
        acc_down[...] += lax.dot_general(grad_out, hidden, contract, preferred_element_type=f32)
        return 0

    lax.fori_loop(0, rows // group, mlp_step, 0)
    blocks = up.shape[1] // channels
    for k in range(blocks):
        part = slice(k * channels, (k + 1) * channels)
        grads[k] = acc_up[:, part]
        grads[blocks + k] = acc_down[:, part].T


def conv_grad_kernel(state, south, north, left, right, grad_conv, out, padded):
    rows, cols, channels = grad_conv.shape
    height = rows + 2 * MARGIN
    fill_rows(padded, state, south, north)
    for h in range(height):
        padded[h, PAD - MARGIN : PAD, :] = left[h].astype(f32)
        padded[h, PAD + cols : PAD + cols + MARGIN, :] = right[h].astype(f32)
    out[...] = jnp.zeros_like(out)
    unroll = 2
    for b in range(TAPS):

        def step_of(step, sums):
            sums = list(sums)
            for u in range(unroll):
                base = pl.multiple_of((step * unroll + u) * 8, 8)
                gc = [grad_conv[r, pl.ds(base, 8), :] for r in range(rows)]
                for h in range(height):
                    x = padded[h, pl.ds(base + (PAD - MARGIN + b), 8), :]
                    for a in range(TAPS):
                        if 0 <= h - a < rows:
                            k = a * 2 + (h - a) % 2
                            sums[k] = sums[k] + gc[h - a] * x
            return tuple(sums)

        zero = jnp.zeros((8, channels), f32)
        sums = lax.fori_loop(0, cols // (8 * unroll), step_of, (zero,) * (2 * TAPS))
        for a in range(TAPS):
            total = sums[2 * a] + sums[2 * a + 1]
            out[pl.ds(a * TAPS + b, 1), :] = jnp.sum(total, axis=0, keepdims=True)


def table_kernel(keys, info, terms, out, *scratch):
    table = scratch[0] if scratch else out
    rows = out.shape[0] if scratch else out.shape[0] - 8
    shift = (terms.shape[0] - 1).bit_length()
    chunk = 512

    def clear(step, _):
        at = pl.multiple_of(step * chunk, chunk)
        table[pl.ds(at, chunk), :] = jnp.zeros((chunk, table.shape[1]), f32)
        return 0

    lax.fori_loop(0, rows // chunk, clear, 0)
    offset = info[0]
    batches = info[1]

    def entry(place):
        key = keys[place]
        return key >> shift, key & ((1 << shift) - 1)

    def add_batch(step, _):
        found = [entry(offset + step + k * batches) for k in range(BATCH)]
        sums = [table[pl.ds(t, 1), :] + terms[pl.ds(e, 1), :] for t, e in found]
        for (t, _), value in zip(found, sums):
            table[pl.ds(t, 1), :] = value
        return 0

    def add_one(step, _):
        t, e = entry(offset + step)
        table[pl.ds(t, 1), :] = table[pl.ds(t, 1), :] + terms[pl.ds(e, 1), :]
        return 0

    @pl.when(info[2] == 0)
    def _():
        lax.fori_loop(0, batches, add_batch, 0)

    @pl.when(info[2] != 0)
    def _():
        lax.fori_loop(0, batches * BATCH, add_one, 0)

    if scratch:

        def give(step, _):
            at = pl.multiple_of(step * chunk, chunk)
            out[pl.ds(at, chunk), :] = table[pl.ds(at, chunk), :].astype(out.dtype)
            return 0

        lax.fori_loop(0, rows // chunk, give, 0)


def swap_bit(array, bit):
    pairs = [(i, i ^ (1 << bit)) for i in range(lax.axis_size("lon"))]
    return lax.ppermute(array, "lon", pairs)


def after(array, *others):
    return lax.optimization_barrier((array,) + others)[0]


def on_device(
    state, forcing, cotangent, land_mask, dw_weight, dw_bias, norm_gain, norm_bias,
    up_weight, up_bias, down_weight, down_bias, layer_scale, owner, atmos_cell, weight_index,
    intersection_weights,
):
    rows, cols, channels = state.shape
    cells = rows * cols
    hid = up_weight.shape[1]
    lat_count = lax.axis_size("lat")
    lon_count = lax.axis_size("lon")
    lat = lax.axis_index("lat")
    lon = lax.axis_index("lon")
    lon_bits = lon_count.bit_length() - 1
    devices = lat_count * lon_count
    entries = owner.shape[0]
    fan = entries // cells

    low_rows = state[:MARGIN]
    high_rows = state[rows - MARGIN :]
    odd = lat % 2 == 1
    last = lat == lat_count - 1
    even_pairs, odd_pairs = [], []
    for l in range(lat_count):
        for j in range(lon_count):
            here = l * lon_count + j
            even_pairs.append((here, (l ^ 1) * lon_count + j))
            beyond = l + 1 if l % 2 else l - 1
            if l == lat_count - 1:
                odd_pairs.append((here, l * lon_count + lon_count - 1 - j))
            elif beyond >= 0:
                odd_pairs.append((here, beyond * lon_count + j))
    got_even = lax.ppermute(jnp.where(odd, low_rows, high_rows), ("lat", "lon"), even_pairs)
    got_odd = lax.ppermute(
        jnp.where(last, high_rows[::-1, ::-1], jnp.where(odd, high_rows, low_rows)),
        ("lat", "lon"),
        odd_pairs,
    )
    south = jnp.where(odd, got_even, got_odd)
    north = jnp.where(odd, got_odd, got_even)

    forward = [(i, (i + 1) % lon_count) for i in range(lon_count)]
    backward = [(t, s) for s, t in forward]
    column = lambda part: jnp.concatenate([south[:, part], state[:, part], north[:, part]], axis=0)
    left = lax.ppermute(column(slice(cols - MARGIN, cols)), "lon", forward)
    right = lax.ppermute(column(slice(0, MARGIN)), "lon", backward)

    owner_lat = owner[:, 0] // lon_count
    relative = (owner[:, 0] % lon_count) ^ lon
    rest = list(range(1, lon_bits))
    orders = [rest, rest[::-1]]
    width = A_DEV // 2
    half_rows = devices // 2 * A_DEV
    numbers = []
    for order in orders:
        number = jnp.zeros_like(relative)
        for bit in order:
            number = number * 2 + ((relative >> bit) & 1)
        numbers.append(number * lat_count + owner_lat)
    upper = (atmos_cell >= width).astype(jnp.int32)
    block = jnp.where(upper == 1, numbers[1], numbers[0])
    row = (relative & 1) * half_rows + upper * (half_rows // 2) + block * width
    row = row + atmos_cell - upper * width
    entry = jnp.arange(entries, dtype=jnp.int32)
    shift = (entries - 1).bit_length()
    keys = lax.sort((row << shift) + (entry % fan) * cells + entry // fan, is_stable=False)
    sorted_row = keys >> shift
    mine = sorted_row < half_rows
    least = 64
    shared = jnp.any(sorted_row[least:] == sorted_row[:-least]).astype(jnp.int32)
    kept = jnp.sum(mine.astype(jnp.int32))
    spare = jnp.full((least * BATCH,), half_rows << shift, jnp.int32)
    batches_of = lambda count: jnp.maximum((count + BATCH - 1) // BATCH, least)
    send_info = jnp.stack([kept, batches_of(entries - kept), shared])
    keep_info = jnp.stack([jnp.zeros_like(kept), batches_of(kept), shared])
    send_keys = jnp.concatenate([keys - (half_rows << shift), spare])
    keep_keys = jnp.concatenate([jnp.where(mine, keys, half_rows << shift), spare])
    index = weight_index.reshape(rows, cols, fan).transpose(2, 0, 1)
    entry_weights = jnp.zeros((fan, rows, cols), f32)
    for k in range(intersection_weights.shape[0]):
        entry_weights = jnp.where(index == k, intersection_weights[k], entry_weights)

    line = lambda v: v.reshape(1, -1)
    taps = dw_weight.reshape(-1, channels).astype(f32)
    conv = pl.pallas_call(
        conv_kernel,
        out_shape=shape((rows, cols, channels), f32),
        in_specs=[vmem()] * 5,
        out_specs=vmem(),
        scratch_shapes=[pltpu.VMEM((rows + 2 * MARGIN, cols + 2 * PAD, channels), f32)],
        compiler_params=params(),
        name="conv",
    )(state, south, north, taps, line(dw_bias))
    result, terms, grad_conv, grads = pl.pallas_call(
        block_kernel,
        out_shape=(
            shape((rows, cols, channels), bf16),
            shape((entries, channels), f32),
            shape((rows, cols, channels), f32),
            shape((2 * hid // channels, channels, channels), f32),
        ),
        in_specs=[vmem()] * 21,
        out_specs=[vmem()] * 4,
        scratch_shapes=[
            pltpu.VMEM((rows, cols, channels), f32),
            pltpu.VMEM((2, rows + 2 * MARGIN, 24, channels), f32),
            pltpu.VMEM((channels, hid), f32),
            pltpu.VMEM((channels, hid), f32),
        ],
        compiler_params=params(),
        name="block",
    )(
        state, south, north, left, right, conv, forcing, cotangent, land_mask, entry_weights,
        taps, line(dw_bias), line(norm_gain), line(norm_bias), up_weight, line(up_bias),
        down_weight, line(down_bias), line(layer_scale), up_weight.T, down_weight.T,
    )

    send = pl.pallas_call(
        table_kernel,
        out_shape=shape((half_rows, channels), bf16),
        in_specs=[smem(), smem(), vmem()],
        out_specs=vmem(),
        scratch_shapes=[pltpu.VMEM((half_rows + 8, channels), f32)],
        compiler_params=params(),
        name="send_table",
    )(send_keys, send_info, terms)
    got = swap_bit(send, 0)
    keep = pl.pallas_call(
        table_kernel,
        out_shape=shape((half_rows + 8, channels), f32),
        in_specs=[smem(), smem(), vmem()],
        out_specs=vmem(),
        compiler_params=params(),
        name="keep_table",
    )(keep_keys, keep_info, after(terms, send))

    middle = half_rows // 2
    parts = [
        keep[:middle] + got[:middle].astype(f32),
        keep[middle : 2 * middle] + got[middle:].astype(f32),
    ]
    for stage in range(len(rest)):
        for q, order in enumerate(orders):
            size = parts[q].shape[0] // 2
            arrived = swap_bit(parts[q][size:].astype(bf16), order[stage])
            parts[q] = parts[q][:size] + arrived.astype(f32)
    lined = jnp.concatenate([p.reshape(lat_count, width, channels) for p in parts], axis=1)
    bands = lax.all_to_all(lined.astype(bf16), "lat", split_axis=0, concat_axis=0, tiled=True)
    forcing_grad = jnp.sum(bands.astype(f32), axis=0)

    tap_count = dw_weight.shape[0] * dw_weight.shape[1]
    dw_rows = -(-tap_count // devices) * devices
    grad_dw = pl.pallas_call(
        conv_grad_kernel,
        out_shape=shape((dw_rows, channels), f32),
        in_specs=[vmem()] * 6,
        out_specs=vmem(),
        scratch_shapes=[pltpu.VMEM((rows + 2 * MARGIN, cols + 2 * PAD, channels), f32)],
        compiler_params=params(),
        name="conv_grad",
    )(state, south, north, left, right, after(grad_conv, keep))
    total = jnp.concatenate([grads.reshape(2 * hid, channels), grad_dw], axis=0).astype(bf16)
    total = total.reshape(devices, -1, channels)
    total = lax.all_to_all(total, ("lat", "lon"), split_axis=0, concat_axis=0, tiled=True)
    total = jnp.sum(total.astype(f32), axis=0, keepdims=True).astype(bf16)
    total = jnp.broadcast_to(total, (devices,) + total.shape[1:])
    total = lax.all_to_all(total, ("lat", "lon"), split_axis=0, concat_axis=0, tiled=True)
    scale = float(cells * devices) ** (-0.5)
    total = total.reshape(-1, channels).astype(f32) * scale
    grad_up = total[:hid].reshape(hid // channels, channels, channels)
    grad_up = grad_up.transpose(1, 0, 2).reshape(channels, hid)
    grad_down = total[hid : 2 * hid]
    grad_dw = total[2 * hid : 2 * hid + tap_count].reshape(dw_weight.shape)
    return (result, grad_dw, grad_up, grad_down, forcing_grad)


def solution(mesh):
    grid = P("lat", "lon", None)
    in_specs = (grid, grid, grid, P("lat", "lon")) + (P(),) * 9
    in_specs += (P(("lat", "lon"), None), P(("lat", "lon")), P(("lat", "lon")), P())
    out_specs = (grid, P(), P(), P(), P(("lat", "lon"), None))
    return jax.shard_map(
        on_device, mesh=mesh, in_specs=in_specs, out_specs=out_specs, check_vma=False
    )
```

```python
import jax
import jax.numpy as jnp
from jax import lax
from jax.experimental import pallas as pl
from jax.experimental.pallas import tpu as pltpu
from jax.sharding import PartitionSpec as P

A_DEV = 512
PAD = 8
TAPS = 7
MARGIN = 3
BATCH = 32
gelu_scale = 0.7978845608028654
cubic_coef = 0.044715
f32 = jnp.float32
bf16 = jnp.bfloat16
shape = jax.ShapeDtypeStruct


def params():
    return pltpu.CompilerParams(vmem_limit_bytes=56 << 20)


def cost(microseconds):
    return pl.CostEstimate(flops=int(microseconds * 1e9), bytes_accessed=0, transcendentals=0)


def vmem():
    return pl.BlockSpec(memory_space=pltpu.VMEM)


def smem():
    return pl.BlockSpec(memory_space=pltpu.SMEM)


def conv_block(field, base, dw, dwb, rows, channels):
    sums = [jnp.broadcast_to(dwb[...], (8, channels)) for _ in range(rows)]
    for b in range(TAPS):
        weights = [
            jnp.broadcast_to(dw[pl.ds(a * TAPS + b, 1), :], (8, channels)) for a in range(TAPS)
        ]
        for h in range(rows + TAPS - 1):
            x = field(h, base + (PAD - MARGIN + b))
            for a in range(TAPS):
                if 0 <= h - a < rows:
                    sums[h - a] = sums[h - a] + weights[a] * x
    return sums


def fill_rows(padded, state, south, north):
    rows, cols, _ = state.shape
    inner = slice(PAD, PAD + cols)
    padded[0:MARGIN, inner, :] = south[...].astype(f32)
    padded[rows + MARGIN : rows + 2 * MARGIN, inner, :] = north[...].astype(f32)
    for r in range(rows):
        padded[r + MARGIN, inner, :] = state[r].astype(f32)


def conv_kernel(state, south, north, dw, dwb, conv, padded):
    rows, cols, channels = state.shape
    fill_rows(padded, state, south, north)

    def step_of(step, _):
        base = pl.multiple_of(step * 8, 8)
        field = lambda h, at: padded[h, pl.ds(at, 8), :]
        sums = conv_block(field, base, dw, dwb, rows, channels)
        for r in range(rows):
            conv[r, pl.ds(base, 8), :] = sums[r]
        return 0

    lax.fori_loop(1, cols // 8 - 1, step_of, 0)


def block_kernel(
    state, south, north, left, right, conv, forcing, cotangent, land, weight_index, weight_table,
    dw, dwb, gain, nbias, up, upb, down, downb, scale, up_t, down_t,
    result, terms, grad_conv, grads, field, edge, acc_up, acc_down, entry_weights, spread,
):
    rows, cols, channels = state.shape
    wide = 16
    for side in range(2):
        own = slice(0, wide) if side == 0 else slice(cols - wide, cols)
        at = PAD if side == 0 else 0
        edge[side, 0:MARGIN, at : at + wide, :] = south[:, own, :].astype(f32)
        edge[side, rows + MARGIN : rows + 2 * MARGIN, at : at + wide, :] = north[:, own, :].astype(f32)
        for r in range(rows):
            edge[side, r + MARGIN, at : at + wide, :] = state[r, own, :].astype(f32)
        for h in range(rows + 2 * MARGIN):
            if side == 0:
                edge[side, h, PAD - MARGIN : PAD, :] = left[h].astype(f32)
            else:
                edge[side, h, wide : wide + MARGIN, :] = right[h].astype(f32)
        sums = conv_block(
            lambda h, at: edge[side, h, pl.ds(at, 8), :], 0, dw, dwb, rows, channels
        )
        out = slice(0, 8) if side == 0 else slice(cols - 8, cols)
        for r in range(rows):
            field[r, out, :] = sums[r]
    for r in range(rows):
        field[r, 8 : cols - 8, :] = conv[r, 8 : cols - 8, :]

    index = weight_index[...]
    looked_up = jnp.zeros(index.shape, f32)
    for k in range(weight_table.shape[0]):
        looked_up = jnp.where(index == k, weight_table[k], looked_up)
    entry_weights[...] = looked_up
    acc_up[...] = jnp.zeros_like(acc_up)
    acc_down[...] = jnp.zeros_like(acc_down)
    group = 2
    size = group * cols
    fan = terms.shape[0] // (rows * cols)
    lines = fan * size // channels

    def column(ref, first, count):
        width = ref.shape[1]
        return jnp.concatenate(
            [
                jnp.broadcast_to(ref[pl.ds(first + k, 1), :].astype(f32), (channels, width)).T
                for k in range(count)
            ],
            axis=0,
        )

    def mlp_step(step, _):
        first = step * group
        here = field[pl.ds(first, group)].reshape(size, channels)
        average = jnp.mean(here, axis=-1, keepdims=True)
        centred = here - average
        variance = jnp.mean(centred * centred, axis=-1, keepdims=True)
        inv_std = lax.rsqrt(variance + 1e-06)
        normed = centred * inv_std
        force = forcing[pl.ds(first, group)].reshape(size, channels).astype(f32)
        mixed = (normed * gain[...] + nbias[...] + force).astype(bf16)
        pre = jnp.dot(mixed, up[...], preferred_element_type=f32) + upb[...]
        square = pre * pre
        tanh_value = jnp.tanh(pre * (gelu_scale + gelu_scale * cubic_coef * square))
        half = 0.5 + 0.5 * tanh_value
        hidden = (pre * half).astype(bf16)
        slope = half + pre * (1.0 - tanh_value * tanh_value) * (
            0.5 * gelu_scale + 1.5 * gelu_scale * cubic_coef * square
        )
        projected = jnp.dot(hidden, down[...], preferred_element_type=f32) + downb[...]
        ocean = column(land, first, group)
        own = state[pl.ds(first, group)].reshape(size, channels).astype(f32)
        out = ocean * (own + scale[...] * projected)
        result[pl.ds(first, group)] = out.astype(bf16).reshape(group, cols, channels)
        cot = cotangent[pl.ds(first, group)].reshape(size, channels).astype(f32)
        grad_out = (ocean * scale[...] * cot).astype(bf16)
        grad_hidden = jnp.dot(grad_out, down_t[...], preferred_element_type=f32)
        grad_pre = (grad_hidden * slope).astype(bf16)
        gmix = jnp.dot(grad_pre, up_t[...], preferred_element_type=f32)
        at = pl.multiple_of(step * size, 8)
        spread[...] = column(entry_weights, step * lines, lines)
        for k in range(fan):
            weights = spread[pl.ds(k, size, stride=fan), :]
            terms[pl.ds(k * rows * cols + at, size), :] = weights * gmix
        gained = gmix * gain[...]
        gconv = inv_std * (
            gained
            - jnp.mean(gained, axis=-1, keepdims=True)
            - normed * jnp.mean(gained * normed, axis=-1, keepdims=True)
        )
        grad_conv[pl.ds(first, group)] = gconv.reshape(group, cols, channels)
        contract = (((0,), (0,)), ((), ()))
        acc_up[...] += lax.dot_general(mixed, grad_pre, contract, preferred_element_type=f32)
        acc_down[...] += lax.dot_general(grad_out, hidden, contract, preferred_element_type=f32)
        return 0

    lax.fori_loop(0, rows // group, mlp_step, 0)
    blocks = up.shape[1] // channels
    for k in range(blocks):
        part = slice(k * channels, (k + 1) * channels)
        grads[k] = acc_up[:, part]
        grads[blocks + k] = acc_down[:, part].T


def conv_grad_kernel(state, south, north, left, right, grad_conv, out, padded):
    rows, cols, channels = grad_conv.shape
    height = rows + 2 * MARGIN
    fill_rows(padded, state, south, north)
    for h in range(height):
        padded[h, PAD - MARGIN : PAD, :] = left[h].astype(f32)
        padded[h, PAD + cols : PAD + cols + MARGIN, :] = right[h].astype(f32)
    out[...] = jnp.zeros_like(out)
    unroll = 2
    for b in range(TAPS):

        def step_of(step, sums):
            sums = list(sums)
            for u in range(unroll):
                base = pl.multiple_of((step * unroll + u) * 8, 8)
                gc = [grad_conv[r, pl.ds(base, 8), :] for r in range(rows)]
                for h in range(height):
                    x = padded[h, pl.ds(base + (PAD - MARGIN + b), 8), :]
                    for a in range(TAPS):
                        if 0 <= h - a < rows:
                            k = a * 2 + (h - a) % 2
                            sums[k] = sums[k] + gc[h - a] * x
            return tuple(sums)

        zero = jnp.zeros((8, channels), f32)
        sums = lax.fori_loop(0, cols // (8 * unroll), step_of, (zero,) * (2 * TAPS))
        for a in range(TAPS):
            total = sums[2 * a] + sums[2 * a + 1]
            out[pl.ds(a * TAPS + b, 1), :] = jnp.sum(total, axis=0, keepdims=True)


def table_kernel(rows, names, info, terms, zeros, table, sem):
    clear = pltpu.make_async_copy(zeros, table, sem)
    clear.start()
    clear.wait()
    offset = info[0]
    batches = info[1]

    def add_batch(step, _):
        place = offset + step
        found = []
        for _ in range(BATCH):
            found.append((rows[place], names[place]))
            place = place + batches
        sums = [table[t] + terms[e] for t, e in found]
        for (t, _), value in zip(found, sums):
            table[t] = value
        return 0

    def add_one(step, _):
        t = rows[offset + step]
        table[t] = table[t] + terms[names[offset + step]]
        return 0

    @pl.when(info[2] == 0)
    def _():
        lax.fori_loop(0, batches, add_batch, 0)

    @pl.when(info[2] != 0)
    def _():
        lax.fori_loop(0, batches * BATCH, add_one, 0)


def swap_bit(array, bit):
    pairs = [(i, i ^ (1 << bit)) for i in range(lax.axis_size("lon"))]
    return lax.ppermute(array, "lon", pairs)


def after(array, *others):
    return lax.optimization_barrier((array,) + others)[0]


def on_device(
    state, forcing, cotangent, land_mask, dw_weight, dw_bias, norm_gain, norm_bias,
    up_weight, up_bias, down_weight, down_bias, layer_scale, owner, atmos_cell, weight_index,
    intersection_weights,
):
    rows, cols, channels = state.shape
    cells = rows * cols
    hid = up_weight.shape[1]
    lat_count = lax.axis_size("lat")
    lon_count = lax.axis_size("lon")
    lat = lax.axis_index("lat")
    lon = lax.axis_index("lon")
    lon_bits = lon_count.bit_length() - 1
    devices = lat_count * lon_count
    entries = owner.shape[0]
    fan = entries // cells

    low_rows = state[:MARGIN]
    high_rows = state[rows - MARGIN :]
    odd = lat % 2 == 1
    last = lat == lat_count - 1
    even_pairs, odd_pairs = [], []
    for l in range(lat_count):
        for j in range(lon_count):
            here = l * lon_count + j
            even_pairs.append((here, (l ^ 1) * lon_count + j))
            beyond = l + 1 if l % 2 else l - 1
            if l == lat_count - 1:
                odd_pairs.append((here, l * lon_count + lon_count - 1 - j))
            elif beyond >= 0:
                odd_pairs.append((here, beyond * lon_count + j))
    got_even = lax.ppermute(jnp.where(odd, low_rows, high_rows), ("lat", "lon"), even_pairs)
    got_odd = lax.ppermute(
        jnp.where(last, high_rows[::-1, ::-1], jnp.where(odd, high_rows, low_rows)),
        ("lat", "lon"),
        odd_pairs,
    )
    south = jnp.where(odd, got_even, got_odd)
    north = jnp.where(odd, got_odd, got_even)

    forward = [(i, (i + 1) % lon_count) for i in range(lon_count)]
    backward = [(t, s) for s, t in forward]
    column = lambda part: jnp.concatenate([south[:, part], state[:, part], north[:, part]], axis=0)
    left = lax.ppermute(column(slice(cols - MARGIN, cols)), "lon", forward)
    right = lax.ppermute(column(slice(0, MARGIN)), "lon", backward)

    owner_lat = owner[:, 0] // lon_count
    relative = (owner[:, 0] % lon_count) ^ lon
    rest = list(range(1, lon_bits))
    orders = [rest, rest[::-1]]
    width = A_DEV // 2
    half_rows = devices // 2 * A_DEV
    numbers = []
    for order in orders:
        number = jnp.zeros_like(relative)
        for bit in order:
            number = number * 2 + ((relative >> bit) & 1)
        numbers.append(number * lat_count + owner_lat)
    upper = (atmos_cell >= width).astype(jnp.int32)
    block = jnp.where(upper == 1, numbers[1], numbers[0])
    row = (relative & 1) * half_rows + upper * (half_rows // 2) + block * width
    row = row + atmos_cell - upper * width
    entry = jnp.arange(entries, dtype=jnp.int32)
    shift = (entries - 1).bit_length()
    least = 64
    spare = jnp.full((least * BATCH,), 2 * half_rows << shift, jnp.int32)
    keys = (row << shift) + (entry % fan) * cells + entry // fan
    keys = lax.sort(jnp.concatenate([keys, spare]), is_stable=False)
    sorted_row = keys >> shift
    names = keys & ((1 << shift) - 1)
    mine = sorted_row < half_rows
    send_rows = jnp.where(mine, 0, sorted_row - half_rows)
    keep_rows = jnp.where(mine, sorted_row, half_rows)
    same = sorted_row[least:entries] == sorted_row[: entries - least]
    shared = jnp.max(same.astype(jnp.int32))
    kept = jnp.sum(mine.astype(jnp.int32))
    batches_of = lambda count: jnp.maximum((count + BATCH - 1) // BATCH, least)
    send_info = jnp.stack([kept, batches_of(entries - kept), shared])
    keep_info = jnp.stack([jnp.zeros_like(kept), batches_of(kept), shared])

    line = lambda v: v.reshape(1, -1)
    taps = dw_weight.reshape(-1, channels).astype(f32)
    conv = pl.pallas_call(
        conv_kernel,
        out_shape=shape((rows, cols, channels), f32),
        in_specs=[vmem()] * 5,
        out_specs=vmem(),
        scratch_shapes=[pltpu.VMEM((rows + 2 * MARGIN, cols + 2 * PAD, channels), f32)],
        compiler_params=params(),
        cost_estimate=cost(10),
        name="conv",
    )(state, south, north, taps, line(dw_bias))
    result, terms, grad_conv, grads = pl.pallas_call(
        block_kernel,
        out_shape=(
            shape((rows, cols, channels), bf16),
            shape((entries, channels), f32),
            shape((rows, cols, channels), f32),
            shape((2 * hid // channels, channels, channels), f32),
        ),
        in_specs=[vmem()] * 10 + [smem()] + [vmem()] * 11,
        out_specs=[vmem()] * 4,
        scratch_shapes=[
            pltpu.VMEM((rows, cols, channels), f32),
            pltpu.VMEM((2, rows + 2 * MARGIN, 24, channels), f32),
            pltpu.VMEM((channels, hid), f32),
            pltpu.VMEM((channels, hid), f32),
            pltpu.VMEM((entries // channels, channels), f32),
            pltpu.VMEM((2 * fan * cols, channels), f32),
        ],
        compiler_params=params(),
        cost_estimate=cost(13),
        name="block",
    )(
        state, south, north, left, right, conv, forcing, cotangent, land_mask,
        weight_index.reshape(-1, channels), intersection_weights, taps, line(dw_bias), line(norm_gain), line(norm_bias), up_weight, line(up_bias),
        down_weight, line(down_bias), line(layer_scale), up_weight.T, down_weight.T,
    )

    zeros = jnp.zeros((half_rows + 8, 1, channels), f32)

    def table(name, place_rows, info, of_terms):
        return pl.pallas_call(
            table_kernel,
            out_shape=shape(zeros.shape, f32),
            in_specs=[smem()] * 3 + [vmem(), pl.BlockSpec(memory_space=pl.ANY)],
            out_specs=vmem(),
            scratch_shapes=[pltpu.SemaphoreType.DMA],
            compiler_params=params(),
            cost_estimate=cost(6),
            name=name,
        )(place_rows, names, info, of_terms, zeros).reshape(-1, channels)

    terms = terms.reshape(entries, 1, channels)
    send = table("send_table", send_rows, send_info, terms)[:half_rows].astype(bf16)
    got = swap_bit(send, 0)
    keep = table("keep_table", keep_rows, keep_info, after(terms, send))

    middle = half_rows // 2
    parts = [
        keep[:middle] + got[:middle].astype(f32),
        keep[middle : 2 * middle] + got[middle:].astype(f32),
    ]
    for stage in range(len(rest)):
        for q, order in enumerate(orders):
            size = parts[q].shape[0] // 2
            arrived = swap_bit(parts[q][size:].astype(bf16), order[stage])
            parts[q] = parts[q][:size] + arrived.astype(f32)
    lined = jnp.concatenate([p.reshape(lat_count, width, channels) for p in parts], axis=1)
    bands = lax.all_to_all(lined.astype(bf16), "lat", split_axis=0, concat_axis=0, tiled=True)
    forcing_grad = jnp.sum(bands.astype(f32), axis=0)

    tap_count = dw_weight.shape[0] * dw_weight.shape[1]
    dw_rows = -(-tap_count // devices) * devices
    grad_dw = pl.pallas_call(
        conv_grad_kernel,
        out_shape=shape((dw_rows, channels), f32),
        in_specs=[vmem()] * 6,
        out_specs=vmem(),
        scratch_shapes=[pltpu.VMEM((rows + 2 * MARGIN, cols + 2 * PAD, channels), f32)],
        compiler_params=params(),
        cost_estimate=cost(9),
        name="conv_grad",
    )(state, south, north, left, right, after(grad_conv, keep))
    total = jnp.concatenate([grads.reshape(2 * hid, channels), grad_dw], axis=0).astype(bf16)
    total = total.reshape(devices, -1, channels)
    total = lax.all_to_all(total, ("lat", "lon"), split_axis=0, concat_axis=0, tiled=True)
    total = jnp.sum(total.astype(f32), axis=0, keepdims=True).astype(bf16)
    total = jnp.broadcast_to(total, (devices,) + total.shape[1:])
    total = lax.all_to_all(total, ("lat", "lon"), split_axis=0, concat_axis=0, tiled=True)
    scale = float(cells * devices) ** (-0.5)
    total = total.reshape(-1, channels).astype(f32) * scale
    grad_up = total[:hid].reshape(hid // channels, channels, channels)
    grad_up = grad_up.transpose(1, 0, 2).reshape(channels, hid)
    grad_down = total[hid : 2 * hid]
    grad_dw = total[2 * hid : 2 * hid + tap_count].reshape(dw_weight.shape)
    return (result, grad_dw, grad_up, grad_down, forcing_grad)


def solution(mesh):
    grid = P("lat", "lon", None)
    in_specs = (grid, grid, grid, P("lat", "lon")) + (P(),) * 9
    in_specs += (P(("lat", "lon"), None), P(("lat", "lon")), P(("lat", "lon")), P())
    out_specs = (grid, P(), P(), P(), P(("lat", "lon"), None))
    return jax.shard_map(
        on_device, mesh=mesh, in_specs=in_specs, out_specs=out_specs, check_vma=False
    )
```

```python
import jax
import jax.numpy as jnp
from jax import lax
from jax.experimental import pallas as pl
from jax.experimental.pallas import tpu as pltpu
from jax.sharding import PartitionSpec as P

A_DEV = 512
PAD = 8
TAPS = 7
MARGIN = 3
GROUP = 256
gelu_scale = 0.7978845608028654
cubic_coef = 0.044715
f32 = jnp.float32
bf16 = jnp.bfloat16
shape = jax.ShapeDtypeStruct


def params():
    return pltpu.CompilerParams(vmem_limit_bytes=56 << 20)


def cost(microseconds):
    return pl.CostEstimate(flops=int(microseconds * 1e9), bytes_accessed=0, transcendentals=0)


def vmem():
    return pl.BlockSpec(memory_space=pltpu.VMEM)


def smem():
    return pl.BlockSpec(memory_space=pltpu.SMEM)


def conv_block(field, base, dw, dwb, rows, channels):
    sums = [jnp.broadcast_to(dwb[...], (8, channels)) for _ in range(rows)]
    for b in range(TAPS):
        weights = [
            jnp.broadcast_to(dw[pl.ds(a * TAPS + b, 1), :], (8, channels)) for a in range(TAPS)
        ]
        for h in range(rows + TAPS - 1):
            x = field(h, base + (PAD - MARGIN + b))
            for a in range(TAPS):
                if 0 <= h - a < rows:
                    sums[h - a] = sums[h - a] + weights[a] * x
    return sums


def fill_rows(padded, state, south, north):
    rows, cols, _ = state.shape
    inner = slice(PAD, PAD + cols)
    padded[0:MARGIN, inner, :] = south[...].astype(f32)
    padded[rows + MARGIN : rows + 2 * MARGIN, inner, :] = north[...].astype(f32)
    for r in range(rows):
        padded[r + MARGIN, inner, :] = state[r].astype(f32)


def conv_kernel(state, south, north, dw, dwb, conv, padded):
    rows, cols, channels = state.shape
    fill_rows(padded, state, south, north)

    def step_of(step, _):
        base = pl.multiple_of(step * 8, 8)
        field = lambda h, at: padded[h, pl.ds(at, 8), :]
        sums = conv_block(field, base, dw, dwb, rows, channels)
        for r in range(rows):
            conv[r, pl.ds(base, 8), :] = sums[r]
        return 0

    lax.fori_loop(1, cols // 8 - 1, step_of, 0)


def block_kernel(
    state, south, north, left, right, conv, forcing, cotangent, land, weight_index, weight_table,
    dw, dwb, gain, nbias, up, upb, down, downb, scale, up_t, down_t,
    result, terms, grad_conv, grads, field, edge, acc_up, acc_down, entry_weights, spread,
):
    rows, cols, channels = state.shape
    wide = 16
    for side in range(2):
        own = slice(0, wide) if side == 0 else slice(cols - wide, cols)
        at = PAD if side == 0 else 0
        edge[side, 0:MARGIN, at : at + wide, :] = south[:, own, :].astype(f32)
        edge[side, rows + MARGIN : rows + 2 * MARGIN, at : at + wide, :] = north[:, own, :].astype(f32)
        for r in range(rows):
            edge[side, r + MARGIN, at : at + wide, :] = state[r, own, :].astype(f32)
        for h in range(rows + 2 * MARGIN):
            if side == 0:
                edge[side, h, PAD - MARGIN : PAD, :] = left[h].astype(f32)
            else:
                edge[side, h, wide : wide + MARGIN, :] = right[h].astype(f32)
        sums = conv_block(
            lambda h, at: edge[side, h, pl.ds(at, 8), :], 0, dw, dwb, rows, channels
        )
        out = slice(0, 8) if side == 0 else slice(cols - 8, cols)
        for r in range(rows):
            field[r, out, :] = sums[r]
    for r in range(rows):
        field[r, 8 : cols - 8, :] = conv[r, 8 : cols - 8, :]

    index = weight_index[...]
    looked_up = jnp.zeros(index.shape, f32)
    for k in range(weight_table.shape[0]):
        looked_up = jnp.where(index == k, weight_table[k], looked_up)
    entry_weights[...] = looked_up
    acc_up[...] = jnp.zeros_like(acc_up)
    acc_down[...] = jnp.zeros_like(acc_down)
    group = 2
    size = group * cols
    fan = terms.shape[0] // (rows * cols)
    lines = fan * size // channels

    def column(ref, first, count):
        width = ref.shape[1]
        return jnp.concatenate(
            [
                jnp.broadcast_to(ref[pl.ds(first + k, 1), :].astype(f32), (channels, width)).T
                for k in range(count)
            ],
            axis=0,
        )

    def mlp_step(step, _):
        first = step * group
        here = field[pl.ds(first, group)].reshape(size, channels)
        average = jnp.mean(here, axis=-1, keepdims=True)
        centred = here - average
        variance = jnp.mean(centred * centred, axis=-1, keepdims=True)
        inv_std = lax.rsqrt(variance + 1e-06)
        normed = centred * inv_std
        force = forcing[pl.ds(first, group)].reshape(size, channels).astype(f32)
        mixed = (normed * gain[...] + nbias[...] + force).astype(bf16)
        pre = jnp.dot(mixed, up[...], preferred_element_type=f32) + upb[...]
        square = pre * pre
        tanh_value = jnp.tanh(pre * (gelu_scale + gelu_scale * cubic_coef * square))
        half = 0.5 + 0.5 * tanh_value
        hidden = (pre * half).astype(bf16)
        slope = half + pre * (1.0 - tanh_value * tanh_value) * (
            0.5 * gelu_scale + 1.5 * gelu_scale * cubic_coef * square
        )
        projected = jnp.dot(hidden, down[...], preferred_element_type=f32) + downb[...]
        ocean = column(land, first, group)
        own = state[pl.ds(first, group)].reshape(size, channels).astype(f32)
        out = ocean * (own + scale[...] * projected)
        result[pl.ds(first, group)] = out.astype(bf16).reshape(group, cols, channels)
        cot = cotangent[pl.ds(first, group)].reshape(size, channels).astype(f32)
        grad_out = (ocean * scale[...] * cot).astype(bf16)
        grad_hidden = jnp.dot(grad_out, down_t[...], preferred_element_type=f32)
        grad_pre = (grad_hidden * slope).astype(bf16)
        gmix = jnp.dot(grad_pre, up_t[...], preferred_element_type=f32)
        at = pl.multiple_of(step * size, 8)
        spread[...] = column(entry_weights, step * lines, lines)
        for k in range(fan):
            weights = spread[pl.ds(k, size, stride=fan), :]
            terms[pl.ds(k * rows * cols + at, size), :] = weights * gmix
        gained = gmix * gain[...]
        gconv = inv_std * (
            gained
            - jnp.mean(gained, axis=-1, keepdims=True)
            - normed * jnp.mean(gained * normed, axis=-1, keepdims=True)
        )
        grad_conv[pl.ds(first, group)] = gconv.reshape(group, cols, channels)
        contract = (((0,), (0,)), ((), ()))
        acc_up[...] += lax.dot_general(mixed, grad_pre, contract, preferred_element_type=f32)
        acc_down[...] += lax.dot_general(grad_out, hidden, contract, preferred_element_type=f32)
        return 0

    lax.fori_loop(0, rows // group, mlp_step, 0)
    blocks = up.shape[1] // channels
    for k in range(blocks):
        part = slice(k * channels, (k + 1) * channels)
        grads[k] = acc_up[:, part]
        grads[blocks + k] = acc_down[:, part].T


def conv_grad_kernel(state, south, north, left, right, grad_conv, out, padded):
    rows, cols, channels = grad_conv.shape
    height = rows + 2 * MARGIN
    fill_rows(padded, state, south, north)
    for h in range(height):
        padded[h, PAD - MARGIN : PAD, :] = left[h].astype(f32)
        padded[h, PAD + cols : PAD + cols + MARGIN, :] = right[h].astype(f32)
    out[...] = jnp.zeros_like(out)
    unroll = 2
    for b in range(TAPS):

        def step_of(step, sums):
            sums = list(sums)
            for u in range(unroll):
                base = pl.multiple_of((step * unroll + u) * 8, 8)
                gc = [grad_conv[r, pl.ds(base, 8), :] for r in range(rows)]
                for h in range(height):
                    x = padded[h, pl.ds(base + (PAD - MARGIN + b), 8), :]
                    for a in range(TAPS):
                        if 0 <= h - a < rows:
                            k = a * 2 + (h - a) % 2
                            sums[k] = sums[k] + gc[h - a] * x
            return tuple(sums)

        zero = jnp.zeros((8, channels), f32)
        sums = lax.fori_loop(0, cols // (8 * unroll), step_of, (zero,) * (2 * TAPS))
        for a in range(TAPS):
            total = sums[2 * a] + sums[2 * a + 1]
            out[pl.ds(a * TAPS + b, 1), :] = jnp.sum(total, axis=0, keepdims=True)


def first_at_least(keys, bound):
    def step_of(_, ends):
        low, high = ends
        middle = (low + high) // 2
        below = keys[middle] < bound
        open_ = low < high
        return (
            jnp.where(open_ & below, middle + 1, low),
            jnp.where(open_ & ~below, middle, high),
        )

    steps = keys.shape[0].bit_length()
    return lax.fori_loop(0, steps, step_of, (jnp.int32(0), jnp.int32(keys.shape[0])))[0]


def add_entries(keys, key_lines, terms, table, block, first_group, groups):
    shift = (terms.shape[0] - 1).bit_length()
    size = block.shape[0]
    group_shift = shift + GROUP.bit_length() - 1
    begin = first_at_least(keys, first_group << group_shift)
    end = first_at_least(keys, (first_group + groups) << group_shift)

    def step_of(step, _):
        base = step * size
        for k in range(size):
            name = keys[base + k] & ((1 << shift) - 1)
            block[pl.ds(k, 1), :] = terms[pl.ds(name, 1), :]
        values = block[...].astype(bf16)
        rows = key_lines[pl.ds(step, 1), :] >> shift
        low = jnp.maximum(keys[base] >> group_shift, first_group)
        high = jnp.minimum(keys[base + size - 1] >> group_shift, first_group + groups - 1)

        def add_group(group, _):
            local = jnp.broadcast_to(rows - group * GROUP, (GROUP, size))
            hit = local == lax.broadcasted_iota(jnp.int32, (GROUP, size), 0)
            one_hot = jnp.where(hit, 1.0, 0.0).astype(bf16)
            at = pl.ds(pl.multiple_of((group - first_group) * GROUP, GROUP), GROUP)
            table[at, :] += jnp.dot(one_hot, values, preferred_element_type=f32)
            return 0

        lax.fori_loop(low, high + 1, add_group, 0)
        return 0

    lax.fori_loop(begin // size, (end + size - 1) // size, step_of, 0)


def in_chunks(rows, body):
    chunk = 512

    def step_of(step, _):
        body(pl.ds(pl.multiple_of(step * chunk, chunk), chunk))
        return 0

    lax.fori_loop(0, rows // chunk, step_of, 0)


def send_kernel(keys, key_lines, terms, out, table, block):
    rows = table.shape[0]

    def clear(at):
        table[at, :] = jnp.zeros((at.size, table.shape[1]), f32)

    def give(at):
        out[at, :] = table[at, :].astype(bf16)

    in_chunks(rows, clear)
    add_entries(keys, key_lines, terms, table, block, rows // GROUP, rows // GROUP)
    in_chunks(rows, give)


def keep_kernel(keys, key_lines, terms, got, kept, send_a, send_b, table, block):
    rows = table.shape[0]

    def fill(at):
        table[at, :] = got[at, :].astype(f32)

    in_chunks(rows, fill)
    add_entries(keys, key_lines, terms, table, block, 0, rows // GROUP)
    quarter = rows // 4
    for part, send in enumerate((send_a, send_b)):
        lower = part * 2 * quarter

        def give(at):
            kept[part, at, :] = table[pl.ds(lower + at.start, at.size), :]
            send[at, :] = table[pl.ds(lower + quarter + at.start, at.size), :].astype(bf16)

        in_chunks(quarter, give)


def swap_bit(array, bit):
    pairs = [(i, i ^ (1 << bit)) for i in range(lax.axis_size("lon"))]
    return lax.ppermute(array, "lon", pairs)


def after(array, *others):
    return lax.optimization_barrier((array,) + others)[0]


def on_device(
    state, forcing, cotangent, land_mask, dw_weight, dw_bias, norm_gain, norm_bias,
    up_weight, up_bias, down_weight, down_bias, layer_scale, owner, atmos_cell, weight_index,
    intersection_weights,
):
    rows, cols, channels = state.shape
    cells = rows * cols
    hid = up_weight.shape[1]
    lat_count = lax.axis_size("lat")
    lon_count = lax.axis_size("lon")
    lat = lax.axis_index("lat")
    lon = lax.axis_index("lon")
    lon_bits = lon_count.bit_length() - 1
    devices = lat_count * lon_count
    entries = owner.shape[0]
    fan = entries // cells

    low_rows = state[:MARGIN]
    high_rows = state[rows - MARGIN :]
    odd = lat % 2 == 1
    last = lat == lat_count - 1
    even_pairs, odd_pairs = [], []
    for l in range(lat_count):
        for j in range(lon_count):
            here = l * lon_count + j
            even_pairs.append((here, (l ^ 1) * lon_count + j))
            beyond = l + 1 if l % 2 else l - 1
            if l == lat_count - 1:
                odd_pairs.append((here, l * lon_count + lon_count - 1 - j))
            elif beyond >= 0:
                odd_pairs.append((here, beyond * lon_count + j))
    got_even = lax.ppermute(jnp.where(odd, low_rows, high_rows), ("lat", "lon"), even_pairs)
    got_odd = lax.ppermute(
        jnp.where(last, high_rows[::-1, ::-1], jnp.where(odd, high_rows, low_rows)),
        ("lat", "lon"),
        odd_pairs,
    )
    south = jnp.where(odd, got_even, got_odd)
    north = jnp.where(odd, got_odd, got_even)

    forward = [(i, (i + 1) % lon_count) for i in range(lon_count)]
    backward = [(t, s) for s, t in forward]
    column = lambda part: jnp.concatenate([south[:, part], state[:, part], north[:, part]], axis=0)
    left = lax.ppermute(column(slice(cols - MARGIN, cols)), "lon", forward)
    right = lax.ppermute(column(slice(0, MARGIN)), "lon", backward)

    lat_relative = (owner[:, 0] // lon_count) ^ lat
    relative = (owner[:, 0] % lon_count) ^ lon
    rest = list(range(1, lon_bits))
    orders = [rest, rest[::-1]]
    width = A_DEV // 2
    half_rows = devices // 2 * A_DEV
    numbers = []
    for order in orders:
        number = jnp.zeros_like(relative)
        for bit in order:
            number = number * 2 + ((relative >> bit) & 1)
        numbers.append(number * lat_count + lat_relative)
    upper = (atmos_cell >= width).astype(jnp.int32)
    block = jnp.where(upper == 1, numbers[1], numbers[0])
    row = (relative & 1) * half_rows + upper * (half_rows // 2) + block * width
    row = row + atmos_cell - upper * width
    entry = jnp.arange(entries, dtype=jnp.int32)
    shift = (entries - 1).bit_length()
    keys = (row << shift) + (entry % fan) * cells + entry // fan
    keys = lax.sort(keys, is_stable=False)
    key_lines = keys.reshape(-1, channels)

    line = lambda v: v.reshape(1, -1)
    taps = dw_weight.reshape(-1, channels).astype(f32)
    conv = pl.pallas_call(
        conv_kernel,
        out_shape=shape((rows, cols, channels), f32),
        in_specs=[vmem()] * 5,
        out_specs=vmem(),
        scratch_shapes=[pltpu.VMEM((rows + 2 * MARGIN, cols + 2 * PAD, channels), f32)],
        compiler_params=params(),
        cost_estimate=cost(10),
        name="conv",
    )(state, south, north, taps, line(dw_bias))
    result, terms, grad_conv, grads = pl.pallas_call(
        block_kernel,
        out_shape=(
            shape((rows, cols, channels), bf16),
            shape((entries, channels), f32),
            shape((rows, cols, channels), f32),
            shape((2 * hid // channels, channels, channels), f32),
        ),
        in_specs=[vmem()] * 10 + [smem()] + [vmem()] * 11,
        out_specs=[vmem()] * 4,
        scratch_shapes=[
            pltpu.VMEM((rows, cols, channels), f32),
            pltpu.VMEM((2, rows + 2 * MARGIN, 24, channels), f32),
            pltpu.VMEM((channels, hid), f32),
            pltpu.VMEM((channels, hid), f32),
            pltpu.VMEM((entries // channels, channels), f32),
            pltpu.VMEM((2 * fan * cols, channels), f32),
        ],
        compiler_params=params(),
        cost_estimate=cost(13),
        name="block",
    )(
        state, south, north, left, right, conv, forcing, cotangent, land_mask,
        weight_index.reshape(-1, channels), intersection_weights, taps, line(dw_bias), line(norm_gain), line(norm_bias), up_weight, line(up_bias),
        down_weight, line(down_bias), line(layer_scale), up_weight.T, down_weight.T,
    )

    block = pltpu.VMEM((channels, channels), f32)
    send = pl.pallas_call(
        send_kernel,
        out_shape=shape((half_rows, channels), bf16),
        in_specs=[smem(), vmem(), vmem()],
        out_specs=vmem(),
        scratch_shapes=[pltpu.VMEM((half_rows, channels), f32), block],
        compiler_params=params(),
        cost_estimate=cost(6),
        name="send_table",
    )(keys, key_lines, terms)
    got = swap_bit(send, 0)

    tap_count = dw_weight.shape[0] * dw_weight.shape[1]
    dw_rows = -(-tap_count // devices) * devices
    grad_dw = pl.pallas_call(
        conv_grad_kernel,
        out_shape=shape((dw_rows, channels), f32),
        in_specs=[vmem()] * 6,
        out_specs=vmem(),
        scratch_shapes=[pltpu.VMEM((rows + 2 * MARGIN, cols + 2 * PAD, channels), f32)],
        compiler_params=params(),
        cost_estimate=cost(9),
        name="conv_grad",
    )(state, south, north, left, right, after(grad_conv, send))

    quarter = half_rows // 4
    kept, send_a, send_b = pl.pallas_call(
        keep_kernel,
        out_shape=(
            shape((2, quarter, channels), f32),
            shape((quarter, channels), bf16),
            shape((quarter, channels), bf16),
        ),
        in_specs=[smem(), vmem(), vmem(), vmem()],
        out_specs=[vmem()] * 3,
        scratch_shapes=[pltpu.VMEM((half_rows, channels), f32), block],
        compiler_params=params(),
        cost_estimate=cost(7),
        name="keep_table",
    )(keys, key_lines, after(terms, grad_dw), got)

    sends = [send_a, send_b]
    kept = [kept[0], kept[1]]
    for stage in range(len(rest)):
        arrived = [swap_bit(sends[q], orders[q][stage]) for q in range(2)]
        if stage + 1 < len(rest):
            size = kept[0].shape[0] // 2
            for q in range(2):
                sends[q] = (kept[q][size:] + arrived[q][size:].astype(f32)).astype(bf16)
                kept[q] = kept[q][:size] + arrived[q][:size].astype(f32)
        else:
            kept = [kept[q] + arrived[q].astype(f32) for q in range(2)]
    lined = jnp.concatenate([p.reshape(lat_count, width, channels) for p in kept], axis=1)
    forcing_grad = lined[0]
    for distance in range(1, lat_count):
        pairs = [(i, i ^ distance) for i in range(lat_count)]
        arrived = lax.ppermute(lined[distance].astype(bf16), "lat", pairs)
        forcing_grad = forcing_grad + arrived.astype(f32)

    total = jnp.concatenate([grads.reshape(2 * hid, channels), grad_dw], axis=0).astype(bf16)
    total = total.reshape(devices, -1, channels)
    total = lax.all_to_all(total, ("lat", "lon"), split_axis=0, concat_axis=0, tiled=True)
    total = jnp.sum(total.astype(f32), axis=0, keepdims=True).astype(bf16)
    total = jnp.broadcast_to(total, (devices,) + total.shape[1:])
    total = lax.all_to_all(total, ("lat", "lon"), split_axis=0, concat_axis=0, tiled=True)
    scale = float(cells * devices) ** (-0.5)
    total = total.reshape(-1, channels).astype(f32) * scale
    grad_up = total[:hid].reshape(hid // channels, channels, channels)
    grad_up = grad_up.transpose(1, 0, 2).reshape(channels, hid)
    grad_down = total[hid : 2 * hid]
    grad_dw = total[2 * hid : 2 * hid + tap_count].reshape(dw_weight.shape)
    return (result, grad_dw, grad_up, grad_down, forcing_grad)


def solution(mesh):
    grid = P("lat", "lon", None)
    in_specs = (grid, grid, grid, P("lat", "lon")) + (P(),) * 9
    in_specs += (P(("lat", "lon"), None), P(("lat", "lon")), P(("lat", "lon")), P())
    out_specs = (grid, P(), P(), P(), P(("lat", "lon"), None))
    return jax.shard_map(
        on_device, mesh=mesh, in_specs=in_specs, out_specs=out_specs, check_vma=False
    )
```

```python
import functools

import jax
import jax.numpy as jnp
from jax import lax
from jax.experimental import pallas as pl
from jax.experimental.pallas import tpu as pltpu
from jax.sharding import PartitionSpec as P

A_DEV = 512
PAD = 8
TAPS = 7
MARGIN = 3
BATCH = 16
BATCHES = 2
gelu_scale = 0.7978845608028654
cubic_coef = 0.044715
f32 = jnp.float32
bf16 = jnp.bfloat16
shape = jax.ShapeDtypeStruct


def params(mebibytes=40):
    return pltpu.CompilerParams(vmem_limit_bytes=mebibytes << 20)


def cost(microseconds):
    return pl.CostEstimate(flops=int(microseconds * 1e9), bytes_accessed=0, transcendentals=0)


def vmem():
    return pl.BlockSpec(memory_space=pltpu.VMEM)


def anywhere():
    return pl.BlockSpec(memory_space=pl.ANY)


def smem():
    return pl.BlockSpec(memory_space=pltpu.SMEM)


def in_chunks(rows, body):
    chunk = 512

    def step_of(step, _):
        body(pl.ds(pl.multiple_of(step * chunk, chunk), chunk))
        return 0

    lax.fori_loop(0, rows // chunk, step_of, 0)


def conv_block(field, base, dw, dwb, rows, channels):
    sums = [jnp.broadcast_to(dwb[...], (8, channels)) for _ in range(rows)]
    for b in range(TAPS):
        weights = [
            jnp.broadcast_to(dw[pl.ds(a * TAPS + b, 1), :], (8, channels)) for a in range(TAPS)
        ]
        for h in range(rows + TAPS - 1):
            x = field(h, base + (PAD - MARGIN + b))
            for a in range(TAPS):
                if 0 <= h - a < rows:
                    sums[h - a] = sums[h - a] + weights[a] * x
    return sums


def fill_rows(padded, state, south, north):
    rows, cols, _ = state.shape
    inner = slice(PAD, PAD + cols)
    padded[0:MARGIN, inner, :] = south[...].astype(f32)
    padded[rows + MARGIN : rows + 2 * MARGIN, inner, :] = north[...].astype(f32)
    for r in range(rows):
        padded[r + MARGIN, inner, :] = state[r].astype(f32)


def conv_kernel(state, south, north, dw, dwb, conv, padded):
    rows, cols, channels = state.shape
    fill_rows(padded, state, south, north)

    def step_of(step, _):
        base = pl.multiple_of(step * 8, 8)
        field = lambda h, at: padded[h, pl.ds(at, 8), :]
        sums = conv_block(field, base, dw, dwb, rows, channels)
        for r in range(rows):
            conv[r, pl.ds(base, 8), :] = sums[r]
        return 0

    lax.fori_loop(1, cols // 8 - 1, step_of, 0)


def block_kernel(
    state, south, north, left, right, conv, forcing, cotangent, land, weight_index, weight_table,
    target_list, clash_list, dw, dwb, gain, nbias, up, upb, down, downb, scale, up_t, down_t,
    result, keep_0, keep_1, keep_2, keep_3, send, grad_conv, grads,
    field, edge, acc_up, acc_down, entry_weights, spread, terms, table, targets, clash, sems,
):
    rows, cols, channels = state.shape
    scalar_copies = [
        pltpu.make_async_copy(target_list, targets, sems.at[0]),
        pltpu.make_async_copy(clash_list, clash, sems.at[1]),
    ]
    for copy in scalar_copies:
        copy.start()
    wide = 16
    for side in range(2):
        own = slice(0, wide) if side == 0 else slice(cols - wide, cols)
        at = PAD if side == 0 else 0
        edge[side, 0:MARGIN, at : at + wide, :] = south[:, own, :].astype(f32)
        edge[side, rows + MARGIN : rows + 2 * MARGIN, at : at + wide, :] = north[:, own, :].astype(f32)
        for r in range(rows):
            edge[side, r + MARGIN, at : at + wide, :] = state[r, own, :].astype(f32)
        for h in range(rows + 2 * MARGIN):
            if side == 0:
                edge[side, h, PAD - MARGIN : PAD, :] = left[h].astype(f32)
            else:
                edge[side, h, wide : wide + MARGIN, :] = right[h].astype(f32)
        sums = conv_block(
            lambda h, at: edge[side, h, pl.ds(at, 8), :], 0, dw, dwb, rows, channels
        )
        out = slice(0, 8) if side == 0 else slice(cols - 8, cols)
        for r in range(rows):
            field[r, out, :] = sums[r]
    for r in range(rows):
        field[r, 8 : cols - 8, :] = conv[r, 8 : cols - 8, :]

    def clear(at):
        table[at, :] = jnp.zeros((at.size, channels), f32)

    in_chunks(table.shape[0], clear)
    index = weight_index[...]
    looked_up = jnp.zeros(index.shape, f32)
    for k in range(weight_table.shape[0]):
        looked_up = jnp.where(index == k, weight_table[k], looked_up)
    entry_weights[...] = looked_up
    acc_up[...] = jnp.zeros_like(acc_up)
    acc_down[...] = jnp.zeros_like(acc_down)
    group = 2
    size = group * cols
    fan = terms.shape[0] // size
    lines = fan * size // channels

    def column(ref, first, count):
        width = ref.shape[1]
        return jnp.concatenate(
            [
                jnp.broadcast_to(ref[pl.ds(first + k, 1), :].astype(f32), (channels, width)).T
                for k in range(count)
            ],
            axis=0,
        )

    def mlp_step(step, _):
        first = step * group
        here = field[pl.ds(first, group)].reshape(size, channels)
        average = jnp.mean(here, axis=-1, keepdims=True)
        centred = here - average
        variance = jnp.mean(centred * centred, axis=-1, keepdims=True)
        inv_std = lax.rsqrt(variance + 1e-06)
        normed = centred * inv_std
        force = forcing[pl.ds(first, group)].reshape(size, channels).astype(f32)
        mixed = (normed * gain[...] + nbias[...] + force).astype(bf16)
        pre = jnp.dot(mixed, up[...], preferred_element_type=f32) + upb[...]
        square = pre * pre
        tanh_value = jnp.tanh(pre * (gelu_scale + gelu_scale * cubic_coef * square))
        half = 0.5 + 0.5 * tanh_value
        hidden = (pre * half).astype(bf16)
        slope = half + pre * (1.0 - tanh_value * tanh_value) * (
            0.5 * gelu_scale + 1.5 * gelu_scale * cubic_coef * square
        )
        projected = jnp.dot(hidden, down[...], preferred_element_type=f32) + downb[...]
        ocean = column(land, first, group)
        own = state[pl.ds(first, group)].reshape(size, channels).astype(f32)
        out = ocean * (own + scale[...] * projected)
        result[pl.ds(first, group)] = out.astype(bf16).reshape(group, cols, channels)
        cot = cotangent[pl.ds(first, group)].reshape(size, channels).astype(f32)
        grad_out = (ocean * scale[...] * cot).astype(bf16)
        grad_hidden = jnp.dot(grad_out, down_t[...], preferred_element_type=f32)
        grad_pre = (grad_hidden * slope).astype(bf16)
        gmix = jnp.dot(grad_pre, up_t[...], preferred_element_type=f32)
        spread[...] = column(entry_weights, step * lines, lines)
        for k in range(fan):
            weights = spread[pl.ds(k, size, stride=fan), :]
            terms[pl.ds(k * size, size), :] = weights * gmix
        gained = gmix * gain[...]
        gconv = inv_std * (
            gained
            - jnp.mean(gained, axis=-1, keepdims=True)
            - normed * jnp.mean(gained * normed, axis=-1, keepdims=True)
        )
        grad_conv[pl.ds(first, group)] = gconv.reshape(group, cols, channels)
        contract = (((0,), (0,)), ((), ()))
        acc_up[...] += lax.dot_general(mixed, grad_pre, contract, preferred_element_type=f32)
        acc_down[...] += lax.dot_general(grad_out, hidden, contract, preferred_element_type=f32)

        @pl.when(step == 0)
        def _():
            for copy in scalar_copies:
                copy.wait()

        unit = BATCH * BATCHES
        units = fan * size // unit

        def add_unit(index, _):
            first_cell = index * (unit // fan)
            first_entry = step * (fan * size) + index * unit

            def entry(k):
                cell = first_cell + k // fan
                return targets[first_entry + k], terms[pl.ds((k % fan) * size + cell, 1), :]

            clashing = clash[first_entry]

            @pl.when(clashing == 0)
            def _():
                for batch in range(BATCHES):
                    found = [entry(batch * BATCH + k) for k in range(BATCH)]
                    sums = [table[pl.ds(t, 1), :] + v for t, v in found]
                    for (t, _), value in zip(found, sums):
                        table[pl.ds(t, 1), :] = value

            @pl.when(clashing != 0)
            def _():
                for k in range(unit):
                    t, v = entry(k)
                    table[pl.ds(t, 1), :] = table[pl.ds(t, 1), :] + v

            return 0

        lax.fori_loop(0, units, add_unit, 0)
        return 0

    lax.fori_loop(0, rows // group, mlp_step, 0)
    half = table.shape[0] // 2

    keep_copies = [
        pltpu.make_async_copy(table.at[pl.ds(k * (half // 4), half // 4)], keep, sems.at[2 + k])
        for k, keep in enumerate((keep_0, keep_1, keep_2, keep_3))
    ]
    for copy in keep_copies:
        copy.start()

    def give(at):
        send[at, :] = table[pl.ds(half + at.start, at.size), :].astype(bf16)

    in_chunks(half, give)
    blocks = up.shape[1] // channels
    for k in range(blocks):
        part = slice(k * channels, (k + 1) * channels)
        grads[k] = acc_up[:, part]
        grads[blocks + k] = acc_down[:, part].T
    for copy in keep_copies:
        copy.wait()


def target_kernel(lat_count, lon_count, orders, owner, cell, targets, clash):
    lat, lon = lax.axis_index("lat"), lax.axis_index("lon")
    lon_bits = lon_count.bit_length() - 1
    half_rows = lat_count * lon_count // 2 * A_DEV
    width = A_DEV // 2
    device = owner[...]
    at_lat = (device >> lon_bits) ^ lat
    at_lon = (device & (lon_count - 1)) ^ lon
    numbers = []
    for order in orders:
        number = jnp.zeros_like(device)
        for bit in order:
            number = number * 2 + ((at_lon >> bit) & 1)
        numbers.append(number * lat_count + at_lat)
    upper = (cell[...] >= width).astype(jnp.int32)
    block = jnp.where(upper == 1, numbers[1], numbers[0])
    row = (at_lon & 1) * half_rows + upper * (half_rows // 2) + block * width
    row = row + cell[...] - upper * width
    targets[...] = row
    lane = lax.broadcasted_iota(jnp.int32, row.shape, 1)
    twice = jnp.zeros_like(row)
    for distance in range(1, BATCH):
        same = (row == pltpu.roll(row, distance, 1)) & (lane % BATCH >= distance)
        twice = jnp.where(same, 1, twice)
    distance = 1
    while distance < BATCH * BATCHES:
        twice = jnp.maximum(twice, pltpu.roll(twice, row.shape[1] - distance, 1))
        distance *= 2
    clash[...] = twice


def conv_grad_kernel(state, south, north, left, right, grad_conv, out, padded):
    rows, cols, channels = grad_conv.shape
    height = rows + 2 * MARGIN
    fill_rows(padded, state, south, north)
    for h in range(height):
        padded[h, PAD - MARGIN : PAD, :] = left[h].astype(f32)
        padded[h, PAD + cols : PAD + cols + MARGIN, :] = right[h].astype(f32)
    out[...] = jnp.zeros_like(out)
    unroll = 2
    for b in range(TAPS):

        def step_of(step, sums):
            sums = list(sums)
            for u in range(unroll):
                base = pl.multiple_of((step * unroll + u) * 8, 8)
                gc = [grad_conv[r, pl.ds(base, 8), :] for r in range(rows)]
                for h in range(height):
                    x = padded[h, pl.ds(base + (PAD - MARGIN + b), 8), :]
                    for a in range(TAPS):
                        if 0 <= h - a < rows:
                            k = a * 2 + (h - a) % 2
                            sums[k] = sums[k] + gc[h - a] * x
            return tuple(sums)

        zero = jnp.zeros((8, channels), f32)
        sums = lax.fori_loop(0, cols // (8 * unroll), step_of, (zero,) * (2 * TAPS))
        for a in range(TAPS):
            total = sums[2 * a] + sums[2 * a + 1]
            out[pl.ds(a * TAPS + b, 1), :] = jnp.sum(total, axis=0, keepdims=True)


def swap_bit(array, bit):
    pairs = [(i, i ^ (1 << bit)) for i in range(lax.axis_size("lon"))]
    return lax.ppermute(array, "lon", pairs)


def after(array, *others):
    return lax.optimization_barrier((array,) + others)[0]


def on_device(
    state, forcing, cotangent, land_mask, dw_weight, dw_bias, norm_gain, norm_bias,
    up_weight, up_bias, down_weight, down_bias, layer_scale, owner, atmos_cell, weight_index,
    intersection_weights,
):
    rows, cols, channels = state.shape
    cells = rows * cols
    hid = up_weight.shape[1]
    lat_count = lax.axis_size("lat")
    lon_count = lax.axis_size("lon")
    lat = lax.axis_index("lat")
    lon = lax.axis_index("lon")
    lon_bits = lon_count.bit_length() - 1
    devices = lat_count * lon_count
    entries = owner.shape[0]
    fan = entries // cells

    low_rows = state[:MARGIN]
    high_rows = state[rows - MARGIN :]
    odd = lat % 2 == 1
    last = lat == lat_count - 1
    even_pairs, odd_pairs = [], []
    for l in range(lat_count):
        for j in range(lon_count):
            here = l * lon_count + j
            even_pairs.append((here, (l ^ 1) * lon_count + j))
            beyond = l + 1 if l % 2 else l - 1
            if l == lat_count - 1:
                odd_pairs.append((here, l * lon_count + lon_count - 1 - j))
            elif beyond >= 0:
                odd_pairs.append((here, beyond * lon_count + j))
    got_even = lax.ppermute(jnp.where(odd, low_rows, high_rows), ("lat", "lon"), even_pairs)
    got_odd = lax.ppermute(
        jnp.where(last, high_rows[::-1, ::-1], jnp.where(odd, high_rows, low_rows)),
        ("lat", "lon"),
        odd_pairs,
    )
    south = jnp.where(odd, got_even, got_odd)
    north = jnp.where(odd, got_odd, got_even)

    forward = [(i, (i + 1) % lon_count) for i in range(lon_count)]
    backward = [(t, s) for s, t in forward]
    column = lambda part: jnp.concatenate([south[:, part], state[:, part], north[:, part]], axis=0)
    left = lax.ppermute(column(slice(cols - MARGIN, cols)), "lon", forward)
    right = lax.ppermute(column(slice(0, MARGIN)), "lon", backward)

    rest = list(range(1, lon_bits))
    orders = [rest, rest[::-1]]
    width = A_DEV // 2
    half_rows = devices // 2 * A_DEV
    lines = (entries // channels, channels)
    targets, clash = pl.pallas_call(
        functools.partial(target_kernel, lat_count, lon_count, orders),
        out_shape=(shape(lines, jnp.int32),) * 2,
        in_specs=[vmem()] * 2,
        out_specs=[vmem()] * 2,
        cost_estimate=cost(1),
        name="targets",
    )(owner.reshape(lines), atmos_cell.reshape(lines))

    line = lambda v: v.reshape(1, -1)
    taps = dw_weight.reshape(-1, channels).astype(f32)
    conv = pl.pallas_call(
        conv_kernel,
        out_shape=shape((rows, cols, channels), f32),
        in_specs=[vmem()] * 5,
        out_specs=vmem(),
        scratch_shapes=[pltpu.VMEM((rows + 2 * MARGIN, cols + 2 * PAD, channels), f32)],
        compiler_params=params(),
        cost_estimate=cost(10),
        name="conv",
    )(state, south, north, taps, line(dw_bias))
    quarter = shape((half_rows // 4, channels), f32)
    result, *keep, send, grad_conv, grads = pl.pallas_call(
        block_kernel,
        out_shape=(
            shape((rows, cols, channels), bf16),
            *(quarter,) * 4,
            shape((half_rows, channels), bf16),
            shape((rows, cols, channels), f32),
            shape((2 * hid // channels, channels, channels), f32),
        ),
        in_specs=[vmem()] * 10 + [smem()] + [anywhere()] * 2 + [vmem()] * 11,
        out_specs=[vmem()] + [anywhere()] * 4 + [vmem()] * 3,
        scratch_shapes=[
            pltpu.VMEM((rows, cols, channels), f32),
            pltpu.VMEM((2, rows + 2 * MARGIN, 24, channels), f32),
            pltpu.VMEM((channels, hid), f32),
            pltpu.VMEM((channels, hid), f32),
            pltpu.VMEM((entries // channels, channels), f32),
            pltpu.VMEM((2 * fan * cols, channels), f32),
            pltpu.VMEM((2 * fan * cols, channels), f32),
            pltpu.VMEM((2 * half_rows, channels), f32),
            pltpu.SMEM((entries,), jnp.int32),
            pltpu.SMEM((entries,), jnp.int32),
            pltpu.SemaphoreType.DMA((6,)),
        ],
        compiler_params=params(min(60, 28 + (half_rows * channels * 10 >> 20))),
        cost_estimate=cost(28),
        name="block",
    )(
        state, south, north, left, right, conv, forcing, cotangent, land_mask,
        weight_index.reshape(-1, channels), intersection_weights,
        targets.reshape(-1), clash.reshape(-1), taps, line(dw_bias), line(norm_gain), line(norm_bias), up_weight, line(up_bias),
        down_weight, line(down_bias), line(layer_scale), up_weight.T, down_weight.T,
    )

    got = swap_bit(send, 0)

    tap_count = dw_weight.shape[0] * dw_weight.shape[1]
    dw_rows = -(-tap_count // devices) * devices
    grad_dw = pl.pallas_call(
        conv_grad_kernel,
        out_shape=shape((dw_rows, channels), f32),
        in_specs=[vmem()] * 6,
        out_specs=vmem(),
        scratch_shapes=[pltpu.VMEM((rows + 2 * MARGIN, cols + 2 * PAD, channels), f32)],
        compiler_params=params(),
        cost_estimate=cost(9),
        name="conv_grad",
    )(state, south, north, left, right, after(grad_conv, send))

    size = half_rows // 4
    got = after(got, grad_dw)
    merged = [keep[k] + got[k * size : (k + 1) * size].astype(f32) for k in range(4)]
    kept = [merged[0], merged[2]]
    sends = [merged[1].astype(bf16), merged[3].astype(bf16)]
    for stage in range(len(rest)):
        arrived = [swap_bit(sends[q], orders[q][stage]) for q in range(2)]
        if stage + 1 < len(rest):
            size = kept[0].shape[0] // 2
            for q in range(2):
                sends[q] = (kept[q][size:] + arrived[q][size:].astype(f32)).astype(bf16)
                kept[q] = kept[q][:size] + arrived[q][:size].astype(f32)
        else:
            kept = [kept[q] + arrived[q].astype(f32) for q in range(2)]
    lined = jnp.concatenate([p.reshape(lat_count, width, channels) for p in kept], axis=1)
    forcing_grad = lined[0]
    for distance in range(1, lat_count):
        pairs = [(i, i ^ distance) for i in range(lat_count)]
        arrived = lax.ppermute(lined[distance].astype(bf16), "lat", pairs)
        forcing_grad = forcing_grad + arrived.astype(f32)

    total = jnp.concatenate([grads.reshape(2 * hid, channels), grad_dw], axis=0).astype(bf16)
    total = total.reshape(devices, -1, channels)
    total = lax.all_to_all(total, ("lat", "lon"), split_axis=0, concat_axis=0, tiled=True)
    total = jnp.sum(total.astype(f32), axis=0, keepdims=True).astype(bf16)
    total = jnp.broadcast_to(total, (devices,) + total.shape[1:])
    total = lax.all_to_all(total, ("lat", "lon"), split_axis=0, concat_axis=0, tiled=True)
    scale = float(cells * devices) ** (-0.5)
    total = total.reshape(-1, channels).astype(f32) * scale
    grad_up = total[:hid].reshape(hid // channels, channels, channels)
    grad_up = grad_up.transpose(1, 0, 2).reshape(channels, hid)
    grad_down = total[hid : 2 * hid]
    grad_dw = total[2 * hid : 2 * hid + tap_count].reshape(dw_weight.shape)
    return (result, grad_dw, grad_up, grad_down, forcing_grad)


def solution(mesh):
    grid = P("lat", "lon", None)
    in_specs = (grid, grid, grid, P("lat", "lon")) + (P(),) * 9
    in_specs += (P(("lat", "lon"), None), P(("lat", "lon")), P(("lat", "lon")), P())
    out_specs = (grid, P(), P(), P(), P(("lat", "lon"), None))
    return jax.shard_map(
        on_device, mesh=mesh, in_specs=in_specs, out_specs=out_specs, check_vma=False
    )
```

```python
import functools

import jax
import jax.numpy as jnp
from jax import lax
from jax.experimental import pallas as pl
from jax.experimental.pallas import tpu as pltpu
from jax.sharding import PartitionSpec as P

A_DEV = 512
PAD = 8
TAPS = 7
MARGIN = 3
BATCH = 16
BATCHES = 2
gelu_scale = 0.7978845608028654
cubic_coef = 0.044715
f32 = jnp.float32
bf16 = jnp.bfloat16
shape = jax.ShapeDtypeStruct


def params(mebibytes=40):
    return pltpu.CompilerParams(vmem_limit_bytes=mebibytes << 20)


def cost(microseconds):
    return pl.CostEstimate(flops=int(microseconds * 1e9), bytes_accessed=0, transcendentals=0)


def vmem():
    return pl.BlockSpec(memory_space=pltpu.VMEM)


def anywhere():
    return pl.BlockSpec(memory_space=pl.ANY)


def smem():
    return pl.BlockSpec(memory_space=pltpu.SMEM)


def in_chunks(rows, body):
    chunk = 512

    def step_of(step, _):
        body(pl.ds(pl.multiple_of(step * chunk, chunk), chunk))
        return 0

    lax.fori_loop(0, rows // chunk, step_of, 0)


def conv_sums(field, base, dw, starts, lines, rows):
    sums = dict(zip(rows, starts))
    for b in range(TAPS):
        weights = [
            jnp.broadcast_to(dw[pl.ds(a * TAPS + b, 1), :], (8, dw.shape[1])) for a in range(TAPS)
        ]
        for h in lines:
            x = field(h, base + (PAD - MARGIN + b))
            for a in range(TAPS):
                if h - a in sums:
                    sums[h - a] = sums[h - a] + weights[a] * x
    return [sums[r] for r in rows]


def edge_kernel(state, even, odd, *, bands):
    rows, cols, channels = state.shape
    lat = lax.axis_index("lat")

    @pl.when(lat % 2 == 1)
    def _():
        even[...] = state[0:MARGIN]
        odd[...] = state[rows - MARGIN : rows]

    @pl.when(lat % 2 == 0)
    def _():
        even[...] = state[rows - MARGIN : rows]
        odd[...] = state[0:MARGIN]

    @pl.when(lat == bands - 1)
    def _():
        column = lax.broadcasted_iota(jnp.int32, (cols, cols), 1)
        line = lax.broadcasted_iota(jnp.int32, (cols, cols), 0)
        reverse = jnp.where(line + column == cols - 1, 1.0, 0.0).astype(bf16)
        for m in range(MARGIN):
            turned = jnp.dot(reverse, state[rows - 1 - m], preferred_element_type=f32)
            odd[m] = turned.astype(bf16)


def inner_conv_kernel(state, dw, dwb, conv, padded):
    rows, cols, channels = state.shape
    for r in range(rows):
        padded[r, PAD : PAD + cols, :] = state[r].astype(f32)

    def step_of(step, _):
        base = pl.multiple_of(step * 8, 8)
        field = lambda h, at: padded[h - MARGIN, pl.ds(at, 8), :]
        bias = jnp.broadcast_to(dwb[...], (8, channels))
        lines = range(MARGIN, rows + MARGIN)
        sums = conv_sums(field, base, dw, [bias] * rows, lines, list(range(rows)))
        for r in range(rows):
            conv[r, pl.ds(base, 8), :] = sums[r]
        return 0

    lax.fori_loop(1, cols // 8 - 1, step_of, 0)


def halo_conv_kernel(south, north, dw, conv, padded, *, rows):
    _, cols, channels = south.shape
    padded[0:MARGIN, PAD : PAD + cols, :] = south[...].astype(f32)
    padded[MARGIN : 2 * MARGIN, PAD : PAD + cols, :] = north[...].astype(f32)

    def step_of(step, _):
        base = pl.multiple_of(step * 8, 8)
        zero = jnp.zeros((8, channels), f32)
        for side in range(2):
            first = 0 if side == 0 else rows + MARGIN
            field = lambda h, at: padded[h - first + side * MARGIN, pl.ds(at, 8), :]
            out = [k if side == 0 else rows - MARGIN + k for k in range(MARGIN)]
            lines = range(first, first + MARGIN)
            sums = conv_sums(field, base, dw, [zero] * MARGIN, lines, out)
            for k in range(MARGIN):
                conv[side * MARGIN + k, pl.ds(base, 8), :] = sums[k]
        return 0

    lax.fori_loop(1, cols // 8 - 1, step_of, 0)


def fill_rows(padded, state, south, north):
    rows, cols, _ = state.shape
    inner = slice(PAD, PAD + cols)
    padded[0:MARGIN, inner, :] = south[...].astype(f32)
    padded[rows + MARGIN : rows + 2 * MARGIN, inner, :] = north[...].astype(f32)
    for r in range(rows):
        padded[r + MARGIN, inner, :] = state[r].astype(f32)


def block_kernel(
    state, south, north, left, right, conv, halo, forcing, cotangent, land, weight_index, weight_table,
    target_list, clash_list, dw, dwb, gain, nbias, up, upb, down, downb, scale, up_t, down_t,
    result, keep_0, keep_1, keep_2, keep_3, send, grad_conv, grads,
    field, edge, acc_up, acc_down, entry_weights, spread, terms, table, targets, clash, sems,
):
    rows, cols, channels = state.shape
    scalar_copies = [
        pltpu.make_async_copy(target_list, targets, sems.at[0]),
        pltpu.make_async_copy(clash_list, clash, sems.at[1]),
    ]
    for copy in scalar_copies:
        copy.start()
    wide = 16
    for side in range(2):
        own = slice(0, wide) if side == 0 else slice(cols - wide, cols)
        at = PAD if side == 0 else 0
        edge[side, 0:MARGIN, at : at + wide, :] = south[:, own, :].astype(f32)
        edge[side, rows + MARGIN : rows + 2 * MARGIN, at : at + wide, :] = north[:, own, :].astype(f32)
        for r in range(rows):
            edge[side, r + MARGIN, at : at + wide, :] = state[r, own, :].astype(f32)
        for h in range(rows + 2 * MARGIN):
            if side == 0:
                edge[side, h, PAD - MARGIN : PAD, :] = left[h].astype(f32)
            else:
                edge[side, h, wide : wide + MARGIN, :] = right[h].astype(f32)
        bias = jnp.broadcast_to(dwb[...], (8, channels))
        lines = range(rows + 2 * MARGIN)
        at_edge = lambda h, at: edge[side, h, pl.ds(at, 8), :]
        sums = conv_sums(at_edge, 0, dw, [bias] * rows, lines, list(range(rows)))
        out = slice(0, 8) if side == 0 else slice(cols - 8, cols)
        for r in range(rows):
            field[r, out, :] = sums[r]
    inner = slice(8, cols - 8)
    for r in range(rows):
        here = conv[r, inner, :]
        if r < MARGIN:
            here = here + halo[r, inner, :]
        if r >= rows - MARGIN:
            here = here + halo[r - rows + 2 * MARGIN, inner, :]
        field[r, inner, :] = here

    def clear(at):
        table[at, :] = jnp.zeros((at.size, channels), f32)

    in_chunks(table.shape[0], clear)
    index = weight_index[...]
    looked_up = jnp.zeros(index.shape, f32)
    for k in range(weight_table.shape[0]):
        looked_up = jnp.where(index == k, weight_table[k], looked_up)
    entry_weights[...] = looked_up
    acc_up[...] = jnp.zeros_like(acc_up)
    acc_down[...] = jnp.zeros_like(acc_down)
    group = 2
    size = group * cols
    fan = terms.shape[0] // size
    lines = fan * size // channels

    def column(ref, first, count):
        width = ref.shape[1]
        return jnp.concatenate(
            [
                jnp.broadcast_to(ref[pl.ds(first + k, 1), :].astype(f32), (channels, width)).T
                for k in range(count)
            ],
            axis=0,
        )

    def mlp_step(step, _):
        first = step * group
        here = field[pl.ds(first, group)].reshape(size, channels)
        average = jnp.mean(here, axis=-1, keepdims=True)
        centred = here - average
        variance = jnp.mean(centred * centred, axis=-1, keepdims=True)
        inv_std = lax.rsqrt(variance + 1e-06)
        normed = centred * inv_std
        force = forcing[pl.ds(first, group)].reshape(size, channels).astype(f32)
        mixed = (normed * gain[...] + nbias[...] + force).astype(bf16)
        pre = jnp.dot(mixed, up[...], preferred_element_type=f32) + upb[...]
        square = pre * pre
        tanh_value = jnp.tanh(pre * (gelu_scale + gelu_scale * cubic_coef * square))
        half = 0.5 + 0.5 * tanh_value
        hidden = (pre * half).astype(bf16)
        slope = half + pre * (1.0 - tanh_value * tanh_value) * (
            0.5 * gelu_scale + 1.5 * gelu_scale * cubic_coef * square
        )
        projected = jnp.dot(hidden, down[...], preferred_element_type=f32) + downb[...]
        ocean = column(land, first, group)
        own = state[pl.ds(first, group)].reshape(size, channels).astype(f32)
        out = ocean * (own + scale[...] * projected)
        result[pl.ds(first, group)] = out.astype(bf16).reshape(group, cols, channels)
        cot = cotangent[pl.ds(first, group)].reshape(size, channels).astype(f32)
        grad_out = (ocean * scale[...] * cot).astype(bf16)
        grad_hidden = jnp.dot(grad_out, down_t[...], preferred_element_type=f32)
        grad_pre = (grad_hidden * slope).astype(bf16)
        gmix = jnp.dot(grad_pre, up_t[...], preferred_element_type=f32)
        spread[...] = column(entry_weights, step * lines, lines)
        for k in range(fan):
            weights = spread[pl.ds(k, size, stride=fan), :]
            terms[pl.ds(k * size, size), :] = weights * gmix
        gained = gmix * gain[...]
        gconv = inv_std * (
            gained
            - jnp.mean(gained, axis=-1, keepdims=True)
            - normed * jnp.mean(gained * normed, axis=-1, keepdims=True)
        )
        grad_conv[pl.ds(first, group)] = gconv.reshape(group, cols, channels)
        contract = (((0,), (0,)), ((), ()))
        acc_up[...] += lax.dot_general(mixed, grad_pre, contract, preferred_element_type=f32)
        acc_down[...] += lax.dot_general(grad_out, hidden, contract, preferred_element_type=f32)

        @pl.when(step == 0)
        def _():
            for copy in scalar_copies:
                copy.wait()

        unit = BATCH * BATCHES
        units = fan * size // unit

        def add_unit(index, _):
            first_cell = index * (unit // fan)
            first_entry = step * (fan * size) + index * unit

            def entry(k):
                cell = first_cell + k // fan
                return targets[first_entry + k], terms[pl.ds((k % fan) * size + cell, 1), :]

            clashing = clash[first_entry]

            @pl.when(clashing == 0)
            def _():
                for batch in range(BATCHES):
                    found = [entry(batch * BATCH + k) for k in range(BATCH)]
                    sums = [table[pl.ds(t, 1), :] + v for t, v in found]
                    for (t, _), value in zip(found, sums):
                        table[pl.ds(t, 1), :] = value

            @pl.when(clashing != 0)
            def _():
                for k in range(unit):
                    t, v = entry(k)
                    table[pl.ds(t, 1), :] = table[pl.ds(t, 1), :] + v

            return 0

        lax.fori_loop(0, units, add_unit, 0)
        return 0

    lax.fori_loop(0, rows // group, mlp_step, 0)
    half = table.shape[0] // 2

    keep_copies = [
        pltpu.make_async_copy(table.at[pl.ds(k * (half // 4), half // 4)], keep, sems.at[2 + k])
        for k, keep in enumerate((keep_0, keep_1, keep_2, keep_3))
    ]
    for copy in keep_copies:
        copy.start()

    def give(at):
        send[at, :] = table[pl.ds(half + at.start, at.size), :].astype(bf16)

    in_chunks(half, give)
    blocks = up.shape[1] // channels
    for k in range(blocks):
        part = slice(k * channels, (k + 1) * channels)
        grads[k] = acc_up[:, part]
        grads[blocks + k] = acc_down[:, part].T
    for copy in keep_copies:
        copy.wait()


def target_kernel(lat_count, lon_count, orders, owner, cell, targets, clash):
    lat, lon = lax.axis_index("lat"), lax.axis_index("lon")
    lon_bits = lon_count.bit_length() - 1
    half_rows = lat_count * lon_count // 2 * A_DEV
    width = A_DEV // 2
    device = owner[...]
    at_lat = (device >> lon_bits) ^ lat
    at_lon = (device & (lon_count - 1)) ^ lon
    numbers = []
    for order in orders:
        number = jnp.zeros_like(device)
        for bit in order:
            number = number * 2 + ((at_lon >> bit) & 1)
        numbers.append(number * lat_count + at_lat)
    upper = (cell[...] >= width).astype(jnp.int32)
    block = jnp.where(upper == 1, numbers[1], numbers[0])
    row = (at_lon & 1) * half_rows + upper * (half_rows // 2) + block * width
    row = row + cell[...] - upper * width
    targets[...] = row
    lane = lax.broadcasted_iota(jnp.int32, row.shape, 1)
    twice = jnp.zeros_like(row)
    for distance in range(1, BATCH):
        same = (row == pltpu.roll(row, distance, 1)) & (lane % BATCH >= distance)
        twice = jnp.where(same, 1, twice)
    distance = 1
    while distance < BATCH * BATCHES:
        twice = jnp.maximum(twice, pltpu.roll(twice, row.shape[1] - distance, 1))
        distance *= 2
    clash[...] = twice


def conv_grad_kernel(state, south, north, left, right, grad_conv, out, padded):
    rows, cols, channels = grad_conv.shape
    height = rows + 2 * MARGIN
    fill_rows(padded, state, south, north)
    for h in range(height):
        padded[h, PAD - MARGIN : PAD, :] = left[h].astype(f32)
        padded[h, PAD + cols : PAD + cols + MARGIN, :] = right[h].astype(f32)
    out[...] = jnp.zeros_like(out)
    unroll = 2
    for b in range(TAPS):

        def step_of(step, sums):
            sums = list(sums)
            for u in range(unroll):
                base = pl.multiple_of((step * unroll + u) * 8, 8)
                gc = [grad_conv[r, pl.ds(base, 8), :] for r in range(rows)]
                for h in range(height):
                    x = padded[h, pl.ds(base + (PAD - MARGIN + b), 8), :]
                    for a in range(TAPS):
                        if 0 <= h - a < rows:
                            k = a * 2 + (h - a) % 2
                            sums[k] = sums[k] + gc[h - a] * x
            return tuple(sums)

        zero = jnp.zeros((8, channels), f32)
        sums = lax.fori_loop(0, cols // (8 * unroll), step_of, (zero,) * (2 * TAPS))
        for a in range(TAPS):
            total = sums[2 * a] + sums[2 * a + 1]
            out[pl.ds(a * TAPS + b, 1), :] = jnp.sum(total, axis=0, keepdims=True)


def swap_bit(array, bit):
    pairs = [(i, i ^ (1 << bit)) for i in range(lax.axis_size("lon"))]
    return lax.ppermute(array, "lon", pairs)


def after(array, *others):
    return lax.optimization_barrier((array,) + others)[0]


def on_device(
    state, forcing, cotangent, land_mask, dw_weight, dw_bias, norm_gain, norm_bias,
    up_weight, up_bias, down_weight, down_bias, layer_scale, owner, atmos_cell, weight_index,
    intersection_weights,
):
    rows, cols, channels = state.shape
    cells = rows * cols
    hid = up_weight.shape[1]
    lat_count = lax.axis_size("lat")
    lon_count = lax.axis_size("lon")
    lat = lax.axis_index("lat")
    lon = lax.axis_index("lon")
    lon_bits = lon_count.bit_length() - 1
    devices = lat_count * lon_count
    entries = owner.shape[0]
    fan = entries // cells

    odd = lat % 2 == 1
    even_pairs, odd_pairs = [], []
    for l in range(lat_count):
        for j in range(lon_count):
            here = l * lon_count + j
            even_pairs.append((here, (l ^ 1) * lon_count + j))
            beyond = l + 1 if l % 2 else l - 1
            if l == lat_count - 1:
                odd_pairs.append((here, l * lon_count + lon_count - 1 - j))
            elif beyond >= 0:
                odd_pairs.append((here, beyond * lon_count + j))
    edge_rows = shape((MARGIN, cols, channels), bf16)
    for_even, for_odd = pl.pallas_call(
        functools.partial(edge_kernel, bands=lat_count),
        out_shape=(edge_rows, edge_rows),
        in_specs=[vmem()],
        out_specs=[vmem()] * 2,
        cost_estimate=cost(1),
        name="edges",
    )(state)
    got_even = lax.ppermute(for_even, ("lat", "lon"), even_pairs)
    got_odd = lax.ppermute(for_odd, ("lat", "lon"), odd_pairs)
    south = jnp.where(odd, got_even, got_odd)
    north = jnp.where(odd, got_odd, got_even)

    forward = [(i, (i + 1) % lon_count) for i in range(lon_count)]
    backward = [(t, s) for s, t in forward]
    column = lambda part: jnp.concatenate([south[:, part], state[:, part], north[:, part]], axis=0)
    left = lax.ppermute(column(slice(cols - MARGIN, cols)), "lon", forward)
    right = lax.ppermute(column(slice(0, MARGIN)), "lon", backward)

    rest = list(range(1, lon_bits))
    orders = [rest, rest[::-1]]
    width = A_DEV // 2
    half_rows = devices // 2 * A_DEV
    lines = (entries // channels, channels)
    targets, clash = pl.pallas_call(
        functools.partial(target_kernel, lat_count, lon_count, orders),
        out_shape=(shape(lines, jnp.int32),) * 2,
        in_specs=[vmem()] * 2,
        out_specs=[vmem()] * 2,
        cost_estimate=cost(1),
        name="targets",
    )(owner.reshape(lines), atmos_cell.reshape(lines))

    line = lambda v: v.reshape(1, -1)
    taps = dw_weight.reshape(-1, channels).astype(f32)
    conv = pl.pallas_call(
        inner_conv_kernel,
        out_shape=shape((rows, cols, channels), f32),
        in_specs=[vmem()] * 3,
        out_specs=vmem(),
        scratch_shapes=[pltpu.VMEM((rows, cols + 2 * PAD, channels), f32)],
        compiler_params=params(),
        cost_estimate=cost(7),
        name="inner_conv",
    )(after(state, for_even), taps, line(dw_bias))
    halo = pl.pallas_call(
        functools.partial(halo_conv_kernel, rows=rows),
        out_shape=shape((2 * MARGIN, cols, channels), f32),
        in_specs=[vmem()] * 3,
        out_specs=vmem(),
        scratch_shapes=[pltpu.VMEM((2 * MARGIN, cols + 2 * PAD, channels), f32)],
        compiler_params=params(),
        cost_estimate=cost(2),
        name="halo_conv",
    )(south, north, taps)
    quarter = shape((half_rows // 4, channels), f32)
    result, *keep, send, grad_conv, grads = pl.pallas_call(
        block_kernel,
        out_shape=(
            shape((rows, cols, channels), bf16),
            *(quarter,) * 4,
            shape((half_rows, channels), bf16),
            shape((rows, cols, channels), f32),
            shape((2 * hid // channels, channels, channels), f32),
        ),
        in_specs=[vmem()] * 11 + [smem()] + [anywhere()] * 2 + [vmem()] * 11,
        out_specs=[vmem()] + [anywhere()] * 4 + [vmem()] * 3,
        scratch_shapes=[
            pltpu.VMEM((rows, cols, channels), f32),
            pltpu.VMEM((2, rows + 2 * MARGIN, 24, channels), f32),
            pltpu.VMEM((channels, hid), f32),
            pltpu.VMEM((channels, hid), f32),
            pltpu.VMEM((entries // channels, channels), f32),
            pltpu.VMEM((2 * fan * cols, channels), f32),
            pltpu.VMEM((2 * fan * cols, channels), f32),
            pltpu.VMEM((2 * half_rows, channels), f32),
            pltpu.SMEM((entries,), jnp.int32),
            pltpu.SMEM((entries,), jnp.int32),
            pltpu.SemaphoreType.DMA((6,)),
        ],
        compiler_params=params(min(60, 28 + (half_rows * channels * 10 >> 20))),
        cost_estimate=cost(28),
        name="block",
    )(
        state, south, north, left, right, conv, halo, forcing, cotangent, land_mask,
        weight_index.reshape(-1, channels), intersection_weights,
        targets.reshape(-1), clash.reshape(-1), taps, line(dw_bias), line(norm_gain), line(norm_bias), up_weight, line(up_bias),
        down_weight, line(down_bias), line(layer_scale), up_weight.T, down_weight.T,
    )

    got = swap_bit(send, 0)

    tap_count = dw_weight.shape[0] * dw_weight.shape[1]
    dw_rows = -(-tap_count // devices) * devices
    grad_dw = pl.pallas_call(
        conv_grad_kernel,
        out_shape=shape((dw_rows, channels), f32),
        in_specs=[vmem()] * 6,
        out_specs=vmem(),
        scratch_shapes=[pltpu.VMEM((rows + 2 * MARGIN, cols + 2 * PAD, channels), f32)],
        compiler_params=params(),
        cost_estimate=cost(9),
        name="conv_grad",
    )(state, south, north, left, right, after(grad_conv, send))

    size = half_rows // 4
    got = after(got, grad_dw)
    slices = [(keep[k], got[k * size : (k + 1) * size]) for k in range(4)]
    add = lambda summands: functools.reduce(lambda x, y: x + y.astype(f32), summands)
    sends = [add(slices[1]).astype(bf16), add(slices[3]).astype(bf16)]
    first_sends = sends
    held = [list(slices[0]), list(slices[2])]
    for stage in range(len(rest)):
        arrived = [swap_bit(sends[q], orders[q][stage]) for q in range(2)]
        arrived = lax.optimization_barrier(tuple(arrived))
        for q in range(2):
            held[q].append(arrived[q])
        if stage + 1 < len(rest):
            size //= 2
            sends = [add([h[size : 2 * size] for h in held[q]]).astype(bf16) for q in range(2)]
            held = [[h[:size] for h in held[q]] for q in range(2)]
    def for_band(distance):
        at = slice(distance * width, (distance + 1) * width)
        return jnp.concatenate([add([h[at] for h in held[q]]) for q in range(2)], axis=0)

    forcing_grad = for_band(0)
    for distance in range(1, lat_count):
        pairs = [(i, i ^ distance) for i in range(lat_count)]
        arrived = lax.ppermute(for_band(distance).astype(bf16), "lat", pairs)
        forcing_grad = forcing_grad + arrived.astype(f32)

    total = jnp.concatenate([grads.reshape(2 * hid, channels), grad_dw], axis=0).astype(bf16)
    total = after(total, *first_sends)
    total = total.reshape(devices, -1, channels)
    total = lax.all_to_all(total, ("lat", "lon"), split_axis=0, concat_axis=0, tiled=True)
    total = jnp.sum(total.astype(f32), axis=0, keepdims=True).astype(bf16)
    total = jnp.broadcast_to(total, (devices,) + total.shape[1:])
    total = lax.all_to_all(total, ("lat", "lon"), split_axis=0, concat_axis=0, tiled=True)
    scale = float(cells * devices) ** (-0.5)
    total = total.reshape(-1, channels).astype(f32) * scale
    grad_up = total[:hid].reshape(hid // channels, channels, channels)
    grad_up = grad_up.transpose(1, 0, 2).reshape(channels, hid)
    grad_down = total[hid : 2 * hid]
    grad_dw = total[2 * hid : 2 * hid + tap_count].reshape(dw_weight.shape)
    return (result, grad_dw, grad_up, grad_down, forcing_grad)


def solution(mesh):
    grid = P("lat", "lon", None)
    in_specs = (grid, grid, grid, P("lat", "lon")) + (P(),) * 9
    in_specs += (P(("lat", "lon"), None), P(("lat", "lon")), P(("lat", "lon")), P())
    out_specs = (grid, P(), P(), P(), P(("lat", "lon"), None))
    return jax.shard_map(
        on_device, mesh=mesh, in_specs=in_specs, out_specs=out_specs, check_vma=False
    )
```

```python
import functools

import jax
import jax.numpy as jnp
from jax import lax
from jax.experimental import pallas as pl
from jax.experimental.pallas import tpu as pltpu
from jax.sharding import PartitionSpec as P

A_DEV = 512
PAD = 8
TAPS = 7
MARGIN = 3
BATCH = 32
SMALL = 8
gelu_scale = 0.7978845608028654
cubic_coef = 0.044715
f32 = jnp.float32
bf16 = jnp.bfloat16
shape = jax.ShapeDtypeStruct


def params(mebibytes=40):
    return pltpu.CompilerParams(vmem_limit_bytes=mebibytes << 20)


def cost(microseconds):
    return pl.CostEstimate(flops=int(microseconds * 1e9), bytes_accessed=0, transcendentals=0)


def vmem():
    return pl.BlockSpec(memory_space=pltpu.VMEM)


def anywhere():
    return pl.BlockSpec(memory_space=pl.ANY)


def smem():
    return pl.BlockSpec(memory_space=pltpu.SMEM)


def in_chunks(rows, body):
    chunk = 512

    def step_of(step, _):
        body(pl.ds(pl.multiple_of(step * chunk, chunk), chunk))
        return 0

    lax.fori_loop(0, rows // chunk, step_of, 0)


def conv_sums(field, base, dw, starts, lines, rows):
    sums = dict(zip(rows, starts))
    for b in range(TAPS):
        weights = [
            jnp.broadcast_to(dw[pl.ds(a * TAPS + b, 1), :], (8, dw.shape[1])) for a in range(TAPS)
        ]
        for h in lines:
            x = field(h, base + (PAD - MARGIN + b))
            for a in range(TAPS):
                if h - a in sums:
                    sums[h - a] = sums[h - a] + weights[a] * x
    return [sums[r] for r in rows]


def edge_kernel(state, even, odd, *, bands):
    rows, cols, channels = state.shape
    lat = lax.axis_index("lat")

    @pl.when(lat % 2 == 1)
    def _():
        even[...] = state[0:MARGIN]
        odd[...] = state[rows - MARGIN : rows]

    @pl.when(lat % 2 == 0)
    def _():
        even[...] = state[rows - MARGIN : rows]
        odd[...] = state[0:MARGIN]

    @pl.when(lat == bands - 1)
    def _():
        column = lax.broadcasted_iota(jnp.int32, (cols, cols), 1)
        line = lax.broadcasted_iota(jnp.int32, (cols, cols), 0)
        reverse = jnp.where(line + column == cols - 1, 1.0, 0.0).astype(bf16)
        for m in range(MARGIN):
            turned = jnp.dot(reverse, state[rows - 1 - m], preferred_element_type=f32)
            odd[m] = turned.astype(bf16)


def inner_conv_kernel(
    lat_count, lon_count, orders, state, dw, dwb, owner, cell, conv, targets, clash, padded
):
    rows, cols, channels = state.shape
    find_targets(lat_count, lon_count, orders, owner, cell, targets, clash)
    for r in range(rows):
        padded[r, PAD : PAD + cols, :] = state[r].astype(f32)

    def step_of(step, _):
        base = pl.multiple_of(step * 8, 8)
        field = lambda h, at: padded[h - MARGIN, pl.ds(at, 8), :]
        bias = jnp.broadcast_to(dwb[...], (8, channels))
        lines = range(MARGIN, rows + MARGIN)
        sums = conv_sums(field, base, dw, [bias] * rows, lines, list(range(rows)))
        for r in range(rows):
            conv[r, pl.ds(base, 8), :] = sums[r]
        return 0

    lax.fori_loop(1, cols // 8 - 1, step_of, 0)


def halo_conv_kernel(south, north, dw, conv, padded, *, rows):
    _, cols, channels = south.shape
    padded[0:MARGIN, PAD : PAD + cols, :] = south[...].astype(f32)
    padded[MARGIN : 2 * MARGIN, PAD : PAD + cols, :] = north[...].astype(f32)

    def step_of(step, _):
        base = pl.multiple_of(step * 8, 8)
        zero = jnp.zeros((8, channels), f32)
        for side in range(2):
            first = 0 if side == 0 else rows + MARGIN
            field = lambda h, at: padded[h - first + side * MARGIN, pl.ds(at, 8), :]
            out = [k if side == 0 else rows - MARGIN + k for k in range(MARGIN)]
            lines = range(first, first + MARGIN)
            sums = conv_sums(field, base, dw, [zero] * MARGIN, lines, out)
            for k in range(MARGIN):
                conv[side * MARGIN + k, pl.ds(base, 8), :] = sums[k]
        return 0

    lax.fori_loop(1, cols // 8 - 1, step_of, 0)


def fill_rows(padded, state, south, north):
    rows, cols, _ = state.shape
    inner = slice(PAD, PAD + cols)
    padded[0:MARGIN, inner, :] = south[...].astype(f32)
    padded[rows + MARGIN : rows + 2 * MARGIN, inner, :] = north[...].astype(f32)
    for r in range(rows):
        padded[r + MARGIN, inner, :] = state[r].astype(f32)


def block_kernel(
    state, south, north, left, right, conv, halo, forcing, cotangent, land, weight_index, weight_table,
    target_list, clash_list, dw, dwb, gain, nbias, up, upb, down, downb, scale, up_t, down_t,
    result, keep_0, keep_1, keep_2, keep_3, send, grad_conv, grads,
    field, edge, acc_up, acc_down, entry_weights, spread, terms, table, targets, clash, sems,
):
    rows, cols, channels = state.shape
    scalar_copies = [
        pltpu.make_async_copy(target_list, targets, sems.at[0]),
        pltpu.make_async_copy(clash_list, clash, sems.at[1]),
    ]
    for copy in scalar_copies:
        copy.start()
    wide = 16
    for side in range(2):
        own = slice(0, wide) if side == 0 else slice(cols - wide, cols)
        at = PAD if side == 0 else 0
        edge[side, 0:MARGIN, at : at + wide, :] = south[:, own, :].astype(f32)
        edge[side, rows + MARGIN : rows + 2 * MARGIN, at : at + wide, :] = north[:, own, :].astype(f32)
        for r in range(rows):
            edge[side, r + MARGIN, at : at + wide, :] = state[r, own, :].astype(f32)
        for h in range(rows + 2 * MARGIN):
            if side == 0:
                edge[side, h, PAD - MARGIN : PAD, :] = left[h].astype(f32)
            else:
                edge[side, h, wide : wide + MARGIN, :] = right[h].astype(f32)
        bias = jnp.broadcast_to(dwb[...], (8, channels))
        lines = range(rows + 2 * MARGIN)
        at_edge = lambda h, at: edge[side, h, pl.ds(at, 8), :]
        sums = conv_sums(at_edge, 0, dw, [bias] * rows, lines, list(range(rows)))
        out = slice(0, 8) if side == 0 else slice(cols - 8, cols)
        for r in range(rows):
            field[r, out, :] = sums[r]
    inner = slice(8, cols - 8)
    for r in range(rows):
        here = conv[r, inner, :]
        if r < MARGIN:
            here = here + halo[r, inner, :]
        if r >= rows - MARGIN:
            here = here + halo[r - rows + 2 * MARGIN, inner, :]
        field[r, inner, :] = here

    def clear(at):
        table[at, :] = jnp.zeros((at.size, channels), f32)

    in_chunks(table.shape[0], clear)
    index = weight_index[...]
    looked_up = jnp.zeros(index.shape, f32)
    for k in range(weight_table.shape[0]):
        looked_up = jnp.where(index == k, weight_table[k], looked_up)
    entry_weights[...] = looked_up
    acc_up[...] = jnp.zeros_like(acc_up)
    acc_down[...] = jnp.zeros_like(acc_down)
    group = 2
    size = group * cols
    fan = terms.shape[0] // size
    lines = fan * size // channels

    def column(ref, first, count):
        width = ref.shape[1]
        return jnp.concatenate(
            [
                jnp.broadcast_to(ref[pl.ds(first + k, 1), :].astype(f32), (channels, width)).T
                for k in range(count)
            ],
            axis=0,
        )

    def mlp_step(step, _):
        first = step * group
        here = field[pl.ds(first, group)].reshape(size, channels)
        average = jnp.mean(here, axis=-1, keepdims=True)
        centred = here - average
        variance = jnp.mean(centred * centred, axis=-1, keepdims=True)
        inv_std = lax.rsqrt(variance + 1e-06)
        normed = centred * inv_std
        force = forcing[pl.ds(first, group)].reshape(size, channels).astype(f32)
        mixed = (normed * gain[...] + nbias[...] + force).astype(bf16)
        pre = jnp.dot(mixed, up[...], preferred_element_type=f32) + upb[...]
        square = pre * pre
        tanh_value = jnp.tanh(pre * (gelu_scale + gelu_scale * cubic_coef * square))
        half = 0.5 + 0.5 * tanh_value
        hidden = (pre * half).astype(bf16)
        slope = half + pre * (1.0 - tanh_value * tanh_value) * (
            0.5 * gelu_scale + 1.5 * gelu_scale * cubic_coef * square
        )
        projected = jnp.dot(hidden, down[...], preferred_element_type=f32) + downb[...]
        ocean = column(land, first, group)
        own = state[pl.ds(first, group)].reshape(size, channels).astype(f32)
        out = ocean * (own + scale[...] * projected)
        result[pl.ds(first, group)] = out.astype(bf16).reshape(group, cols, channels)
        cot = cotangent[pl.ds(first, group)].reshape(size, channels).astype(f32)
        grad_out = (ocean * scale[...] * cot).astype(bf16)
        grad_hidden = jnp.dot(grad_out, down_t[...], preferred_element_type=f32)
        grad_pre = (grad_hidden * slope).astype(bf16)
        gmix = jnp.dot(grad_pre, up_t[...], preferred_element_type=f32)
        spread[...] = column(entry_weights, step * lines, lines)
        for k in range(fan):
            weights = spread[pl.ds(k, size, stride=fan), :]
            terms[pl.ds(k * size, size), :] = weights * gmix
        gained = gmix * gain[...]
        gconv = inv_std * (
            gained
            - jnp.mean(gained, axis=-1, keepdims=True)
            - normed * jnp.mean(gained * normed, axis=-1, keepdims=True)
        )
        grad_conv[pl.ds(first, group)] = gconv.reshape(group, cols, channels)
        contract = (((0,), (0,)), ((), ()))
        acc_up[...] += lax.dot_general(mixed, grad_pre, contract, preferred_element_type=f32)
        acc_down[...] += lax.dot_general(grad_out, hidden, contract, preferred_element_type=f32)

        @pl.when(step == 0)
        def _():
            for copy in scalar_copies:
                copy.wait()

        units = fan * size // BATCH

        def add_unit(index, _):
            first_cell = index * (BATCH // fan)
            first_entry = step * (fan * size) + index * BATCH

            def add_batch(first, count):
                found = []
                for k in range(first, first + count):
                    value = terms[pl.ds((k % fan) * size + first_cell + k // fan, 1), :]
                    found.append((targets[first_entry + k], value))
                sums = [table[pl.ds(t, 1), :] + v for t, v in found]
                for (t, _), value in zip(found, sums):
                    table[pl.ds(t, 1), :] = value

            clashing = clash[first_entry]
            for level, count in enumerate((BATCH, SMALL, 1)):

                @pl.when(clashing == level)
                def _():
                    for first in range(0, BATCH, count):
                        add_batch(first, count)

            return 0

        lax.fori_loop(0, units, add_unit, 0)
        return 0

    lax.fori_loop(0, rows // group, mlp_step, 0)
    half = table.shape[0] // 2

    keep_copies = [
        pltpu.make_async_copy(table.at[pl.ds(k * (half // 4), half // 4)], keep, sems.at[2 + k])
        for k, keep in enumerate((keep_0, keep_1, keep_2, keep_3))
    ]
    for copy in keep_copies:
        copy.start()

    def give(at):
        send[at, :] = table[pl.ds(half + at.start, at.size), :].astype(bf16)

    in_chunks(half, give)
    blocks = up.shape[1] // channels
    for k in range(blocks):
        part = slice(k * channels, (k + 1) * channels)
        grads[k] = acc_up[:, part]
        grads[blocks + k] = acc_down[:, part].T
    for copy in keep_copies:
        copy.wait()


def find_targets(lat_count, lon_count, orders, owner, cell, targets, clash):
    lat, lon = lax.axis_index("lat"), lax.axis_index("lon")
    lon_bits = lon_count.bit_length() - 1
    half_rows = lat_count * lon_count // 2 * A_DEV
    width = A_DEV // 2
    device = owner[...]
    at_lat = (device >> lon_bits) ^ lat
    at_lon = (device & (lon_count - 1)) ^ lon
    numbers = []
    for order in orders:
        number = jnp.zeros_like(device)
        for bit in order:
            number = number * 2 + ((at_lon >> bit) & 1)
        numbers.append(number * lat_count + at_lat)
    upper = (cell[...] >= width).astype(jnp.int32)
    block = jnp.where(upper == 1, numbers[1], numbers[0])
    row = (at_lon & 1) * half_rows + upper * (half_rows // 2) + block * width
    row = row + cell[...] - upper * width
    targets[...] = row
    lane = lax.broadcasted_iota(jnp.int32, row.shape, 1)
    twice = jnp.zeros_like(row)
    for distance in range(BATCH - 1, 0, -1):
        same = row == pltpu.roll(row, distance, 1)
        twice = jnp.where(same & (lane % BATCH >= distance), jnp.maximum(twice, 1), twice)
        if distance < SMALL:
            twice = jnp.where(same & (lane % SMALL >= distance), 2, twice)
    distance = 1
    while distance < BATCH:
        twice = jnp.maximum(twice, pltpu.roll(twice, row.shape[1] - distance, 1))
        distance *= 2
    clash[...] = twice


def conv_grad_kernel(state, south, north, left, right, grad_conv, out, padded):
    rows, cols, channels = grad_conv.shape
    height = rows + 2 * MARGIN
    fill_rows(padded, state, south, north)
    for h in range(height):
        padded[h, PAD - MARGIN : PAD, :] = left[h].astype(f32)
        padded[h, PAD + cols : PAD + cols + MARGIN, :] = right[h].astype(f32)
    out[...] = jnp.zeros_like(out)
    unroll = 2
    for b in range(TAPS):

        def step_of(step, sums):
            sums = list(sums)
            for u in range(unroll):
                base = pl.multiple_of((step * unroll + u) * 8, 8)
                gc = [grad_conv[r, pl.ds(base, 8), :] for r in range(rows)]
                for h in range(height):
                    x = padded[h, pl.ds(base + (PAD - MARGIN + b), 8), :]
                    for a in range(TAPS):
                        if 0 <= h - a < rows:
                            k = a * 2 + (h - a) % 2
                            sums[k] = sums[k] + gc[h - a] * x
            return tuple(sums)

        zero = jnp.zeros((8, channels), f32)
        sums = lax.fori_loop(0, cols // (8 * unroll), step_of, (zero,) * (2 * TAPS))
        for a in range(TAPS):
            total = sums[2 * a] + sums[2 * a + 1]
            out[pl.ds(a * TAPS + b, 1), :] = jnp.sum(total, axis=0, keepdims=True)


def swap_bit(array, bit):
    pairs = [(i, i ^ (1 << bit)) for i in range(lax.axis_size("lon"))]
    return lax.ppermute(array, "lon", pairs)


def after(array, *others):
    return lax.optimization_barrier((array,) + others)[0]


def on_device(
    state, forcing, cotangent, land_mask, dw_weight, dw_bias, norm_gain, norm_bias,
    up_weight, up_bias, down_weight, down_bias, layer_scale, owner, atmos_cell, weight_index,
    intersection_weights,
):
    rows, cols, channels = state.shape
    cells = rows * cols
    hid = up_weight.shape[1]
    lat_count = lax.axis_size("lat")
    lon_count = lax.axis_size("lon")
    lat = lax.axis_index("lat")
    lon = lax.axis_index("lon")
    lon_bits = lon_count.bit_length() - 1
    devices = lat_count * lon_count
    entries = owner.shape[0]
    fan = entries // cells

    odd = lat % 2 == 1
    even_pairs, odd_pairs = [], []
    for l in range(lat_count):
        for j in range(lon_count):
            here = l * lon_count + j
            even_pairs.append((here, (l ^ 1) * lon_count + j))
            beyond = l + 1 if l % 2 else l - 1
            if 0 <= beyond < lat_count:
                odd_pairs.append((here, beyond * lon_count + j))
            else:
                odd_pairs.append((here, l * lon_count + lon_count - 1 - j))
    edge_rows = shape((MARGIN, cols, channels), bf16)
    for_even, for_odd = pl.pallas_call(
        functools.partial(edge_kernel, bands=lat_count),
        out_shape=(edge_rows, edge_rows),
        in_specs=[vmem()],
        out_specs=[vmem()] * 2,
        cost_estimate=cost(1),
        name="edges",
    )(state)
    got_even = lax.ppermute(for_even, ("lat", "lon"), even_pairs)
    got_odd = lax.ppermute(for_odd, ("lat", "lon"), odd_pairs)
    south = jnp.where(odd, got_even, jnp.where(lat == 0, jnp.zeros_like(got_odd), got_odd))
    north = jnp.where(odd, got_odd, got_even)

    forward = [(i, (i + 1) % lon_count) for i in range(lon_count)]
    backward = [(t, s) for s, t in forward]
    column = lambda part: jnp.concatenate([south[:, part], state[:, part], north[:, part]], axis=0)
    left = lax.ppermute(column(slice(cols - MARGIN, cols)), "lon", forward)
    right = lax.ppermute(column(slice(0, MARGIN)), "lon", backward)

    rest = list(range(1, lon_bits))
    orders = [rest, rest[::-1]]
    width = A_DEV // 2
    half_rows = devices // 2 * A_DEV
    lines = (entries // channels, channels)
    line = lambda v: v.reshape(1, -1)
    taps = dw_weight.reshape(-1, channels).astype(f32)
    conv, targets, clash = pl.pallas_call(
        functools.partial(inner_conv_kernel, lat_count, lon_count, orders),
        out_shape=(shape((rows, cols, channels), f32),) + (shape(lines, jnp.int32),) * 2,
        in_specs=[vmem()] * 5,
        out_specs=[vmem()] * 3,
        scratch_shapes=[pltpu.VMEM((rows, cols + 2 * PAD, channels), f32)],
        compiler_params=params(),
        cost_estimate=cost(7),
        name="inner_conv",
    )(
        after(state, for_even), taps, line(dw_bias), owner.reshape(lines), atmos_cell.reshape(lines)
    )
    halo = pl.pallas_call(
        functools.partial(halo_conv_kernel, rows=rows),
        out_shape=shape((2 * MARGIN, cols, channels), f32),
        in_specs=[vmem()] * 3,
        out_specs=vmem(),
        scratch_shapes=[pltpu.VMEM((2 * MARGIN, cols + 2 * PAD, channels), f32)],
        compiler_params=params(),
        cost_estimate=cost(2),
        name="halo_conv",
    )(south, north, taps)
    quarter = shape((half_rows // 4, channels), f32)
    result, *keep, send, grad_conv, grads = pl.pallas_call(
        block_kernel,
        out_shape=(
            shape((rows, cols, channels), bf16),
            *(quarter,) * 4,
            shape((half_rows, channels), bf16),
            shape((rows, cols, channels), f32),
            shape((2 * hid // channels, channels, channels), f32),
        ),
        in_specs=[vmem()] * 11 + [smem()] + [anywhere()] * 2 + [vmem()] * 11,
        out_specs=[vmem()] + [anywhere()] * 4 + [vmem()] * 3,
        scratch_shapes=[
            pltpu.VMEM((rows, cols, channels), f32),
            pltpu.VMEM((2, rows + 2 * MARGIN, 24, channels), f32),
            pltpu.VMEM((channels, hid), f32),
            pltpu.VMEM((channels, hid), f32),
            pltpu.VMEM((entries // channels, channels), f32),
            pltpu.VMEM((2 * fan * cols, channels), f32),
            pltpu.VMEM((2 * fan * cols, channels), f32),
            pltpu.VMEM((2 * half_rows, channels), f32),
            pltpu.SMEM((entries,), jnp.int32),
            pltpu.SMEM((entries,), jnp.int32),
            pltpu.SemaphoreType.DMA((6,)),
        ],
        compiler_params=params(min(60, 28 + (half_rows * channels * 10 >> 20))),
        cost_estimate=cost(28),
        name="block",
    )(
        state, south, north, left, right, conv, halo, forcing, cotangent, land_mask,
        weight_index.reshape(-1, channels), intersection_weights,
        targets.reshape(-1), clash.reshape(-1), taps, line(dw_bias), line(norm_gain), line(norm_bias), up_weight, line(up_bias),
        down_weight, line(down_bias), line(layer_scale), up_weight.T, down_weight.T,
    )

    got = swap_bit(send, 0)

    tap_count = dw_weight.shape[0] * dw_weight.shape[1]
    dw_rows = -(-tap_count // devices) * devices
    grad_dw = pl.pallas_call(
        conv_grad_kernel,
        out_shape=shape((dw_rows, channels), f32),
        in_specs=[vmem()] * 6,
        out_specs=vmem(),
        scratch_shapes=[pltpu.VMEM((rows + 2 * MARGIN, cols + 2 * PAD, channels), f32)],
        compiler_params=params(),
        cost_estimate=cost(9),
        name="conv_grad",
    )(state, south, north, left, right, after(grad_conv, send))

    size = half_rows // 4
    got = after(got, grad_dw)
    slices = [(keep[k], got[k * size : (k + 1) * size]) for k in range(4)]
    add = lambda summands: functools.reduce(lambda x, y: x + y.astype(f32), summands)
    sends = [add(slices[1]).astype(bf16), add(slices[3]).astype(bf16)]
    first_sends = sends
    held = [list(slices[0]), list(slices[2])]
    for stage in range(len(rest)):
        arrived = [swap_bit(sends[q], orders[q][stage]) for q in range(2)]
        arrived = lax.optimization_barrier(tuple(arrived))
        for q in range(2):
            held[q].append(arrived[q])
        if stage + 1 < len(rest):
            size //= 2
            sends = [add([h[size : 2 * size] for h in held[q]]).astype(bf16) for q in range(2)]
            held = [[h[:size] for h in held[q]] for q in range(2)]
    def for_band(distance):
        at = slice(distance * width, (distance + 1) * width)
        return jnp.concatenate([add([h[at] for h in held[q]]) for q in range(2)], axis=0)

    forcing_grad = for_band(0)
    from_bands = []
    for distance in range(1, lat_count):
        pairs = [(i, i ^ distance) for i in range(lat_count)]
        from_bands.append(lax.ppermute(for_band(distance).astype(bf16), "lat", pairs))

    total = jnp.concatenate([grads.reshape(2 * hid, channels), grad_dw], axis=0).astype(bf16)
    total = after(total, *first_sends)
    total = total.reshape(devices, -1, channels)
    total = lax.all_to_all(total, ("lat", "lon"), split_axis=0, concat_axis=0, tiled=True)
    total = jnp.sum(total.astype(f32), axis=0, keepdims=True).astype(bf16)
    total = jnp.broadcast_to(total, (devices,) + total.shape[1:])
    total = lax.all_to_all(total, ("lat", "lon"), split_axis=0, concat_axis=0, tiled=True)
    scale = float(cells * devices) ** (-0.5)
    total = total.reshape(-1, channels).astype(f32) * scale
    grad_up = total[:hid].reshape(hid // channels, channels, channels)
    grad_up = grad_up.transpose(1, 0, 2).reshape(channels, hid)
    grad_down = total[hid : 2 * hid]
    grad_dw = total[2 * hid : 2 * hid + tap_count].reshape(dw_weight.shape)
    arrived, grad_dw, grad_up, grad_down = lax.optimization_barrier(
        (from_bands, grad_dw, grad_up, grad_down)
    )
    forcing_grad = add([forcing_grad] + list(arrived))
    return (result, grad_dw, grad_up, grad_down, forcing_grad)


def solution(mesh):
    grid = P("lat", "lon", None)
    in_specs = (grid, grid, grid, P("lat", "lon")) + (P(),) * 9
    in_specs += (P(("lat", "lon"), None), P(("lat", "lon")), P(("lat", "lon")), P())
    out_specs = (grid, P(), P(), P(), P(("lat", "lon"), None))
    return jax.shard_map(
        on_device, mesh=mesh, in_specs=in_specs, out_specs=out_specs, check_vma=False
    )
```

```python
import functools

import jax
import jax.numpy as jnp
from jax import lax
from jax.experimental import pallas as pl
from jax.experimental.pallas import tpu as pltpu
from jax.sharding import PartitionSpec as P

A_DEV = 512
PAD = 8
TAPS = 7
MARGIN = 3
BATCH = 16
BATCHES = 2
SMALL = 8
gelu_scale = 0.7978845608028654
cubic_coef = 0.044715
f32 = jnp.float32
bf16 = jnp.bfloat16
shape = jax.ShapeDtypeStruct


def params(mebibytes=40):
    return pltpu.CompilerParams(vmem_limit_bytes=mebibytes << 20)


def cost(microseconds):
    return pl.CostEstimate(flops=int(microseconds * 1e9), bytes_accessed=0, transcendentals=0)


def vmem():
    return pl.BlockSpec(memory_space=pltpu.VMEM)


def anywhere():
    return pl.BlockSpec(memory_space=pl.ANY)


def smem():
    return pl.BlockSpec(memory_space=pltpu.SMEM)


def in_chunks(rows, body):
    chunk = 512

    def step_of(step, _):
        body(pl.ds(pl.multiple_of(step * chunk, chunk), chunk))
        return 0

    lax.fori_loop(0, rows // chunk, step_of, 0)


def conv_sums(field, base, dw, starts, lines, rows):
    sums = dict(zip(rows, starts))
    for b in range(TAPS):
        weights = [
            jnp.broadcast_to(dw[pl.ds(a * TAPS + b, 1), :], (8, dw.shape[1])) for a in range(TAPS)
        ]
        for h in lines:
            x = field(h, base + (PAD - MARGIN + b))
            for a in range(TAPS):
                if h - a in sums:
                    sums[h - a] = sums[h - a] + weights[a] * x
    return [sums[r] for r in rows]


def edge_kernel(state, even, odd, *, bands):
    rows, cols, channels = state.shape
    lat = lax.axis_index("lat")

    @pl.when(lat % 2 == 1)
    def _():
        even[...] = state[0:MARGIN]
        odd[...] = state[rows - MARGIN : rows]

    @pl.when(lat % 2 == 0)
    def _():
        even[...] = state[rows - MARGIN : rows]
        odd[...] = state[0:MARGIN]

    @pl.when(lat == bands - 1)
    def _():
        column = lax.broadcasted_iota(jnp.int32, (cols, cols), 1)
        line = lax.broadcasted_iota(jnp.int32, (cols, cols), 0)
        reverse = jnp.where(line + column == cols - 1, 1.0, 0.0).astype(bf16)
        for m in range(MARGIN):
            turned = jnp.dot(reverse, state[rows - 1 - m], preferred_element_type=f32)
            odd[m] = turned.astype(bf16)


def inner_conv_kernel(
    lat_count, lon_count, orders, state, dw, dwb, owner, cell, conv, targets, clash, padded
):
    rows, cols, channels = state.shape
    find_targets(lat_count, lon_count, orders, owner, cell, targets, clash)
    for r in range(rows):
        padded[r, PAD : PAD + cols, :] = state[r].astype(f32)

    def step_of(step, _):
        base = pl.multiple_of(step * 8, 8)
        field = lambda h, at: padded[h - MARGIN, pl.ds(at, 8), :]
        bias = jnp.broadcast_to(dwb[...], (8, channels))
        lines = range(MARGIN, rows + MARGIN)
        sums = conv_sums(field, base, dw, [bias] * rows, lines, list(range(rows)))
        for r in range(rows):
            conv[r, pl.ds(base, 8), :] = sums[r]
        return 0

    lax.fori_loop(1, cols // 8 - 1, step_of, 0)


def halo_conv_kernel(south, north, dw, conv, padded, *, rows):
    _, cols, channels = south.shape
    padded[0:MARGIN, PAD : PAD + cols, :] = south[...].astype(f32)
    padded[MARGIN : 2 * MARGIN, PAD : PAD + cols, :] = north[...].astype(f32)

    def step_of(step, _):
        base = pl.multiple_of(step * 8, 8)
        zero = jnp.zeros((8, channels), f32)
        for side in range(2):
            first = 0 if side == 0 else rows + MARGIN
            field = lambda h, at: padded[h - first + side * MARGIN, pl.ds(at, 8), :]
            out = [k if side == 0 else rows - MARGIN + k for k in range(MARGIN)]
            lines = range(first, first + MARGIN)
            sums = conv_sums(field, base, dw, [zero] * MARGIN, lines, out)
            for k in range(MARGIN):
                conv[side * MARGIN + k, pl.ds(base, 8), :] = sums[k]
        return 0

    lax.fori_loop(1, cols // 8 - 1, step_of, 0)


def fill_rows(padded, state, south, north):
    rows, cols, _ = state.shape
    inner = slice(PAD, PAD + cols)
    padded[0:MARGIN, inner, :] = south[...].astype(f32)
    padded[rows + MARGIN : rows + 2 * MARGIN, inner, :] = north[...].astype(f32)
    for r in range(rows):
        padded[r + MARGIN, inner, :] = state[r].astype(f32)


def block_kernel(
    state, south, north, left, right, conv, halo, forcing, cotangent, land, weight_index, weight_table,
    target_list, clash_list, dw, dwb, gain, nbias, up, upb, down, downb, scale, up_t, down_t,
    result, keep_0, keep_1, keep_2, keep_3, send, grad_conv, grads,
    field, edge, acc_up, acc_down, entry_weights, spread, terms, table, targets, clash, sems,
):
    rows, cols, channels = state.shape
    scalar_copies = [
        pltpu.make_async_copy(target_list, targets, sems.at[0]),
        pltpu.make_async_copy(clash_list, clash, sems.at[1]),
    ]
    for copy in scalar_copies:
        copy.start()
    wide = 16
    for side in range(2):
        own = slice(0, wide) if side == 0 else slice(cols - wide, cols)
        at = PAD if side == 0 else 0
        edge[side, 0:MARGIN, at : at + wide, :] = south[:, own, :].astype(f32)
        edge[side, rows + MARGIN : rows + 2 * MARGIN, at : at + wide, :] = north[:, own, :].astype(f32)
        for r in range(rows):
            edge[side, r + MARGIN, at : at + wide, :] = state[r, own, :].astype(f32)
        for h in range(rows + 2 * MARGIN):
            if side == 0:
                edge[side, h, PAD - MARGIN : PAD, :] = left[h].astype(f32)
            else:
                edge[side, h, wide : wide + MARGIN, :] = right[h].astype(f32)
        bias = jnp.broadcast_to(dwb[...], (8, channels))
        lines = range(rows + 2 * MARGIN)
        at_edge = lambda h, at: edge[side, h, pl.ds(at, 8), :]
        sums = conv_sums(at_edge, 0, dw, [bias] * rows, lines, list(range(rows)))
        out = slice(0, 8) if side == 0 else slice(cols - 8, cols)
        for r in range(rows):
            field[r, out, :] = sums[r]
    inner = slice(8, cols - 8)
    for r in range(rows):
        here = conv[r, inner, :]
        if r < MARGIN:
            here = here + halo[r, inner, :]
        if r >= rows - MARGIN:
            here = here + halo[r - rows + 2 * MARGIN, inner, :]
        field[r, inner, :] = here

    def clear(at):
        table[at, :] = jnp.zeros((at.size, channels), f32)

    in_chunks(table.shape[0], clear)
    index = weight_index[...]
    looked_up = jnp.zeros(index.shape, f32)
    for k in range(weight_table.shape[0]):
        looked_up = jnp.where(index == k, weight_table[k], looked_up)
    entry_weights[...] = looked_up
    acc_up[...] = jnp.zeros_like(acc_up)
    acc_down[...] = jnp.zeros_like(acc_down)
    group = 2
    size = group * cols
    fan = terms.shape[0] // size
    lines = fan * size // channels

    def column(ref, first, count):
        width = ref.shape[1]
        return jnp.concatenate(
            [
                jnp.broadcast_to(ref[pl.ds(first + k, 1), :].astype(f32), (channels, width)).T
                for k in range(count)
            ],
            axis=0,
        )

    def mlp_step(step, _):
        first = step * group
        here = field[pl.ds(first, group)].reshape(size, channels)
        average = jnp.mean(here, axis=-1, keepdims=True)
        centred = here - average
        variance = jnp.mean(centred * centred, axis=-1, keepdims=True)
        inv_std = lax.rsqrt(variance + 1e-06)
        normed = centred * inv_std
        force = forcing[pl.ds(first, group)].reshape(size, channels).astype(f32)
        mixed = (normed * gain[...] + nbias[...] + force).astype(bf16)
        pre = jnp.dot(mixed, up[...], preferred_element_type=f32) + upb[...]
        square = pre * pre
        tanh_value = jnp.tanh(pre * (gelu_scale + gelu_scale * cubic_coef * square))
        half = 0.5 + 0.5 * tanh_value
        hidden = (pre * half).astype(bf16)
        slope = half + pre * (1.0 - tanh_value * tanh_value) * (
            0.5 * gelu_scale + 1.5 * gelu_scale * cubic_coef * square
        )
        projected = jnp.dot(hidden, down[...], preferred_element_type=f32) + downb[...]
        ocean = column(land, first, group)
        own = state[pl.ds(first, group)].reshape(size, channels).astype(f32)
        out = ocean * (own + scale[...] * projected)
        result[pl.ds(first, group)] = out.astype(bf16).reshape(group, cols, channels)
        cot = cotangent[pl.ds(first, group)].reshape(size, channels).astype(f32)
        grad_out = (ocean * scale[...] * cot).astype(bf16)
        grad_hidden = jnp.dot(grad_out, down_t[...], preferred_element_type=f32)
        grad_pre = (grad_hidden * slope).astype(bf16)
        gmix = jnp.dot(grad_pre, up_t[...], preferred_element_type=f32)
        spread[...] = column(entry_weights, step * lines, lines)
        for k in range(fan):
            weights = spread[pl.ds(k, size, stride=fan), :]
            terms[pl.ds(k * size, size), :] = weights * gmix
        gained = gmix * gain[...]
        gconv = inv_std * (
            gained
            - jnp.mean(gained, axis=-1, keepdims=True)
            - normed * jnp.mean(gained * normed, axis=-1, keepdims=True)
        )
        grad_conv[pl.ds(first, group)] = gconv.reshape(group, cols, channels)
        contract = (((0,), (0,)), ((), ()))
        acc_up[...] += lax.dot_general(mixed, grad_pre, contract, preferred_element_type=f32)
        acc_down[...] += lax.dot_general(grad_out, hidden, contract, preferred_element_type=f32)

        @pl.when(step == 0)
        def _():
            for copy in scalar_copies:
                copy.wait()

        unit = BATCH * BATCHES
        units = fan * size // unit

        def add_unit(index, _):
            first_cell = index * (unit // fan)
            first_entry = step * (fan * size) + index * unit

            def add_batch(first, count):
                found = []
                for k in range(first, first + count):
                    value = terms[pl.ds((k % fan) * size + first_cell + k // fan, 1), :]
                    found.append((targets[first_entry + k], value))
                sums = [table[pl.ds(t, 1), :] + v for t, v in found]
                for (t, _), value in zip(found, sums):
                    table[pl.ds(t, 1), :] = value

            clashing = clash[first_entry]
            for level, count in enumerate((BATCH, SMALL, 1)):

                @pl.when(clashing == level)
                def _():
                    for first in range(0, unit, count):
                        add_batch(first, count)

            return 0

        lax.fori_loop(0, units, add_unit, 0)
        return 0

    lax.fori_loop(0, rows // group, mlp_step, 0)
    half = table.shape[0] // 2

    keep_copies = [
        pltpu.make_async_copy(table.at[pl.ds(k * (half // 4), half // 4)], keep, sems.at[2 + k])
        for k, keep in enumerate((keep_0, keep_1, keep_2, keep_3))
    ]
    for copy in keep_copies:
        copy.start()

    def give(at):
        send[at, :] = table[pl.ds(half + at.start, at.size), :].astype(bf16)

    in_chunks(half, give)
    blocks = up.shape[1] // channels
    for k in range(blocks):
        part = slice(k * channels, (k + 1) * channels)
        grads[k] = acc_up[:, part]
        grads[blocks + k] = acc_down[:, part].T
    for copy in keep_copies:
        copy.wait()


def find_targets(lat_count, lon_count, orders, owner, cell, targets, clash):
    lat, lon = lax.axis_index("lat"), lax.axis_index("lon")
    lon_bits = lon_count.bit_length() - 1
    half_rows = lat_count * lon_count // 2 * A_DEV
    width = A_DEV // 2
    device = owner[...]
    at_lat = (device >> lon_bits) ^ lat
    at_lon = (device & (lon_count - 1)) ^ lon
    numbers = []
    for order in orders:
        number = jnp.zeros_like(device)
        for bit in order:
            number = number * 2 + ((at_lon >> bit) & 1)
        numbers.append(number * lat_count + at_lat)
    upper = (cell[...] >= width).astype(jnp.int32)
    block = jnp.where(upper == 1, numbers[1], numbers[0])
    row = (at_lon & 1) * half_rows + upper * (half_rows // 2) + block * width
    row = row + cell[...] - upper * width
    targets[...] = row
    lane = lax.broadcasted_iota(jnp.int32, row.shape, 1)
    twice = jnp.zeros_like(row)
    for distance in range(BATCH - 1, 0, -1):
        same = row == pltpu.roll(row, distance, 1)
        twice = jnp.where(same & (lane % BATCH >= distance), jnp.maximum(twice, 1), twice)
        if distance < SMALL:
            twice = jnp.where(same & (lane % SMALL >= distance), 2, twice)
    distance = 1
    while distance < BATCH * BATCHES:
        twice = jnp.maximum(twice, pltpu.roll(twice, row.shape[1] - distance, 1))
        distance *= 2
    clash[...] = twice


def conv_grad_kernel(state, south, north, left, right, grad_conv, out, padded):
    rows, cols, channels = grad_conv.shape
    height = rows + 2 * MARGIN
    fill_rows(padded, state, south, north)
    for h in range(height):
        padded[h, PAD - MARGIN : PAD, :] = left[h].astype(f32)
        padded[h, PAD + cols : PAD + cols + MARGIN, :] = right[h].astype(f32)
    out[...] = jnp.zeros_like(out)
    unroll = 2
    for b in range(TAPS):

        def step_of(step, sums):
            sums = list(sums)
            for u in range(unroll):
                base = pl.multiple_of((step * unroll + u) * 8, 8)
                gc = [grad_conv[r, pl.ds(base, 8), :] for r in range(rows)]
                for h in range(height):
                    x = padded[h, pl.ds(base + (PAD - MARGIN + b), 8), :]
                    for a in range(TAPS):
                        if 0 <= h - a < rows:
                            k = a * 2 + (h - a) % 2
                            sums[k] = sums[k] + gc[h - a] * x
            return tuple(sums)

        zero = jnp.zeros((8, channels), f32)
        sums = lax.fori_loop(0, cols // (8 * unroll), step_of, (zero,) * (2 * TAPS))
        for a in range(TAPS):
            total = sums[2 * a] + sums[2 * a + 1]
            out[pl.ds(a * TAPS + b, 1), :] = jnp.sum(total, axis=0, keepdims=True)


def swap_bit(array, bit):
    pairs = [(i, i ^ (1 << bit)) for i in range(lax.axis_size("lon"))]
    return lax.ppermute(array, "lon", pairs)


def after(array, *others):
    return lax.optimization_barrier((array,) + others)[0]


def on_device(
    state, forcing, cotangent, land_mask, dw_weight, dw_bias, norm_gain, norm_bias,
    up_weight, up_bias, down_weight, down_bias, layer_scale, owner, atmos_cell, weight_index,
    intersection_weights,
):
    rows, cols, channels = state.shape
    cells = rows * cols
    hid = up_weight.shape[1]
    lat_count = lax.axis_size("lat")
    lon_count = lax.axis_size("lon")
    lat = lax.axis_index("lat")
    lon = lax.axis_index("lon")
    lon_bits = lon_count.bit_length() - 1
    devices = lat_count * lon_count
    entries = owner.shape[0]
    fan = entries // cells

    odd = lat % 2 == 1
    even_pairs, odd_pairs = [], []
    for l in range(lat_count):
        for j in range(lon_count):
            here = l * lon_count + j
            even_pairs.append((here, (l ^ 1) * lon_count + j))
            beyond = l + 1 if l % 2 else l - 1
            if 0 <= beyond < lat_count:
                odd_pairs.append((here, beyond * lon_count + j))
            else:
                odd_pairs.append((here, l * lon_count + lon_count - 1 - j))
    edge_rows = shape((MARGIN, cols, channels), bf16)
    for_even, for_odd = pl.pallas_call(
        functools.partial(edge_kernel, bands=lat_count),
        out_shape=(edge_rows, edge_rows),
        in_specs=[vmem()],
        out_specs=[vmem()] * 2,
        cost_estimate=cost(1),
        name="edges",
    )(state)
    got_even = lax.ppermute(for_even, ("lat", "lon"), even_pairs)
    got_odd = lax.ppermute(for_odd, ("lat", "lon"), odd_pairs)
    south = jnp.where(odd, got_even, jnp.where(lat == 0, jnp.zeros_like(got_odd), got_odd))
    north = jnp.where(odd, got_odd, got_even)

    forward = [(i, (i + 1) % lon_count) for i in range(lon_count)]
    backward = [(t, s) for s, t in forward]
    column = lambda part: jnp.concatenate([south[:, part], state[:, part], north[:, part]], axis=0)
    left = lax.ppermute(column(slice(cols - MARGIN, cols)), "lon", forward)
    right = lax.ppermute(column(slice(0, MARGIN)), "lon", backward)

    rest = list(range(1, lon_bits))
    orders = [rest, rest[::-1]]
    width = A_DEV // 2
    half_rows = devices // 2 * A_DEV
    lines = (entries // channels, channels)
    line = lambda v: v.reshape(1, -1)
    taps = dw_weight.reshape(-1, channels).astype(f32)
    conv, targets, clash = pl.pallas_call(
        functools.partial(inner_conv_kernel, lat_count, lon_count, orders),
        out_shape=(shape((rows, cols, channels), f32),) + (shape(lines, jnp.int32),) * 2,
        in_specs=[vmem()] * 5,
        out_specs=[vmem()] * 3,
        scratch_shapes=[pltpu.VMEM((rows, cols + 2 * PAD, channels), f32)],
        compiler_params=params(),
        cost_estimate=cost(7),
        name="inner_conv",
    )(
        after(state, for_even), taps, line(dw_bias), owner.reshape(lines), atmos_cell.reshape(lines)
    )
    halo = pl.pallas_call(
        functools.partial(halo_conv_kernel, rows=rows),
        out_shape=shape((2 * MARGIN, cols, channels), f32),
        in_specs=[vmem()] * 3,
        out_specs=vmem(),
        scratch_shapes=[pltpu.VMEM((2 * MARGIN, cols + 2 * PAD, channels), f32)],
        compiler_params=params(),
        cost_estimate=cost(2),
        name="halo_conv",
    )(south, north, taps)
    quarter = shape((half_rows // 4, channels), f32)
    result, *keep, send, grad_conv, grads = pl.pallas_call(
        block_kernel,
        out_shape=(
            shape((rows, cols, channels), bf16),
            *(quarter,) * 4,
            shape((half_rows, channels), bf16),
            shape((rows, cols, channels), f32),
            shape((2 * hid // channels, channels, channels), f32),
        ),
        in_specs=[vmem()] * 11 + [smem()] + [anywhere()] * 2 + [vmem()] * 11,
        out_specs=[vmem()] + [anywhere()] * 4 + [vmem()] * 3,
        scratch_shapes=[
            pltpu.VMEM((rows, cols, channels), f32),
            pltpu.VMEM((2, rows + 2 * MARGIN, 24, channels), f32),
            pltpu.VMEM((channels, hid), f32),
            pltpu.VMEM((channels, hid), f32),
            pltpu.VMEM((entries // channels, channels), f32),
            pltpu.VMEM((2 * fan * cols, channels), f32),
            pltpu.VMEM((2 * fan * cols, channels), f32),
            pltpu.VMEM((2 * half_rows, channels), f32),
            pltpu.SMEM((entries,), jnp.int32),
            pltpu.SMEM((entries,), jnp.int32),
            pltpu.SemaphoreType.DMA((6,)),
        ],
        compiler_params=params(min(60, 28 + (half_rows * channels * 10 >> 20))),
        cost_estimate=cost(28),
        name="block",
    )(
        state, south, north, left, right, conv, halo, forcing, cotangent, land_mask,
        weight_index.reshape(-1, channels), intersection_weights,
        targets.reshape(-1), clash.reshape(-1), taps, line(dw_bias), line(norm_gain), line(norm_bias), up_weight, line(up_bias),
        down_weight, line(down_bias), line(layer_scale), up_weight.T, down_weight.T,
    )

    got = swap_bit(send, 0)

    tap_count = dw_weight.shape[0] * dw_weight.shape[1]
    dw_rows = -(-tap_count // devices) * devices
    grad_dw = pl.pallas_call(
        conv_grad_kernel,
        out_shape=shape((dw_rows, channels), f32),
        in_specs=[vmem()] * 6,
        out_specs=vmem(),
        scratch_shapes=[pltpu.VMEM((rows + 2 * MARGIN, cols + 2 * PAD, channels), f32)],
        compiler_params=params(),
        cost_estimate=cost(9),
        name="conv_grad",
    )(state, south, north, left, right, after(grad_conv, send))

    size = half_rows // 4
    got = after(got, grad_dw)
    slices = [(keep[k], got[k * size : (k + 1) * size]) for k in range(4)]
    add = lambda summands: functools.reduce(lambda x, y: x + y.astype(f32), summands)
    sends = [add(slices[1]).astype(bf16), add(slices[3]).astype(bf16)]
    first_sends = sends
    held = [list(slices[0]), list(slices[2])]
    for stage in range(len(rest)):
        arrived = [swap_bit(sends[q], orders[q][stage]) for q in range(2)]
        arrived = lax.optimization_barrier(tuple(arrived))
        for q in range(2):
            held[q].append(arrived[q])
        if stage + 1 < len(rest):
            size //= 2
            sends = [add([h[size : 2 * size] for h in held[q]]).astype(bf16) for q in range(2)]
            held = [[h[:size] for h in held[q]] for q in range(2)]
    def for_band(distance):
        at = slice(distance * width, (distance + 1) * width)
        return jnp.concatenate([add([h[at] for h in held[q]]) for q in range(2)], axis=0)

    forcing_grad = for_band(0)
    from_bands = []
    for distance in range(1, lat_count):
        pairs = [(i, i ^ distance) for i in range(lat_count)]
        from_bands.append(lax.ppermute(for_band(distance).astype(bf16), "lat", pairs))

    total = jnp.concatenate([grads.reshape(2 * hid, channels), grad_dw], axis=0).astype(bf16)
    total = after(total, *first_sends)
    total = total.reshape(lon_count, -1, channels)
    exchange = functools.partial(lax.all_to_all, split_axis=0, concat_axis=0, tiled=True)
    spread = lambda x, count: jnp.broadcast_to(x, (count,) + x.shape)
    total = jnp.sum(exchange(total, "lon").astype(f32), axis=0).astype(bf16)
    total = jnp.sum(exchange(spread(total, lat_count), "lat").astype(f32), axis=0).astype(bf16)
    total = exchange(spread(total, lon_count), "lon")
    scale = float(cells * devices) ** (-0.5)
    total = total.reshape(-1, channels).astype(f32) * scale
    grad_up = total[:hid].reshape(hid // channels, channels, channels)
    grad_up = grad_up.transpose(1, 0, 2).reshape(channels, hid)
    grad_down = total[hid : 2 * hid]
    grad_dw = total[2 * hid : 2 * hid + tap_count].reshape(dw_weight.shape)
    arrived, grad_dw, grad_up, grad_down = lax.optimization_barrier(
        (from_bands, grad_dw, grad_up, grad_down)
    )
    forcing_grad = add([forcing_grad] + list(arrived))
    return (result, grad_dw, grad_up, grad_down, forcing_grad)


def solution(mesh):
    grid = P("lat", "lon", None)
    in_specs = (grid, grid, grid, P("lat", "lon")) + (P(),) * 9
    in_specs += (P(("lat", "lon"), None), P(("lat", "lon")), P(("lat", "lon")), P())
    out_specs = (grid, P(), P(), P(), P(("lat", "lon"), None))
    return jax.shard_map(
        on_device, mesh=mesh, in_specs=in_specs, out_specs=out_specs, check_vma=False
    )
```

```python
import functools

import jax
import jax.numpy as jnp
from jax import lax
from jax.experimental import pallas as pl
from jax.experimental.pallas import tpu as pltpu
from jax.sharding import PartitionSpec as P

A_DEV = 512
PAD = 8
TAPS = 7
MARGIN = 3
BATCH = 16
BATCHES = 2
SMALL = 8
GROUP = 1
gelu_scale = 0.7978845608028654
cubic_coef = 0.044715
f32 = jnp.float32
bf16 = jnp.bfloat16
shape = jax.ShapeDtypeStruct


def params(mebibytes=40):
    return pltpu.CompilerParams(vmem_limit_bytes=mebibytes << 20)


def cost(microseconds):
    return pl.CostEstimate(flops=int(microseconds * 1e9), bytes_accessed=0, transcendentals=0)


def vmem():
    return pl.BlockSpec(memory_space=pltpu.VMEM)


def anywhere():
    return pl.BlockSpec(memory_space=pl.ANY)


def smem():
    return pl.BlockSpec(memory_space=pltpu.SMEM)


def in_chunks(rows, body):
    chunk = 512

    def step_of(step, _):
        body(pl.ds(pl.multiple_of(step * chunk, chunk), chunk))
        return 0

    lax.fori_loop(0, rows // chunk, step_of, 0)


def conv_sums(field, base, dw, starts, lines, rows):
    sums = dict(zip(rows, starts))
    for b in range(TAPS):
        weights = [
            jnp.broadcast_to(dw[pl.ds(a * TAPS + b, 1), :], (8, dw.shape[1])) for a in range(TAPS)
        ]
        for h in lines:
            x = field(h, base + (PAD - MARGIN + b))
            for a in range(TAPS):
                if h - a in sums:
                    sums[h - a] = sums[h - a] + weights[a] * x
    return [sums[r] for r in rows]


def edge_kernel(state, even, odd, *, bands):
    rows, cols, channels = state.shape
    lat = lax.axis_index("lat")

    @pl.when(lat % 2 == 1)
    def _():
        even[...] = state[0:MARGIN]
        odd[...] = state[rows - MARGIN : rows]

    @pl.when(lat % 2 == 0)
    def _():
        even[...] = state[rows - MARGIN : rows]
        odd[...] = state[0:MARGIN]

    @pl.when(lat == bands - 1)
    def _():
        column = lax.broadcasted_iota(jnp.int32, (cols, cols), 1)
        line = lax.broadcasted_iota(jnp.int32, (cols, cols), 0)
        reverse = jnp.where(line + column == cols - 1, 1.0, 0.0).astype(bf16)
        for m in range(MARGIN):
            turned = jnp.dot(reverse, state[rows - 1 - m], preferred_element_type=f32)
            odd[m] = turned.astype(bf16)


def inner_conv_kernel(
    lat_count, lon_count, orders, state, dw, dwb, owner, cell, conv, targets, clash, padded
):
    rows, cols, channels = state.shape
    find_targets(lat_count, lon_count, orders, owner, cell, targets, clash)
    for r in range(rows):
        padded[r, PAD : PAD + cols, :] = state[r].astype(f32)

    def step_of(step, _):
        base = pl.multiple_of(step * 8, 8)
        field = lambda h, at: padded[h - MARGIN, pl.ds(at, 8), :]
        bias = jnp.broadcast_to(dwb[...], (8, channels))
        lines = range(MARGIN, rows + MARGIN)
        sums = conv_sums(field, base, dw, [bias] * rows, lines, list(range(rows)))
        for r in range(rows):
            conv[r, pl.ds(base, 8), :] = sums[r]
        return 0

    lax.fori_loop(1, cols // 8 - 1, step_of, 0)


def halo_conv_kernel(south, north, dw, conv, padded, *, rows):
    _, cols, channels = south.shape
    padded[0:MARGIN, PAD : PAD + cols, :] = south[...].astype(f32)
    padded[MARGIN : 2 * MARGIN, PAD : PAD + cols, :] = north[...].astype(f32)

    def step_of(step, _):
        base = pl.multiple_of(step * 8, 8)
        zero = jnp.zeros((8, channels), f32)
        for side in range(2):
            first = 0 if side == 0 else rows + MARGIN
            field = lambda h, at: padded[h - first + side * MARGIN, pl.ds(at, 8), :]
            out = [k if side == 0 else rows - MARGIN + k for k in range(MARGIN)]
            lines = range(first, first + MARGIN)
            sums = conv_sums(field, base, dw, [zero] * MARGIN, lines, out)
            for k in range(MARGIN):
                conv[side * MARGIN + k, pl.ds(base, 8), :] = sums[k]
        return 0

    lax.fori_loop(1, cols // 8 - 1, step_of, 0)


def fill_rows(padded, state, south, north):
    rows, cols, _ = state.shape
    inner = slice(PAD, PAD + cols)
    padded[0:MARGIN, inner, :] = south[...].astype(f32)
    padded[rows + MARGIN : rows + 2 * MARGIN, inner, :] = north[...].astype(f32)
    for r in range(rows):
        padded[r + MARGIN, inner, :] = state[r].astype(f32)


def block_kernel(
    state, south, north, left, right, conv, halo, forcing, cotangent, land, weight_index, weight_table,
    target_list, clash_list, dw, dwb, gain, nbias, up, upb, down, downb, scale, up_t, down_t,
    result, keep_0, keep_1, keep_2, keep_3, send, grad_conv, grads,
    field, edge, acc_up, acc_down, entry_weights, spread, terms, table, targets, clash, sems,
):
    rows, cols, channels = state.shape
    scalar_copies = [
        pltpu.make_async_copy(target_list, targets, sems.at[0]),
        pltpu.make_async_copy(clash_list, clash, sems.at[1]),
    ]
    for copy in scalar_copies:
        copy.start()
    wide = 16
    for side in range(2):
        own = slice(0, wide) if side == 0 else slice(cols - wide, cols)
        at = PAD if side == 0 else 0
        edge[side, 0:MARGIN, at : at + wide, :] = south[:, own, :].astype(f32)
        edge[side, rows + MARGIN : rows + 2 * MARGIN, at : at + wide, :] = north[:, own, :].astype(f32)
        for r in range(rows):
            edge[side, r + MARGIN, at : at + wide, :] = state[r, own, :].astype(f32)
        for h in range(rows + 2 * MARGIN):
            if side == 0:
                edge[side, h, PAD - MARGIN : PAD, :] = left[h].astype(f32)
            else:
                edge[side, h, wide : wide + MARGIN, :] = right[h].astype(f32)
        bias = jnp.broadcast_to(dwb[...], (8, channels))
        lines = range(rows + 2 * MARGIN)
        at_edge = lambda h, at: edge[side, h, pl.ds(at, 8), :]
        sums = conv_sums(at_edge, 0, dw, [bias] * rows, lines, list(range(rows)))
        out = slice(0, 8) if side == 0 else slice(cols - 8, cols)
        for r in range(rows):
            field[r, out, :] = sums[r]
    inner = slice(8, cols - 8)
    for r in range(rows):
        here = conv[r, inner, :]
        if r < MARGIN:
            here = here + halo[r, inner, :]
        if r >= rows - MARGIN:
            here = here + halo[r - rows + 2 * MARGIN, inner, :]
        field[r, inner, :] = here

    def clear(at):
        table[at, :] = jnp.zeros((at.size, channels), f32)

    in_chunks(table.shape[0], clear)
    index = weight_index[...]
    looked_up = jnp.zeros(index.shape, f32)
    for k in range(weight_table.shape[0]):
        looked_up = jnp.where(index == k, weight_table[k], looked_up)
    entry_weights[...] = looked_up
    acc_up[...] = jnp.zeros_like(acc_up)
    acc_down[...] = jnp.zeros_like(acc_down)
    group = GROUP
    size = group * cols
    fan = terms.shape[0] // size
    lines = fan * size // channels

    def column(ref, first, count):
        width = ref.shape[1]
        return jnp.concatenate(
            [
                jnp.broadcast_to(ref[pl.ds(first + k, 1), :].astype(f32), (channels, width)).T
                for k in range(count)
            ],
            axis=0,
        )

    def mlp_step(step, _):
        first = step * group
        here = field[pl.ds(first, group)].reshape(size, channels)
        average = jnp.mean(here, axis=-1, keepdims=True)
        centred = here - average
        variance = jnp.mean(centred * centred, axis=-1, keepdims=True)
        inv_std = lax.rsqrt(variance + 1e-06)
        normed = centred * inv_std
        force = forcing[pl.ds(first, group)].reshape(size, channels).astype(f32)
        mixed = (normed * gain[...] + nbias[...] + force).astype(bf16)
        pre = jnp.dot(mixed, up[...], preferred_element_type=f32) + upb[...]
        square = pre * pre
        tanh_value = jnp.tanh(pre * (gelu_scale + gelu_scale * cubic_coef * square))
        half = 0.5 + 0.5 * tanh_value
        hidden = (pre * half).astype(bf16)
        slope = half + pre * (1.0 - tanh_value * tanh_value) * (
            0.5 * gelu_scale + 1.5 * gelu_scale * cubic_coef * square
        )
        projected = jnp.dot(hidden, down[...], preferred_element_type=f32) + downb[...]
        ocean = column(land, first, group)
        own = state[pl.ds(first, group)].reshape(size, channels).astype(f32)
        out = ocean * (own + scale[...] * projected)
        result[pl.ds(first, group)] = out.astype(bf16).reshape(group, cols, channels)
        cot = cotangent[pl.ds(first, group)].reshape(size, channels).astype(f32)
        grad_out = (ocean * scale[...] * cot).astype(bf16)
        grad_hidden = jnp.dot(grad_out, down_t[...], preferred_element_type=f32)
        grad_pre = (grad_hidden * slope).astype(bf16)
        gmix = jnp.dot(grad_pre, up_t[...], preferred_element_type=f32)
        spread[...] = column(entry_weights, step * lines, lines)
        for k in range(fan):
            weights = spread[pl.ds(k, size, stride=fan), :]
            terms[pl.ds(k * size, size), :] = weights * gmix
        gained = gmix * gain[...]
        gconv = inv_std * (
            gained
            - jnp.mean(gained, axis=-1, keepdims=True)
            - normed * jnp.mean(gained * normed, axis=-1, keepdims=True)
        )
        grad_conv[pl.ds(first, group)] = gconv.reshape(group, cols, channels)
        contract = (((0,), (0,)), ((), ()))
        acc_up[...] += lax.dot_general(mixed, grad_pre, contract, preferred_element_type=f32)
        acc_down[...] += lax.dot_general(grad_out, hidden, contract, preferred_element_type=f32)

        @pl.when(step == 0)
        def _():
            for copy in scalar_copies:
                copy.wait()

        unit = BATCH * BATCHES
        units = fan * size // unit

        def add_unit(index, _):
            first_cell = index * (unit // fan)
            first_entry = step * (fan * size) + index * unit

            def add_batch(first, count):
                found = []
                for k in range(first, first + count):
                    value = terms[pl.ds((k % fan) * size + first_cell + k // fan, 1), :]
                    found.append((targets[first_entry + k], value))
                sums = [table[pl.ds(t, 1), :] + v for t, v in found]
                for (t, _), value in zip(found, sums):
                    table[pl.ds(t, 1), :] = value

            clashing = clash[first_entry]
            for level, count in enumerate((BATCH, SMALL, 1)):

                @pl.when(clashing == level)
                def _():
                    for first in range(0, unit, count):
                        add_batch(first, count)

            return 0

        lax.fori_loop(0, units, add_unit, 0)
        return 0

    lax.fori_loop(0, rows // group, mlp_step, 0)
    half = table.shape[0] // 2

    keep_copies = [
        pltpu.make_async_copy(table.at[pl.ds(k * (half // 4), half // 4)], keep, sems.at[2 + k])
        for k, keep in enumerate((keep_0, keep_1, keep_2, keep_3))
    ]
    for copy in keep_copies:
        copy.start()

    def give(at):
        send[at, :] = table[pl.ds(half + at.start, at.size), :].astype(bf16)

    in_chunks(half, give)
    blocks = up.shape[1] // channels
    for k in range(blocks):
        part = slice(k * channels, (k + 1) * channels)
        grads[k] = acc_up[:, part]
        grads[blocks + k] = acc_down[:, part].T
    for copy in keep_copies:
        copy.wait()


def find_targets(lat_count, lon_count, orders, owner, cell, targets, clash):
    lat, lon = lax.axis_index("lat"), lax.axis_index("lon")
    lon_bits = lon_count.bit_length() - 1
    half_rows = lat_count * lon_count // 2 * A_DEV
    width = A_DEV // 2
    device = owner[...]
    at_lat = (device >> lon_bits) ^ lat
    at_lon = (device & (lon_count - 1)) ^ lon
    numbers = []
    for order in orders:
        number = jnp.zeros_like(device)
        for bit in order:
            number = number * 2 + ((at_lon >> bit) & 1)
        numbers.append(number * lat_count + at_lat)
    upper = (cell[...] >= width).astype(jnp.int32)
    block = jnp.where(upper == 1, numbers[1], numbers[0])
    row = (at_lon & 1) * half_rows + upper * (half_rows // 2) + block * width
    row = row + cell[...] - upper * width
    targets[...] = row
    lane = lax.broadcasted_iota(jnp.int32, row.shape, 1)
    twice = jnp.zeros_like(row)
    for distance in range(BATCH - 1, 0, -1):
        same = row == pltpu.roll(row, distance, 1)
        twice = jnp.where(same & (lane % BATCH >= distance), jnp.maximum(twice, 1), twice)
        if distance < SMALL:
            twice = jnp.where(same & (lane % SMALL >= distance), 2, twice)
    distance = 1
    while distance < BATCH * BATCHES:
        twice = jnp.maximum(twice, pltpu.roll(twice, row.shape[1] - distance, 1))
        distance *= 2
    clash[...] = twice


def conv_grad_kernel(state, south, north, left, right, grad_conv, out, padded):
    rows, cols, channels = grad_conv.shape
    height = rows + 2 * MARGIN
    fill_rows(padded, state, south, north)
    for h in range(height):
        padded[h, PAD - MARGIN : PAD, :] = left[h].astype(f32)
        padded[h, PAD + cols : PAD + cols + MARGIN, :] = right[h].astype(f32)
    out[...] = jnp.zeros_like(out)
    unroll = 2
    for b in range(TAPS):

        def step_of(step, sums):
            sums = list(sums)
            for u in range(unroll):
                base = pl.multiple_of((step * unroll + u) * 8, 8)
                gc = [grad_conv[r, pl.ds(base, 8), :] for r in range(rows)]
                for h in range(height):
                    x = padded[h, pl.ds(base + (PAD - MARGIN + b), 8), :]
                    for a in range(TAPS):
                        if 0 <= h - a < rows:
                            k = a * 2 + (h - a) % 2
                            sums[k] = sums[k] + gc[h - a] * x
            return tuple(sums)

        zero = jnp.zeros((8, channels), f32)
        sums = lax.fori_loop(0, cols // (8 * unroll), step_of, (zero,) * (2 * TAPS))
        for a in range(TAPS):
            total = sums[2 * a] + sums[2 * a + 1]
            out[pl.ds(a * TAPS + b, 1), :] = jnp.sum(total, axis=0, keepdims=True)


def swap_bit(array, bit):
    pairs = [(i, i ^ (1 << bit)) for i in range(lax.axis_size("lon"))]
    return lax.ppermute(array, "lon", pairs)


def after(array, *others):
    return lax.optimization_barrier((array,) + others)[0]


def on_device(
    state, forcing, cotangent, land_mask, dw_weight, dw_bias, norm_gain, norm_bias,
    up_weight, up_bias, down_weight, down_bias, layer_scale, owner, atmos_cell, weight_index,
    intersection_weights,
):
    rows, cols, channels = state.shape
    cells = rows * cols
    hid = up_weight.shape[1]
    lat_count = lax.axis_size("lat")
    lon_count = lax.axis_size("lon")
    lat = lax.axis_index("lat")
    lon = lax.axis_index("lon")
    lon_bits = lon_count.bit_length() - 1
    devices = lat_count * lon_count
    entries = owner.shape[0]
    fan = entries // cells

    odd = lat % 2 == 1
    even_pairs, odd_pairs = [], []
    for l in range(lat_count):
        for j in range(lon_count):
            here = l * lon_count + j
            even_pairs.append((here, (l ^ 1) * lon_count + j))
            beyond = l + 1 if l % 2 else l - 1
            if 0 <= beyond < lat_count:
                odd_pairs.append((here, beyond * lon_count + j))
            else:
                odd_pairs.append((here, l * lon_count + lon_count - 1 - j))
    edge_rows = shape((MARGIN, cols, channels), bf16)
    for_even, for_odd = pl.pallas_call(
        functools.partial(edge_kernel, bands=lat_count),
        out_shape=(edge_rows, edge_rows),
        in_specs=[vmem()],
        out_specs=[vmem()] * 2,
        cost_estimate=cost(1),
        name="edges",
    )(state)
    got_even = lax.ppermute(for_even, ("lat", "lon"), even_pairs)
    got_odd = lax.ppermute(for_odd, ("lat", "lon"), odd_pairs)
    south = jnp.where(odd, got_even, jnp.where(lat == 0, jnp.zeros_like(got_odd), got_odd))
    north = jnp.where(odd, got_odd, got_even)

    forward = [(i, (i + 1) % lon_count) for i in range(lon_count)]
    backward = [(t, s) for s, t in forward]
    column = lambda part: jnp.concatenate([south[:, part], state[:, part], north[:, part]], axis=0)
    left = lax.ppermute(column(slice(cols - MARGIN, cols)), "lon", forward)
    right = lax.ppermute(column(slice(0, MARGIN)), "lon", backward)

    rest = list(range(1, lon_bits))
    orders = [rest, rest[::-1]]
    width = A_DEV // 2
    half_rows = devices // 2 * A_DEV
    lines = (entries // channels, channels)
    line = lambda v: v.reshape(1, -1)
    taps = dw_weight.reshape(-1, channels).astype(f32)
    conv, targets, clash = pl.pallas_call(
        functools.partial(inner_conv_kernel, lat_count, lon_count, orders),
        out_shape=(shape((rows, cols, channels), f32),) + (shape(lines, jnp.int32),) * 2,
        in_specs=[vmem()] * 5,
        out_specs=[vmem()] * 3,
        scratch_shapes=[pltpu.VMEM((rows, cols + 2 * PAD, channels), f32)],
        compiler_params=params(),
        cost_estimate=cost(7),
        name="inner_conv",
    )(
        after(state, for_even), taps, line(dw_bias), owner.reshape(lines), atmos_cell.reshape(lines)
    )
    halo = pl.pallas_call(
        functools.partial(halo_conv_kernel, rows=rows),
        out_shape=shape((2 * MARGIN, cols, channels), f32),
        in_specs=[vmem()] * 3,
        out_specs=vmem(),
        scratch_shapes=[pltpu.VMEM((2 * MARGIN, cols + 2 * PAD, channels), f32)],
        compiler_params=params(),
        cost_estimate=cost(2),
        name="halo_conv",
    )(south, north, taps)
    quarter = shape((half_rows // 4, channels), f32)
    result, *keep, send, grad_conv, grads = pl.pallas_call(
        block_kernel,
        out_shape=(
            shape((rows, cols, channels), bf16),
            *(quarter,) * 4,
            shape((half_rows, channels), bf16),
            shape((rows, cols, channels), f32),
            shape((2 * hid // channels, channels, channels), f32),
        ),
        in_specs=[vmem()] * 11 + [smem()] + [anywhere()] * 2 + [vmem()] * 11,
        out_specs=[vmem()] + [anywhere()] * 4 + [vmem()] * 3,
        scratch_shapes=[
            pltpu.VMEM((rows, cols, channels), f32),
            pltpu.VMEM((2, rows + 2 * MARGIN, 24, channels), f32),
            pltpu.VMEM((channels, hid), f32),
            pltpu.VMEM((channels, hid), f32),
            pltpu.VMEM((entries // channels, channels), f32),
            pltpu.VMEM((GROUP * fan * cols, channels), f32),
            pltpu.VMEM((GROUP * fan * cols, channels), f32),
            pltpu.VMEM((2 * half_rows, channels), f32),
            pltpu.SMEM((entries,), jnp.int32),
            pltpu.SMEM((entries,), jnp.int32),
            pltpu.SemaphoreType.DMA((6,)),
        ],
        compiler_params=params(min(60, 28 + (half_rows * channels * 10 >> 20))),
        cost_estimate=cost(28),
        name="block",
    )(
        state, south, north, left, right, conv, halo, forcing, cotangent, land_mask,
        weight_index.reshape(-1, channels), intersection_weights,
        targets.reshape(-1), clash.reshape(-1), taps, line(dw_bias), line(norm_gain), line(norm_bias), up_weight, line(up_bias),
        down_weight, line(down_bias), line(layer_scale), up_weight.T, down_weight.T,
    )

    got = swap_bit(send, 0)

    tap_count = dw_weight.shape[0] * dw_weight.shape[1]
    dw_rows = -(-tap_count // devices) * devices
    grad_dw = pl.pallas_call(
        conv_grad_kernel,
        out_shape=shape((dw_rows, channels), f32),
        in_specs=[vmem()] * 6,
        out_specs=vmem(),
        scratch_shapes=[pltpu.VMEM((rows + 2 * MARGIN, cols + 2 * PAD, channels), f32)],
        compiler_params=params(),
        cost_estimate=cost(9),
        name="conv_grad",
    )(state, south, north, left, right, after(grad_conv, send))

    size = half_rows // 4
    got = after(got, grad_dw)
    slices = [(keep[k], got[k * size : (k + 1) * size]) for k in range(4)]
    add = lambda summands: functools.reduce(lambda x, y: x + y.astype(f32), summands)
    exchange = functools.partial(lax.all_to_all, split_axis=0, concat_axis=0, tiled=True)
    spread = lambda x, count: jnp.broadcast_to(x, (count,) + x.shape)
    total = jnp.concatenate([grads.reshape(2 * hid, channels), grad_dw], axis=0).astype(bf16)
    sum_first = lambda x: jnp.sum(x.astype(f32), axis=0).astype(bf16)
    side_steps = [
        lambda x: sum_first(exchange(x.reshape(lon_count, -1, channels), "lon")),
        lambda x: sum_first(exchange(spread(x, lat_count), "lat")),
    ]
    sends = [add(slices[1]).astype(bf16), add(slices[3]).astype(bf16)]
    held = [list(slices[0]), list(slices[2])]
    for stage in range(len(rest)):
        arrived = [swap_bit(sends[q], orders[q][stage]) for q in range(2)]
        if stage < len(side_steps):
            total = side_steps[stage](after(total, *sends))
        *arrived, total = lax.optimization_barrier((*arrived, total))
        for q in range(2):
            held[q].append(arrived[q])
        if stage + 1 < len(rest):
            size //= 2
            sends = [add([h[size : 2 * size] for h in held[q]]).astype(bf16) for q in range(2)]
            held = [[h[:size] for h in held[q]] for q in range(2)]
    for step in side_steps[len(rest) :]:
        total = step(total)

    def for_band(distance):
        at = slice(distance * width, (distance + 1) * width)
        return jnp.concatenate([add([h[at] for h in held[q]]) for q in range(2)], axis=0)

    forcing_grad = for_band(0)
    sends = [for_band(distance).astype(bf16) for distance in range(1, lat_count)]
    from_bands = [
        lax.ppermute(sends[distance - 1], "lat", [(i, i ^ distance) for i in range(lat_count)])
        for distance in range(1, lat_count)
    ]
    total = exchange(spread(after(total, *sends), lon_count), "lon")
    scale = float(cells * devices) ** (-0.5)
    total = total.reshape(-1, channels).astype(f32) * scale
    grad_up = total[:hid].reshape(hid // channels, channels, channels)
    grad_up = grad_up.transpose(1, 0, 2).reshape(channels, hid)
    grad_down = total[hid : 2 * hid]
    grad_dw = total[2 * hid : 2 * hid + tap_count].reshape(dw_weight.shape)
    arrived, grad_dw, grad_up, grad_down = lax.optimization_barrier(
        (from_bands, grad_dw, grad_up, grad_down)
    )
    forcing_grad = add([forcing_grad] + list(arrived))
    return (result, grad_dw, grad_up, grad_down, forcing_grad)


def solution(mesh):
    grid = P("lat", "lon", None)
    in_specs = (grid, grid, grid, P("lat", "lon")) + (P(),) * 9
    in_specs += (P(("lat", "lon"), None), P(("lat", "lon")), P(("lat", "lon")), P())
    out_specs = (grid, P(), P(), P(), P(("lat", "lon"), None))
    return jax.shard_map(
        on_device, mesh=mesh, in_specs=in_specs, out_specs=out_specs, check_vma=False
    )
```

```python
import functools

import jax
import jax.numpy as jnp
from jax import lax
from jax.experimental import pallas as pl
from jax.experimental.pallas import tpu as pltpu
from jax.sharding import PartitionSpec as P

A_DEV = 512
WIDTHS = (192, 192, 128)
PAD = 8
TAPS = 7
MARGIN = 3
BATCH = 16
BATCHES = 2
SMALL = 8
GROUP = 2
gelu_scale = 0.7978845608028654
cubic_coef = 0.044715
f32 = jnp.float32
bf16 = jnp.bfloat16
shape = jax.ShapeDtypeStruct


def params(mebibytes=40):
    return pltpu.CompilerParams(vmem_limit_bytes=mebibytes << 20)


def cost(microseconds):
    return pl.CostEstimate(flops=int(microseconds * 1e9), bytes_accessed=0, transcendentals=0)


def vmem():
    return pl.BlockSpec(memory_space=pltpu.VMEM)


def anywhere():
    return pl.BlockSpec(memory_space=pl.ANY)


def smem():
    return pl.BlockSpec(memory_space=pltpu.SMEM)


def in_chunks(rows, body):
    chunk = 512

    def step_of(step, _):
        body(pl.ds(pl.multiple_of(step * chunk, chunk), chunk))
        return 0

    lax.fori_loop(0, rows // chunk, step_of, 0)


def conv_sums(field, base, dw, starts, lines, rows):
    sums = dict(zip(rows, starts))
    for b in range(TAPS):
        weights = [
            jnp.broadcast_to(dw[pl.ds(a * TAPS + b, 1), :], (8, dw.shape[1])) for a in range(TAPS)
        ]
        for h in lines:
            x = field(h, base + (PAD - MARGIN + b))
            for a in range(TAPS):
                if h - a in sums:
                    sums[h - a] = sums[h - a] + weights[a] * x
    return [sums[r] for r in rows]


def edge_kernel(state, even, odd, *, bands):
    rows, cols, channels = state.shape
    lat = lax.axis_index("lat")

    @pl.when(lat % 2 == 1)
    def _():
        even[...] = state[0:MARGIN]
        odd[...] = state[rows - MARGIN : rows]

    @pl.when(lat % 2 == 0)
    def _():
        even[...] = state[rows - MARGIN : rows]
        odd[...] = state[0:MARGIN]

    @pl.when(lat == bands - 1)
    def _():
        column = lax.broadcasted_iota(jnp.int32, (cols, cols), 1)
        line = lax.broadcasted_iota(jnp.int32, (cols, cols), 0)
        reverse = jnp.where(line + column == cols - 1, 1.0, 0.0).astype(bf16)
        for m in range(MARGIN):
            turned = jnp.dot(reverse, state[rows - 1 - m], preferred_element_type=f32)
            odd[m] = turned.astype(bf16)


def inner_conv_kernel(
    lat_count, lon_count, orders, state, dw, dwb, owner, cell, conv, targets, clash, padded
):
    rows, cols, channels = state.shape
    find_targets(lat_count, lon_count, orders, owner, cell, targets, clash)
    for r in range(rows):
        padded[r, PAD : PAD + cols, :] = state[r].astype(f32)

    def step_of(step, _):
        base = pl.multiple_of(step * 8, 8)
        field = lambda h, at: padded[h - MARGIN, pl.ds(at, 8), :]
        bias = jnp.broadcast_to(dwb[...], (8, channels))
        lines = range(MARGIN, rows + MARGIN)
        sums = conv_sums(field, base, dw, [bias] * rows, lines, list(range(rows)))
        for r in range(rows):
            conv[r, pl.ds(base, 8), :] = sums[r]
        return 0

    lax.fori_loop(1, cols // 8 - 1, step_of, 0)


def halo_conv_kernel(south, north, dw, conv, padded, *, rows):
    _, cols, channels = south.shape
    padded[0:MARGIN, PAD : PAD + cols, :] = south[...].astype(f32)
    padded[MARGIN : 2 * MARGIN, PAD : PAD + cols, :] = north[...].astype(f32)

    def step_of(step, _):
        base = pl.multiple_of(step * 8, 8)
        zero = jnp.zeros((8, channels), f32)
        for side in range(2):
            first = 0 if side == 0 else rows + MARGIN
            field = lambda h, at: padded[h - first + side * MARGIN, pl.ds(at, 8), :]
            out = [k if side == 0 else rows - MARGIN + k for k in range(MARGIN)]
            lines = range(first, first + MARGIN)
            sums = conv_sums(field, base, dw, [zero] * MARGIN, lines, out)
            for k in range(MARGIN):
                conv[side * MARGIN + k, pl.ds(base, 8), :] = sums[k]
        return 0

    lax.fori_loop(1, cols // 8 - 1, step_of, 0)


def fill_rows(padded, state, south, north):
    rows, cols, _ = state.shape
    inner = slice(PAD, PAD + cols)
    padded[0:MARGIN, inner, :] = south[...].astype(f32)
    padded[rows + MARGIN : rows + 2 * MARGIN, inner, :] = north[...].astype(f32)
    for r in range(rows):
        padded[r + MARGIN, inner, :] = state[r].astype(f32)


def block_kernel(
    state, south, north, left, right, conv, halo, forcing, cotangent, land, weight_index, weight_table,
    target_list, clash_list, dw, dwb, gain, nbias, up, upb, down, downb, scale, up_t, down_t,
    result, keep_0, keep_1, keep_2, keep_3, keep_4, send, grad_conv, grads,
    field, edge, acc_up, acc_down, entry_weights, spread, terms, table, targets, clash, sems,
):
    rows, cols, channels = state.shape
    scalar_copies = [
        pltpu.make_async_copy(target_list, targets, sems.at[0]),
        pltpu.make_async_copy(clash_list, clash, sems.at[1]),
    ]
    for copy in scalar_copies:
        copy.start()
    wide = 16
    for side in range(2):
        own = slice(0, wide) if side == 0 else slice(cols - wide, cols)
        at = PAD if side == 0 else 0
        edge[side, 0:MARGIN, at : at + wide, :] = south[:, own, :].astype(f32)
        edge[side, rows + MARGIN : rows + 2 * MARGIN, at : at + wide, :] = north[:, own, :].astype(f32)
        for r in range(rows):
            edge[side, r + MARGIN, at : at + wide, :] = state[r, own, :].astype(f32)
        for h in range(rows + 2 * MARGIN):
            if side == 0:
                edge[side, h, PAD - MARGIN : PAD, :] = left[h].astype(f32)
            else:
                edge[side, h, wide : wide + MARGIN, :] = right[h].astype(f32)
        bias = jnp.broadcast_to(dwb[...], (8, channels))
        lines = range(rows + 2 * MARGIN)
        at_edge = lambda h, at: edge[side, h, pl.ds(at, 8), :]
        sums = conv_sums(at_edge, 0, dw, [bias] * rows, lines, list(range(rows)))
        out = slice(0, 8) if side == 0 else slice(cols - 8, cols)
        for r in range(rows):
            field[r, out, :] = sums[r]
    inner = slice(8, cols - 8)
    for r in range(rows):
        here = conv[r, inner, :]
        if r < MARGIN:
            here = here + halo[r, inner, :]
        if r >= rows - MARGIN:
            here = here + halo[r - rows + 2 * MARGIN, inner, :]
        field[r, inner, :] = here

    def clear(at):
        table[at, :] = jnp.zeros((at.size, channels), f32)

    in_chunks(table.shape[0], clear)
    index = weight_index[...]
    looked_up = jnp.zeros(index.shape, f32)
    for k in range(weight_table.shape[0]):
        looked_up = jnp.where(index == k, weight_table[k], looked_up)
    entry_weights[...] = looked_up
    acc_up[...] = jnp.zeros_like(acc_up)
    acc_down[...] = jnp.zeros_like(acc_down)
    group = GROUP
    size = group * cols
    fan = terms.shape[0] // size
    lines = fan * size // channels

    def column(ref, first, count):
        width = ref.shape[1]
        return jnp.concatenate(
            [
                jnp.broadcast_to(ref[pl.ds(first + k, 1), :].astype(f32), (channels, width)).T
                for k in range(count)
            ],
            axis=0,
        )

    def mlp_step(step, _):
        first = step * group
        here = field[pl.ds(first, group)].reshape(size, channels)
        average = jnp.mean(here, axis=-1, keepdims=True)
        centred = here - average
        variance = jnp.mean(centred * centred, axis=-1, keepdims=True)
        inv_std = lax.rsqrt(variance + 1e-06)
        normed = centred * inv_std
        force = forcing[pl.ds(first, group)].reshape(size, channels).astype(f32)
        mixed = (normed * gain[...] + nbias[...] + force).astype(bf16)
        pre = jnp.dot(mixed, up[...], preferred_element_type=f32) + upb[...]
        square = pre * pre
        tanh_value = jnp.tanh(pre * (gelu_scale + gelu_scale * cubic_coef * square))
        half = 0.5 + 0.5 * tanh_value
        hidden = (pre * half).astype(bf16)
        slope = half + pre * (1.0 - tanh_value * tanh_value) * (
            0.5 * gelu_scale + 1.5 * gelu_scale * cubic_coef * square
        )
        projected = jnp.dot(hidden, down[...], preferred_element_type=f32) + downb[...]
        ocean = column(land, first, group)
        own = state[pl.ds(first, group)].reshape(size, channels).astype(f32)
        out = ocean * (own + scale[...] * projected)
        result[pl.ds(first, group)] = out.astype(bf16).reshape(group, cols, channels)
        cot = cotangent[pl.ds(first, group)].reshape(size, channels).astype(f32)
        grad_out = (ocean * scale[...] * cot).astype(bf16)
        grad_hidden = jnp.dot(grad_out, down_t[...], preferred_element_type=f32)
        grad_pre = (grad_hidden * slope).astype(bf16)
        gmix = jnp.dot(grad_pre, up_t[...], preferred_element_type=f32)
        spread[...] = column(entry_weights, step * lines, lines)
        for k in range(fan):
            weights = spread[pl.ds(k, size, stride=fan), :]
            terms[pl.ds(k * size, size), :] = weights * gmix
        gained = gmix * gain[...]
        gconv = inv_std * (
            gained
            - jnp.mean(gained, axis=-1, keepdims=True)
            - normed * jnp.mean(gained * normed, axis=-1, keepdims=True)
        )
        grad_conv[pl.ds(first, group)] = gconv.reshape(group, cols, channels)
        contract = (((0,), (0,)), ((), ()))
        acc_up[...] += lax.dot_general(mixed, grad_pre, contract, preferred_element_type=f32)
        acc_down[...] += lax.dot_general(grad_out, hidden, contract, preferred_element_type=f32)

        @pl.when(step == 0)
        def _():
            for copy in scalar_copies:
                copy.wait()

        unit = BATCH * BATCHES
        units = fan * size // unit

        def add_unit(index, _):
            first_cell = index * (unit // fan)
            first_entry = step * (fan * size) + index * unit

            def add_batch(first, count):
                found = []
                for k in range(first, first + count):
                    value = terms[pl.ds((k % fan) * size + first_cell + k // fan, 1), :]
                    found.append((targets[first_entry + k], value))
                sums = [table[pl.ds(t, 1), :] + v for t, v in found]
                for (t, _), value in zip(found, sums):
                    table[pl.ds(t, 1), :] = value

            clashing = clash[first_entry]
            for level, count in enumerate((BATCH, SMALL, 1)):

                @pl.when(clashing == level)
                def _():
                    for first in range(0, unit, count):
                        add_batch(first, count)

            return 0

        lax.fori_loop(0, units, add_unit, 0)
        return 0

    lax.fori_loop(0, rows // group, mlp_step, 0)
    half = table.shape[0] // 2

    keep_copies = []
    first = 0
    for k, keep in enumerate((keep_0, keep_1, keep_2, keep_3, keep_4)):
        from_rows = table.at[pl.ds(first, keep.shape[0])]
        keep_copies.append(pltpu.make_async_copy(from_rows, keep, sems.at[2 + k]))
        first += keep.shape[0]
    for copy in keep_copies:
        copy.start()

    def give(at):
        send[at, :] = table[pl.ds(half + at.start, at.size), :].astype(bf16)

    in_chunks(half, give)
    blocks = up.shape[1] // channels
    for k in range(blocks):
        part = slice(k * channels, (k + 1) * channels)
        grads[k] = acc_up[:, part]
        grads[blocks + k] = acc_down[:, part].T
    for copy in keep_copies:
        copy.wait()


def find_targets(lat_count, lon_count, orders, owner, cell, targets, clash):
    lat, lon = lax.axis_index("lat"), lax.axis_index("lon")
    lon_bits = lon_count.bit_length() - 1
    half_rows = lat_count * lon_count // 2 * A_DEV
    device = owner[...]
    at_lat = (device >> lon_bits) ^ lat
    at_lon = (device & (lon_count - 1)) ^ lon
    blocks = lat_count * lon_count // 2
    row = jnp.zeros_like(device)
    first = 0
    for part, (order, width) in enumerate(zip(orders, WIDTHS)):
        number = jnp.zeros_like(device)
        for bit in order:
            number = number * 2 + ((at_lon >> bit) & 1)
        if part < 2:
            number = number * lat_count + at_lat
        else:
            number = at_lat * (lon_count // 2) + number
        place = blocks * first + number * width + (cell[...] - first)
        row = jnp.where(cell[...] >= first, place, row)
        first += width
    row = row + (at_lon & 1) * half_rows
    targets[...] = row
    lane = lax.broadcasted_iota(jnp.int32, row.shape, 1)
    twice = jnp.zeros_like(row)
    for distance in range(BATCH - 1, 0, -1):
        same = row == pltpu.roll(row, distance, 1)
        twice = jnp.where(same & (lane % BATCH >= distance), jnp.maximum(twice, 1), twice)
        if distance < SMALL:
            twice = jnp.where(same & (lane % SMALL >= distance), 2, twice)
    distance = 1
    while distance < BATCH * BATCHES:
        twice = jnp.maximum(twice, pltpu.roll(twice, row.shape[1] - distance, 1))
        distance *= 2
    clash[...] = twice


def conv_grad_kernel(state, south, north, left, right, grad_conv, out, padded):
    rows, cols, channels = grad_conv.shape
    height = rows + 2 * MARGIN
    fill_rows(padded, state, south, north)
    for h in range(height):
        padded[h, PAD - MARGIN : PAD, :] = left[h].astype(f32)
        padded[h, PAD + cols : PAD + cols + MARGIN, :] = right[h].astype(f32)
    out[...] = jnp.zeros_like(out)
    unroll = 2
    for b in range(TAPS):

        def step_of(step, sums):
            sums = list(sums)
            for u in range(unroll):
                base = pl.multiple_of((step * unroll + u) * 8, 8)
                gc = [grad_conv[r, pl.ds(base, 8), :] for r in range(rows)]
                for h in range(height):
                    x = padded[h, pl.ds(base + (PAD - MARGIN + b), 8), :]
                    for a in range(TAPS):
                        if 0 <= h - a < rows:
                            k = a * 2 + (h - a) % 2
                            sums[k] = sums[k] + gc[h - a] * x
            return tuple(sums)

        zero = jnp.zeros((8, channels), f32)
        sums = lax.fori_loop(0, cols // (8 * unroll), step_of, (zero,) * (2 * TAPS))
        for a in range(TAPS):
            total = sums[2 * a] + sums[2 * a + 1]
            out[pl.ds(a * TAPS + b, 1), :] = jnp.sum(total, axis=0, keepdims=True)


def swap_bit(array, bit):
    pairs = [(i, i ^ (1 << bit)) for i in range(lax.axis_size("lon"))]
    return lax.ppermute(array, "lon", pairs)


def after(array, *others):
    return lax.optimization_barrier((array,) + others)[0]


def on_device(
    state, forcing, cotangent, land_mask, dw_weight, dw_bias, norm_gain, norm_bias,
    up_weight, up_bias, down_weight, down_bias, layer_scale, owner, atmos_cell, weight_index,
    intersection_weights,
):
    rows, cols, channels = state.shape
    cells = rows * cols
    hid = up_weight.shape[1]
    lat_count = lax.axis_size("lat")
    lon_count = lax.axis_size("lon")
    lat = lax.axis_index("lat")
    lon = lax.axis_index("lon")
    lon_bits = lon_count.bit_length() - 1
    devices = lat_count * lon_count
    entries = owner.shape[0]
    fan = entries // cells

    odd = lat % 2 == 1
    even_pairs, odd_pairs = [], []
    for l in range(lat_count):
        for j in range(lon_count):
            here = l * lon_count + j
            even_pairs.append((here, (l ^ 1) * lon_count + j))
            beyond = l + 1 if l % 2 else l - 1
            if 0 <= beyond < lat_count:
                odd_pairs.append((here, beyond * lon_count + j))
            else:
                odd_pairs.append((here, l * lon_count + lon_count - 1 - j))
    edge_rows = shape((MARGIN, cols, channels), bf16)
    for_even, for_odd = pl.pallas_call(
        functools.partial(edge_kernel, bands=lat_count),
        out_shape=(edge_rows, edge_rows),
        in_specs=[vmem()],
        out_specs=[vmem()] * 2,
        cost_estimate=cost(1),
        name="edges",
    )(state)
    got_even = lax.ppermute(for_even, ("lat", "lon"), even_pairs)
    got_odd = lax.ppermute(for_odd, ("lat", "lon"), odd_pairs)
    south = jnp.where(odd, got_even, jnp.where(lat == 0, jnp.zeros_like(got_odd), got_odd))
    north = jnp.where(odd, got_odd, got_even)

    forward = [(i, (i + 1) % lon_count) for i in range(lon_count)]
    backward = [(t, s) for s, t in forward]
    column = lambda part: jnp.concatenate([south[:, part], state[:, part], north[:, part]], axis=0)
    left = lax.ppermute(column(slice(cols - MARGIN, cols)), "lon", forward)
    right = lax.ppermute(column(slice(0, MARGIN)), "lon", backward)

    rest = list(range(1, lon_bits))
    orders = [rest, rest[::-1], rest]
    half_rows = devices // 2 * A_DEV
    lines = (entries // channels, channels)
    line = lambda v: v.reshape(1, -1)
    taps = dw_weight.reshape(-1, channels).astype(f32)
    conv, targets, clash = pl.pallas_call(
        functools.partial(inner_conv_kernel, lat_count, lon_count, orders),
        out_shape=(shape((rows, cols, channels), f32),) + (shape(lines, jnp.int32),) * 2,
        in_specs=[vmem()] * 5,
        out_specs=[vmem()] * 3,
        scratch_shapes=[pltpu.VMEM((rows, cols + 2 * PAD, channels), f32)],
        compiler_params=params(),
        cost_estimate=cost(7),
        name="inner_conv",
    )(
        after(state, for_even), taps, line(dw_bias), owner.reshape(lines), atmos_cell.reshape(lines)
    )
    halo = pl.pallas_call(
        functools.partial(halo_conv_kernel, rows=rows),
        out_shape=shape((2 * MARGIN, cols, channels), f32),
        in_specs=[vmem()] * 3,
        out_specs=vmem(),
        scratch_shapes=[pltpu.VMEM((2 * MARGIN, cols + 2 * PAD, channels), f32)],
        compiler_params=params(),
        cost_estimate=cost(2),
        name="halo_conv",
    )(south, north, taps)
    blocks = devices // 2
    sizes = [blocks * WIDTHS[0] // 2] * 2 + [blocks * WIDTHS[1] // 2] * 2 + [blocks * WIDTHS[2]]
    result, *keep, send, grad_conv, grads = pl.pallas_call(
        block_kernel,
        out_shape=(
            shape((rows, cols, channels), bf16),
            *(shape((size, channels), f32) for size in sizes),
            shape((half_rows, channels), bf16),
            shape((rows, cols, channels), f32),
            shape((2 * hid // channels, channels, channels), f32),
        ),
        in_specs=[vmem()] * 11 + [smem()] + [anywhere()] * 2 + [vmem()] * 11,
        out_specs=[vmem()] + [anywhere()] * 5 + [vmem()] * 3,
        scratch_shapes=[
            pltpu.VMEM((rows, cols, channels), f32),
            pltpu.VMEM((2, rows + 2 * MARGIN, 24, channels), f32),
            pltpu.VMEM((channels, hid), f32),
            pltpu.VMEM((channels, hid), f32),
            pltpu.VMEM((entries // channels, channels), f32),
            pltpu.VMEM((GROUP * fan * cols, channels), f32),
            pltpu.VMEM((GROUP * fan * cols, channels), f32),
            pltpu.VMEM((2 * half_rows, channels), f32),
            pltpu.SMEM((entries,), jnp.int32),
            pltpu.SMEM((entries,), jnp.int32),
            pltpu.SemaphoreType.DMA((7,)),
        ],
        compiler_params=params(min(60, 28 + (half_rows * channels * 10 >> 20))),
        cost_estimate=cost(28),
        name="block",
    )(
        state, south, north, left, right, conv, halo, forcing, cotangent, land_mask,
        weight_index.reshape(-1, channels), intersection_weights,
        targets.reshape(-1), clash.reshape(-1), taps, line(dw_bias), line(norm_gain), line(norm_bias), up_weight, line(up_bias),
        down_weight, line(down_bias), line(layer_scale), up_weight.T, down_weight.T,
    )

    got = swap_bit(send, 0)

    tap_count = dw_weight.shape[0] * dw_weight.shape[1]
    dw_rows = -(-tap_count // devices) * devices
    grad_dw = pl.pallas_call(
        conv_grad_kernel,
        out_shape=shape((dw_rows, channels), f32),
        in_specs=[vmem()] * 6,
        out_specs=vmem(),
        scratch_shapes=[pltpu.VMEM((rows + 2 * MARGIN, cols + 2 * PAD, channels), f32)],
        compiler_params=params(),
        cost_estimate=cost(9),
        name="conv_grad",
    )(state, south, north, left, right, after(grad_conv, send))

    got = after(got, grad_dw)
    add = lambda summands: functools.reduce(lambda x, y: x + y.astype(f32), summands)
    slices = []
    first = 0
    for held, size in zip(keep, sizes):
        slices.append((held, got[first : first + size]))
        first += size

    def to_bands(arrays):
        return [
            lax.ppermute(array, "lat", [(i, i ^ distance) for i in range(lat_count)])
            for distance, array in enumerate(arrays, 1)
        ]

    def band_part(held, width, distance):
        return add([h[distance * width : (distance + 1) * width] for h in held])

    sends = [add(slices[1]).astype(bf16), add(slices[3]).astype(bf16)]
    held = [list(slices[0]), list(slices[2])]
    z_rows = blocks // lat_count * WIDTHS[2]
    z_held = list(slices[4])
    z_sends = [band_part(z_held, z_rows, d).astype(bf16) for d in range(1, lat_count)]
    arrived = [swap_bit(sends[q], orders[q][0]) for q in range(2)]
    z_arrived = to_bands(lax.optimization_barrier((*z_sends, *sends))[: lat_count - 1])
    z_held = [h[:z_rows] for h in z_held] + z_arrived

    total = jnp.concatenate([grads.reshape(2 * hid, channels), grad_dw], axis=0).astype(bf16)
    exchange = functools.partial(
        lax.all_to_all, axis_name=("lat", "lon"), split_axis=0, concat_axis=0, tiled=True
    )
    total = exchange(after(total, *sends).reshape(devices, -1, channels))

    def z_plane_step(z_held, bit, sends):
        size = z_held[-1].shape[0] // 2
        out = add([h[size : 2 * size] for h in z_held]).astype(bf16)
        return [h[:size] for h in z_held] + [swap_bit(after(out, *sends), bit)]

    size = sizes[0]
    for stage in range(1, len(rest)):
        arrived = lax.optimization_barrier(tuple(arrived))
        size //= 2
        for q in range(2):
            held[q].append(arrived[q])
        sends = [add([h[size : 2 * size] for h in held[q]]).astype(bf16) for q in range(2)]
        held = [[h[:size] for h in held[q]] for q in range(2)]
        arrived = [swap_bit(sends[q], orders[q][stage]) for q in range(2)]
        if stage == 1:
            total = jnp.sum(after(total, *sends).astype(f32), axis=0, keepdims=True).astype(bf16)
            total = exchange(jnp.broadcast_to(total, (devices,) + total.shape[1:]))
        z_held = z_plane_step(z_held, rest[stage - 1], sends)
    arrived = lax.optimization_barrier(tuple(arrived))
    for q in range(2):
        held[q].append(arrived[q])
    sends = [
        jnp.concatenate([band_part(held[q], WIDTHS[q], d) for q in range(2)], axis=0).astype(bf16)
        for d in range(1, lat_count)
    ]
    from_bands = to_bands(sends)
    z_held = z_plane_step(z_held, rest[-1], sends)

    scale = float(cells * devices) ** (-0.5)
    total = total.reshape(-1, channels).astype(f32) * scale
    grad_up = total[:hid].reshape(hid // channels, channels, channels)
    grad_up = grad_up.transpose(1, 0, 2).reshape(channels, hid)
    grad_down = total[hid : 2 * hid]
    grad_dw = total[2 * hid : 2 * hid + tap_count].reshape(dw_weight.shape)
    from_bands, z_last, grad_dw, grad_up, grad_down = lax.optimization_barrier(
        (from_bands, z_held[-1], grad_dw, grad_up, grad_down)
    )
    from_plane = jnp.concatenate([band_part(held[q], WIDTHS[q], 0) for q in range(2)], axis=0)
    forcing_grad = jnp.concatenate(
        [add([from_plane] + list(from_bands)), add(z_held[:-1] + [z_last])], axis=0
    )
    return (result, grad_dw, grad_up, grad_down, forcing_grad)


def solution(mesh):
    grid = P("lat", "lon", None)
    in_specs = (grid, grid, grid, P("lat", "lon")) + (P(),) * 9
    in_specs += (P(("lat", "lon"), None), P(("lat", "lon")), P(("lat", "lon")), P())
    out_specs = (grid, P(), P(), P(), P(("lat", "lon"), None))
    return jax.shard_map(
        on_device, mesh=mesh, in_specs=in_specs, out_specs=out_specs, check_vma=False
    )
```

```python
import functools

import jax
import jax.numpy as jnp
from jax import lax
from jax.experimental import pallas as pl
from jax.experimental.pallas import tpu as pltpu
from jax.sharding import PartitionSpec as P

A_DEV = 512
PAD = 8
TAPS = 7
MARGIN = 3
BATCH = 16
BATCHES = 2
SMALL = 8
gelu_scale = 0.7978845608028654
cubic_coef = 0.044715
f32 = jnp.float32
bf16 = jnp.bfloat16
shape = jax.ShapeDtypeStruct


def params(mebibytes=40):
    return pltpu.CompilerParams(vmem_limit_bytes=mebibytes << 20)


def cost(microseconds):
    return pl.CostEstimate(flops=int(microseconds * 1e9), bytes_accessed=0, transcendentals=0)


def vmem():
    return pl.BlockSpec(memory_space=pltpu.VMEM)


def anywhere():
    return pl.BlockSpec(memory_space=pl.ANY)


def smem():
    return pl.BlockSpec(memory_space=pltpu.SMEM)


def in_chunks(rows, body):
    chunk = 512

    def step_of(step, _):
        body(pl.ds(pl.multiple_of(step * chunk, chunk), chunk))
        return 0

    lax.fori_loop(0, rows // chunk, step_of, 0)


def conv_sums(field, base, dw, starts, lines, rows):
    sums = dict(zip(rows, starts))
    for b in range(TAPS):
        weights = [
            jnp.broadcast_to(dw[pl.ds(a * TAPS + b, 1), :], (8, dw.shape[1])) for a in range(TAPS)
        ]
        for h in lines:
            x = field(h, base + (PAD - MARGIN + b))
            for a in range(TAPS):
                if h - a in sums:
                    sums[h - a] = sums[h - a] + weights[a] * x
    return [sums[r] for r in rows]


def edge_kernel(state, even, odd, *, bands):
    rows, cols, channels = state.shape
    lat = lax.axis_index("lat")

    @pl.when(lat % 2 == 1)
    def _():
        even[...] = state[0:MARGIN]
        odd[...] = state[rows - MARGIN : rows]

    @pl.when(lat % 2 == 0)
    def _():
        even[...] = state[rows - MARGIN : rows]
        odd[...] = state[0:MARGIN]

    @pl.when(lat == bands - 1)
    def _():
        column = lax.broadcasted_iota(jnp.int32, (cols, cols), 1)
        line = lax.broadcasted_iota(jnp.int32, (cols, cols), 0)
        reverse = jnp.where(line + column == cols - 1, 1.0, 0.0).astype(bf16)
        for m in range(MARGIN):
            turned = jnp.dot(reverse, state[rows - 1 - m], preferred_element_type=f32)
            odd[m] = turned.astype(bf16)


def inner_conv_kernel(
    lat_count, lon_count, orders, state, dw, dwb, owner, cell, conv, targets, clash, padded
):
    rows, cols, channels = state.shape
    find_targets(lat_count, lon_count, orders, owner, cell, targets, clash)
    for r in range(rows):
        padded[r, PAD : PAD + cols, :] = state[r].astype(f32)

    def step_of(step, _):
        base = pl.multiple_of(step * 8, 8)
        field = lambda h, at: padded[h - MARGIN, pl.ds(at, 8), :]
        bias = jnp.broadcast_to(dwb[...], (8, channels))
        lines = range(MARGIN, rows + MARGIN)
        sums = conv_sums(field, base, dw, [bias] * rows, lines, list(range(rows)))
        for r in range(rows):
            conv[r, pl.ds(base, 8), :] = sums[r]
        return 0

    lax.fori_loop(1, cols // 8 - 1, step_of, 0)


def halo_conv_kernel(south, north, dw, conv, padded, *, rows):
    _, cols, channels = south.shape
    padded[0:MARGIN, PAD : PAD + cols, :] = south[...].astype(f32)
    padded[MARGIN : 2 * MARGIN, PAD : PAD + cols, :] = north[...].astype(f32)

    def step_of(step, _):
        base = pl.multiple_of(step * 8, 8)
        zero = jnp.zeros((8, channels), f32)
        for side in range(2):
            first = 0 if side == 0 else rows + MARGIN
            field = lambda h, at: padded[h - first + side * MARGIN, pl.ds(at, 8), :]
            out = [k if side == 0 else rows - MARGIN + k for k in range(MARGIN)]
            lines = range(first, first + MARGIN)
            sums = conv_sums(field, base, dw, [zero] * MARGIN, lines, out)
            for k in range(MARGIN):
                conv[side * MARGIN + k, pl.ds(base, 8), :] = sums[k]
        return 0

    lax.fori_loop(1, cols // 8 - 1, step_of, 0)


def fill_rows(padded, state, south, north):
    rows, cols, _ = state.shape
    inner = slice(PAD, PAD + cols)
    padded[0:MARGIN, inner, :] = south[...].astype(f32)
    padded[rows + MARGIN : rows + 2 * MARGIN, inner, :] = north[...].astype(f32)
    for r in range(rows):
        padded[r + MARGIN, inner, :] = state[r].astype(f32)


def block_kernel(
    state, south, north, left, right, conv, halo, forcing, cotangent, land, weight_index, weight_table,
    target_list, clash_list, dw, dwb, gain, nbias, up, upb, down, downb, scale, up_t, down_t,
    result, keep_0, keep_1, keep_2, keep_3, send, grad_conv, grads,
    field, edge, acc_up, acc_down, entry_weights, spread, terms, table, targets, clash, sems,
):
    rows, cols, channels = state.shape
    scalar_copies = [
        pltpu.make_async_copy(target_list, targets, sems.at[0]),
        pltpu.make_async_copy(clash_list, clash, sems.at[1]),
    ]
    for copy in scalar_copies:
        copy.start()
    wide = 16
    for side in range(2):
        own = slice(0, wide) if side == 0 else slice(cols - wide, cols)
        at = PAD if side == 0 else 0
        edge[side, 0:MARGIN, at : at + wide, :] = south[:, own, :].astype(f32)
        edge[side, rows + MARGIN : rows + 2 * MARGIN, at : at + wide, :] = north[:, own, :].astype(f32)
        for r in range(rows):
            edge[side, r + MARGIN, at : at + wide, :] = state[r, own, :].astype(f32)
        for h in range(rows + 2 * MARGIN):
            if side == 0:
                edge[side, h, PAD - MARGIN : PAD, :] = left[h].astype(f32)
            else:
                edge[side, h, wide : wide + MARGIN, :] = right[h].astype(f32)
        bias = jnp.broadcast_to(dwb[...], (8, channels))
        lines = range(rows + 2 * MARGIN)
        at_edge = lambda h, at: edge[side, h, pl.ds(at, 8), :]
        sums = conv_sums(at_edge, 0, dw, [bias] * rows, lines, list(range(rows)))
        out = slice(0, 8) if side == 0 else slice(cols - 8, cols)
        for r in range(rows):
            field[r, out, :] = sums[r]
    inner = slice(8, cols - 8)
    for r in range(rows):
        here = conv[r, inner, :]
        if r < MARGIN:
            here = here + halo[r, inner, :]
        if r >= rows - MARGIN:
            here = here + halo[r - rows + 2 * MARGIN, inner, :]
        field[r, inner, :] = here

    def clear(at):
        table[at, :] = jnp.zeros((at.size, channels), f32)

    in_chunks(table.shape[0], clear)
    index = weight_index[...]
    looked_up = jnp.zeros(index.shape, f32)
    for k in range(weight_table.shape[0]):
        looked_up = jnp.where(index == k, weight_table[k], looked_up)
    entry_weights[...] = looked_up
    acc_up[...] = jnp.zeros_like(acc_up)
    acc_down[...] = jnp.zeros_like(acc_down)
    group = 2
    size = group * cols
    fan = terms.shape[0] // size
    lines = fan * size // channels

    def column(ref, first, count):
        width = ref.shape[1]
        return jnp.concatenate(
            [
                jnp.broadcast_to(ref[pl.ds(first + k, 1), :].astype(f32), (channels, width)).T
                for k in range(count)
            ],
            axis=0,
        )

    def mlp_step(step, _):
        first = step * group
        here = field[pl.ds(first, group)].reshape(size, channels)
        average = jnp.mean(here, axis=-1, keepdims=True)
        centred = here - average
        variance = jnp.mean(centred * centred, axis=-1, keepdims=True)
        inv_std = lax.rsqrt(variance + 1e-06)
        normed = centred * inv_std
        force = forcing[pl.ds(first, group)].reshape(size, channels).astype(f32)
        mixed = (normed * gain[...] + nbias[...] + force).astype(bf16)
        pre = jnp.dot(mixed, up[...], preferred_element_type=f32) + upb[...]
        square = pre * pre
        tanh_value = jnp.tanh(pre * (gelu_scale + gelu_scale * cubic_coef * square))
        half = 0.5 + 0.5 * tanh_value
        hidden = (pre * half).astype(bf16)
        slope = half + pre * (1.0 - tanh_value * tanh_value) * (
            0.5 * gelu_scale + 1.5 * gelu_scale * cubic_coef * square
        )
        projected = jnp.dot(hidden, down[...], preferred_element_type=f32) + downb[...]
        ocean = column(land, first, group)
        own = state[pl.ds(first, group)].reshape(size, channels).astype(f32)
        out = ocean * (own + scale[...] * projected)
        result[pl.ds(first, group)] = out.astype(bf16).reshape(group, cols, channels)
        cot = cotangent[pl.ds(first, group)].reshape(size, channels).astype(f32)
        grad_out = (ocean * scale[...] * cot).astype(bf16)
        grad_hidden = jnp.dot(grad_out, down_t[...], preferred_element_type=f32)
        grad_pre = (grad_hidden * slope).astype(bf16)
        gmix = jnp.dot(grad_pre, up_t[...], preferred_element_type=f32)
        spread[...] = column(entry_weights, step * lines, lines)
        for k in range(fan):
            weights = spread[pl.ds(k, size, stride=fan), :]
            terms[pl.ds(k * size, size), :] = weights * gmix
        gained = gmix * gain[...]
        gconv = inv_std * (
            gained
            - jnp.mean(gained, axis=-1, keepdims=True)
            - normed * jnp.mean(gained * normed, axis=-1, keepdims=True)
        )
        grad_conv[pl.ds(first, group)] = gconv.reshape(group, cols, channels)
        contract = (((0,), (0,)), ((), ()))
        acc_up[...] += lax.dot_general(mixed, grad_pre, contract, preferred_element_type=f32)
        acc_down[...] += lax.dot_general(grad_out, hidden, contract, preferred_element_type=f32)

        @pl.when(step == 0)
        def _():
            for copy in scalar_copies:
                copy.wait()

        unit = BATCH * BATCHES
        units = fan * size // unit

        def add_unit(index, _):
            first_cell = index * (unit // fan)
            first_entry = step * (fan * size) + index * unit

            def add_batch(first, count):
                found = []
                for k in range(first, first + count):
                    value = terms[pl.ds((k % fan) * size + first_cell + k // fan, 1), :]
                    found.append((targets[first_entry + k], value))
                sums = [table[pl.ds(t, 1), :] + v for t, v in found]
                for (t, _), value in zip(found, sums):
                    table[pl.ds(t, 1), :] = value

            clashing = clash[first_entry]
            for level, count in enumerate((BATCH, SMALL, 1)):

                @pl.when(clashing == level)
                def _():
                    for first in range(0, unit, count):
                        add_batch(first, count)

            return 0

        lax.fori_loop(0, units, add_unit, 0)
        return 0

    lax.fori_loop(0, rows // group, mlp_step, 0)
    half = table.shape[0] // 2

    keep_copies = [
        pltpu.make_async_copy(table.at[pl.ds(k * (half // 4), half // 4)], keep, sems.at[2 + k])
        for k, keep in enumerate((keep_0, keep_1, keep_2, keep_3))
    ]
    for copy in keep_copies:
        copy.start()

    def give(at):
        send[at, :] = table[pl.ds(half + at.start, at.size), :].astype(bf16)

    in_chunks(half, give)
    blocks = up.shape[1] // channels
    for k in range(blocks):
        part = slice(k * channels, (k + 1) * channels)
        grads[k] = acc_up[:, part]
        grads[blocks + k] = acc_down[:, part].T
    for copy in keep_copies:
        copy.wait()


def find_targets(lat_count, lon_count, orders, owner, cell, targets, clash):
    lat, lon = lax.axis_index("lat"), lax.axis_index("lon")
    lon_bits = lon_count.bit_length() - 1
    half_rows = lat_count * lon_count // 2 * A_DEV
    width = A_DEV // 2
    device = owner[...]
    at_lat = (device >> lon_bits) ^ lat
    at_lon = (device & (lon_count - 1)) ^ lon
    numbers = []
    for order in orders:
        number = jnp.zeros_like(device)
        for bit in order:
            number = number * 2 + ((at_lon >> bit) & 1)
        numbers.append(number * lat_count + at_lat)
    upper = (cell[...] >= width).astype(jnp.int32)
    block = jnp.where(upper == 1, numbers[1], numbers[0])
    row = (at_lon & 1) * half_rows + upper * (half_rows // 2) + block * width
    row = row + cell[...] - upper * width
    targets[...] = row
    lane = lax.broadcasted_iota(jnp.int32, row.shape, 1)
    twice = jnp.zeros_like(row)
    for distance in range(BATCH - 1, 0, -1):
        same = row == pltpu.roll(row, distance, 1)
        twice = jnp.where(same & (lane % BATCH >= distance), jnp.maximum(twice, 1), twice)
        if distance < SMALL:
            twice = jnp.where(same & (lane % SMALL >= distance), 2, twice)
    distance = 1
    while distance < BATCH * BATCHES:
        twice = jnp.maximum(twice, pltpu.roll(twice, row.shape[1] - distance, 1))
        distance *= 2
    clash[...] = twice


def conv_grad_kernel(state, south, north, left, right, grad_conv, out, padded):
    rows, cols, channels = grad_conv.shape
    height = rows + 2 * MARGIN
    fill_rows(padded, state, south, north)
    for h in range(height):
        padded[h, PAD - MARGIN : PAD, :] = left[h].astype(f32)
        padded[h, PAD + cols : PAD + cols + MARGIN, :] = right[h].astype(f32)
    out[...] = jnp.zeros_like(out)
    unroll = 2
    for b in range(TAPS):

        def step_of(step, sums):
            sums = list(sums)
            for u in range(unroll):
                base = pl.multiple_of((step * unroll + u) * 8, 8)
                gc = [grad_conv[r, pl.ds(base, 8), :] for r in range(rows)]
                for h in range(height):
                    x = padded[h, pl.ds(base + (PAD - MARGIN + b), 8), :]
                    for a in range(TAPS):
                        if 0 <= h - a < rows:
                            k = a * 2 + (h - a) % 2
                            sums[k] = sums[k] + gc[h - a] * x
            return tuple(sums)

        zero = jnp.zeros((8, channels), f32)
        sums = lax.fori_loop(0, cols // (8 * unroll), step_of, (zero,) * (2 * TAPS))
        for a in range(TAPS):
            total = sums[2 * a] + sums[2 * a + 1]
            out[pl.ds(a * TAPS + b, 1), :] = jnp.sum(total, axis=0, keepdims=True)


def swap_bit(array, bit):
    pairs = [(i, i ^ (1 << bit)) for i in range(lax.axis_size("lon"))]
    return lax.ppermute(array, "lon", pairs)


def after(array, *others):
    return lax.optimization_barrier((array,) + others)[0]


def on_device(
    state, forcing, cotangent, land_mask, dw_weight, dw_bias, norm_gain, norm_bias,
    up_weight, up_bias, down_weight, down_bias, layer_scale, owner, atmos_cell, weight_index,
    intersection_weights,
):
    rows, cols, channels = state.shape
    cells = rows * cols
    hid = up_weight.shape[1]
    lat_count = lax.axis_size("lat")
    lon_count = lax.axis_size("lon")
    lat = lax.axis_index("lat")
    lon = lax.axis_index("lon")
    lon_bits = lon_count.bit_length() - 1
    devices = lat_count * lon_count
    entries = owner.shape[0]
    fan = entries // cells

    odd = lat % 2 == 1
    even_pairs, odd_pairs = [], []
    for l in range(lat_count):
        for j in range(lon_count):
            here = l * lon_count + j
            even_pairs.append((here, (l ^ 1) * lon_count + j))
            beyond = l + 1 if l % 2 else l - 1
            if 0 <= beyond < lat_count:
                odd_pairs.append((here, beyond * lon_count + j))
            else:
                odd_pairs.append((here, l * lon_count + lon_count - 1 - j))
    edge_rows = shape((MARGIN, cols, channels), bf16)
    for_even, for_odd = pl.pallas_call(
        functools.partial(edge_kernel, bands=lat_count),
        out_shape=(edge_rows, edge_rows),
        in_specs=[vmem()],
        out_specs=[vmem()] * 2,
        cost_estimate=cost(1),
        name="edges",
    )(state)
    got_even = lax.ppermute(for_even, ("lat", "lon"), even_pairs)
    got_odd = lax.ppermute(for_odd, ("lat", "lon"), odd_pairs)
    south = jnp.where(odd, got_even, jnp.where(lat == 0, jnp.zeros_like(got_odd), got_odd))
    north = jnp.where(odd, got_odd, got_even)

    forward = [(i, (i + 1) % lon_count) for i in range(lon_count)]
    backward = [(t, s) for s, t in forward]
    column = lambda part: jnp.concatenate([south[:, part], state[:, part], north[:, part]], axis=0)
    left = lax.ppermute(column(slice(cols - MARGIN, cols)), "lon", forward)
    right = lax.ppermute(column(slice(0, MARGIN)), "lon", backward)

    rest = list(range(1, lon_bits))
    orders = [rest, rest[::-1]]
    width = A_DEV // 2
    half_rows = devices // 2 * A_DEV
    lines = (entries // channels, channels)
    line = lambda v: v.reshape(1, -1)
    taps = dw_weight.reshape(-1, channels).astype(f32)
    conv, targets, clash = pl.pallas_call(
        functools.partial(inner_conv_kernel, lat_count, lon_count, orders),
        out_shape=(shape((rows, cols, channels), f32),) + (shape(lines, jnp.int32),) * 2,
        in_specs=[vmem()] * 5,
        out_specs=[vmem()] * 3,
        scratch_shapes=[pltpu.VMEM((rows, cols + 2 * PAD, channels), f32)],
        compiler_params=params(),
        cost_estimate=cost(7),
        name="inner_conv",
    )(
        after(state, for_even), taps, line(dw_bias), owner.reshape(lines), atmos_cell.reshape(lines)
    )
    halo = pl.pallas_call(
        functools.partial(halo_conv_kernel, rows=rows),
        out_shape=shape((2 * MARGIN, cols, channels), f32),
        in_specs=[vmem()] * 3,
        out_specs=vmem(),
        scratch_shapes=[pltpu.VMEM((2 * MARGIN, cols + 2 * PAD, channels), f32)],
        compiler_params=params(),
        cost_estimate=cost(2),
        name="halo_conv",
    )(south, north, taps)
    quarter = shape((half_rows // 4, channels), f32)
    result, *keep, send, grad_conv, grads = pl.pallas_call(
        block_kernel,
        out_shape=(
            shape((rows, cols, channels), bf16),
            *(quarter,) * 4,
            shape((half_rows, channels), bf16),
            shape((rows, cols, channels), f32),
            shape((2 * hid // channels, channels, channels), f32),
        ),
        in_specs=[vmem()] * 11 + [smem()] + [anywhere()] * 2 + [vmem()] * 11,
        out_specs=[vmem()] + [anywhere()] * 4 + [vmem()] * 3,
        scratch_shapes=[
            pltpu.VMEM((rows, cols, channels), f32),
            pltpu.VMEM((2, rows + 2 * MARGIN, 24, channels), f32),
            pltpu.VMEM((channels, hid), f32),
            pltpu.VMEM((channels, hid), f32),
            pltpu.VMEM((entries // channels, channels), f32),
            pltpu.VMEM((2 * fan * cols, channels), f32),
            pltpu.VMEM((2 * fan * cols, channels), f32),
            pltpu.VMEM((2 * half_rows, channels), f32),
            pltpu.SMEM((entries,), jnp.int32),
            pltpu.SMEM((entries,), jnp.int32),
            pltpu.SemaphoreType.DMA((6,)),
        ],
        compiler_params=params(min(60, 28 + (half_rows * channels * 10 >> 20))),
        cost_estimate=cost(28),
        name="block",
    )(
        state, south, north, left, right, conv, halo, forcing, cotangent, land_mask,
        weight_index.reshape(-1, channels), intersection_weights,
        targets.reshape(-1), clash.reshape(-1), taps, line(dw_bias), line(norm_gain), line(norm_bias), up_weight, line(up_bias),
        down_weight, line(down_bias), line(layer_scale), up_weight.T, down_weight.T,
    )

    got = swap_bit(send, 0)

    tap_count = dw_weight.shape[0] * dw_weight.shape[1]
    dw_rows = -(-tap_count // devices) * devices
    grad_dw = pl.pallas_call(
        conv_grad_kernel,
        out_shape=shape((dw_rows, channels), f32),
        in_specs=[vmem()] * 6,
        out_specs=vmem(),
        scratch_shapes=[pltpu.VMEM((rows + 2 * MARGIN, cols + 2 * PAD, channels), f32)],
        compiler_params=params(),
        cost_estimate=cost(9),
        name="conv_grad",
    )(state, south, north, left, right, after(grad_conv, send))

    size = half_rows // 4
    got = after(got, grad_dw)
    slices = [(keep[k], got[k * size : (k + 1) * size]) for k in range(4)]
    add = lambda summands: functools.reduce(lambda x, y: x + y.astype(f32), summands)
    sends = [add(slices[1]).astype(bf16), add(slices[3]).astype(bf16)]
    first_sends = sends
    held = [list(slices[0]), list(slices[2])]
    for stage in range(len(rest)):
        arrived = [swap_bit(sends[q], orders[q][stage]) for q in range(2)]
        arrived = lax.optimization_barrier(tuple(arrived))
        for q in range(2):
            held[q].append(arrived[q])
        if stage + 1 < len(rest):
            size //= 2
            sends = [add([h[size : 2 * size] for h in held[q]]).astype(bf16) for q in range(2)]
            held = [[h[:size] for h in held[q]] for q in range(2)]
    def for_band(distance):
        at = slice(distance * width, (distance + 1) * width)
        return jnp.concatenate([add([h[at] for h in held[q]]) for q in range(2)], axis=0)

    forcing_grad = for_band(0)
    from_bands = []
    for distance in range(1, lat_count):
        pairs = [(i, i ^ distance) for i in range(lat_count)]
        from_bands.append(lax.ppermute(for_band(distance).astype(bf16), "lat", pairs))

    total = jnp.concatenate([grads.reshape(2 * hid, channels), grad_dw], axis=0).astype(bf16)
    total = after(total, *first_sends)
    total = total.reshape(devices, -1, channels)
    total = lax.all_to_all(total, ("lat", "lon"), split_axis=0, concat_axis=0, tiled=True)
    total = jnp.sum(total.astype(f32), axis=0, keepdims=True).astype(bf16)
    total = jnp.broadcast_to(total, (devices,) + total.shape[1:])
    total = lax.all_to_all(total, ("lat", "lon"), split_axis=0, concat_axis=0, tiled=True)
    scale = float(cells * devices) ** (-0.5)
    total = total.reshape(-1, channels).astype(f32) * scale
    grad_up = total[:hid].reshape(hid // channels, channels, channels)
    grad_up = grad_up.transpose(1, 0, 2).reshape(channels, hid)
    grad_down = total[hid : 2 * hid]
    grad_dw = total[2 * hid : 2 * hid + tap_count].reshape(dw_weight.shape)
    arrived, grad_dw, grad_up, grad_down = lax.optimization_barrier(
        (from_bands, grad_dw, grad_up, grad_down)
    )
    forcing_grad = add([forcing_grad] + list(arrived))
    return (result, grad_dw, grad_up, grad_down, forcing_grad)


def solution(mesh):
    grid = P("lat", "lon", None)
    in_specs = (grid, grid, grid, P("lat", "lon")) + (P(),) * 9
    in_specs += (P(("lat", "lon"), None), P(("lat", "lon")), P(("lat", "lon")), P())
    out_specs = (grid, P(), P(), P(), P(("lat", "lon"), None))
    return jax.shard_map(
        on_device, mesh=mesh, in_specs=in_specs, out_specs=out_specs, check_vma=False
    )
```

```python
import functools

import jax
import jax.numpy as jnp
from jax import lax
from jax.experimental import pallas as pl
from jax.experimental.pallas import tpu as pltpu
from jax.sharding import PartitionSpec as P

A_DEV = 512
PAD = 8
TAPS = 7
MARGIN = 3
BATCH = 16
BATCHES = 2
SMALL = 8
ROUND = 2
gelu_scale = 0.7978845608028654
cubic_coef = 0.044715
f32 = jnp.float32
bf16 = jnp.bfloat16
shape = jax.ShapeDtypeStruct


def params(mebibytes):
    return pltpu.CompilerParams(vmem_limit_bytes=mebibytes << 20)


def cost(microseconds):
    return pl.CostEstimate(flops=int(microseconds * 1e9), bytes_accessed=0, transcendentals=0)


def vmem():
    return pl.BlockSpec(memory_space=pltpu.VMEM)


def anywhere():
    return pl.BlockSpec(memory_space=pl.ANY)


def smem():
    return pl.BlockSpec(memory_space=pltpu.SMEM)


def in_chunks(rows, body):
    chunk = 512

    def step_of(step, _):
        body(pl.ds(pl.multiple_of(step * chunk, chunk), chunk))
        return 0

    lax.fori_loop(0, rows // chunk, step_of, 0)


def conv_sums(field, base, dw, starts, lines, rows):
    sums = dict(zip(rows, starts))
    for b in range(TAPS):
        weights = [
            jnp.broadcast_to(dw[pl.ds(a * TAPS + b, 1), :], (8, dw.shape[1])) for a in range(TAPS)
        ]
        for h in lines:
            x = field(h, base + (PAD - MARGIN + b))
            for a in range(TAPS):
                if h - a in sums:
                    sums[h - a] = sums[h - a] + weights[a] * x
    return [sums[r] for r in rows]


def edge_kernel(state, even, odd, *, bands):
    rows, cols, channels = state.shape
    lat = lax.axis_index("lat")

    @pl.when(lat % 2 == 1)
    def _():
        even[...] = state[0:MARGIN]
        odd[...] = state[rows - MARGIN : rows]

    @pl.when(lat % 2 == 0)
    def _():
        even[...] = state[rows - MARGIN : rows]
        odd[...] = state[0:MARGIN]

    @pl.when(lat == bands - 1)
    def _():
        column = lax.broadcasted_iota(jnp.int32, (cols, cols), 1)
        line = lax.broadcasted_iota(jnp.int32, (cols, cols), 0)
        reverse = jnp.where(line + column == cols - 1, 1.0, 0.0).astype(bf16)
        for m in range(MARGIN):
            turned = jnp.dot(reverse, state[rows - 1 - m], preferred_element_type=f32)
            odd[m] = turned.astype(bf16)


def inner_conv_kernel(
    lat_count, lon_count, orders, state, dw, dwb, owner, cell, conv, targets, clash, padded
):
    rows, cols, channels = state.shape
    find_targets(lat_count, lon_count, orders, owner, cell, targets, clash)
    for r in range(rows):
        padded[r, PAD : PAD + cols, :] = state[r].astype(f32)

    def step_of(step, _):
        base = pl.multiple_of(step * 8, 8)
        field = lambda h, at: padded[h - MARGIN, pl.ds(at, 8), :]
        bias = jnp.broadcast_to(dwb[...], (8, channels))
        lines = range(MARGIN, rows + MARGIN)
        sums = conv_sums(field, base, dw, [bias] * rows, lines, list(range(rows)))
        for r in range(rows):
            conv[r, pl.ds(base, 8), :] = sums[r]
        return 0

    lax.fori_loop(1, cols // 8 - 1, step_of, 0)


def halo_conv_kernel(south, north, dw, conv, padded, *, rows):
    _, cols, channels = south.shape
    padded[0:MARGIN, PAD : PAD + cols, :] = south[...].astype(f32)
    padded[MARGIN : 2 * MARGIN, PAD : PAD + cols, :] = north[...].astype(f32)

    def step_of(step, _):
        base = pl.multiple_of(step * 8, 8)
        zero = jnp.zeros((8, channels), f32)
        for side in range(2):
            first = 0 if side == 0 else rows + MARGIN
            field = lambda h, at: padded[h - first + side * MARGIN, pl.ds(at, 8), :]
            out = [k if side == 0 else rows - MARGIN + k for k in range(MARGIN)]
            lines = range(first, first + MARGIN)
            sums = conv_sums(field, base, dw, [zero] * MARGIN, lines, out)
            for k in range(MARGIN):
                conv[side * MARGIN + k, pl.ds(base, 8), :] = sums[k]
        return 0

    lax.fori_loop(1, cols // 8 - 1, step_of, 0)


def fill_rows(padded, state, south, north):
    rows, cols, _ = state.shape
    inner = slice(PAD, PAD + cols)
    padded[0:MARGIN, inner, :] = south[...].astype(f32)
    padded[rows + MARGIN : rows + 2 * MARGIN, inner, :] = north[...].astype(f32)
    for r in range(rows):
        padded[r + MARGIN, inner, :] = state[r].astype(f32)


def block_kernel(
    state, south, north, left, right, conv, halo, forcing, cotangent, land, weight_index, weight_table,
    target_list, clash_list, dw, dwb, gain, nbias, up, upb, down, downb, scale, up_t, down_t,
    result, keep_0, keep_1, keep_2, keep_3, send, grad_conv, grads,
    field, edge, acc_up, acc_down, entry_weights, spread, terms, table, outgoing, targets, clash, sems,
):
    rows, cols, channels = state.shape
    scalar_copies = [
        pltpu.make_async_copy(target_list, targets, sems.at[0]),
        pltpu.make_async_copy(clash_list, clash, sems.at[1]),
    ]
    for copy in scalar_copies:
        copy.start()
    wide = 16
    for side in range(2):
        own = slice(0, wide) if side == 0 else slice(cols - wide, cols)
        at = PAD if side == 0 else 0
        edge[side, 0:MARGIN, at : at + wide, :] = south[:, own, :].astype(f32)
        edge[side, rows + MARGIN : rows + 2 * MARGIN, at : at + wide, :] = north[:, own, :].astype(f32)
        for r in range(rows):
            edge[side, r + MARGIN, at : at + wide, :] = state[r, own, :].astype(f32)
        for h in range(rows + 2 * MARGIN):
            if side == 0:
                edge[side, h, PAD - MARGIN : PAD, :] = left[h].astype(f32)
            else:
                edge[side, h, wide : wide + MARGIN, :] = right[h].astype(f32)
        bias = jnp.broadcast_to(dwb[...], (8, channels))
        lines = range(rows + 2 * MARGIN)
        at_edge = lambda h, at: edge[side, h, pl.ds(at, 8), :]
        sums = conv_sums(at_edge, 0, dw, [bias] * rows, lines, list(range(rows)))
        out = slice(0, 8) if side == 0 else slice(cols - 8, cols)
        for r in range(rows):
            field[r, out, :] = sums[r]
    inner = slice(8, cols - 8)
    for r in range(rows):
        here = conv[r, inner, :]
        if r < MARGIN:
            here = here + halo[r, inner, :]
        if r >= rows - MARGIN:
            here = here + halo[r - rows + 2 * MARGIN, inner, :]
        field[r, inner, :] = here

    def clear(at):
        table[at, :] = jnp.zeros((at.size, channels), f32)

    in_chunks(table.shape[0], clear)
    index = weight_index[...]
    looked_up = jnp.zeros(index.shape, f32)
    for k in range(weight_table.shape[0]):
        looked_up = jnp.where(index == k, weight_table[k], looked_up)
    entry_weights[...] = looked_up
    acc_up[...] = jnp.zeros_like(acc_up)
    acc_down[...] = jnp.zeros_like(acc_down)
    group = 2
    size = group * cols
    fan = terms.shape[0] // (ROUND * size)
    lines = fan * size // channels

    def column(ref, first, count):
        width = ref.shape[1]
        return jnp.concatenate(
            [
                jnp.broadcast_to(ref[pl.ds(first + k, 1), :].astype(f32), (channels, width)).T
                for k in range(count)
            ],
            axis=0,
        )

    def mlp_step(step, place):
        first = step * group
        here = field[pl.ds(first, group)].reshape(size, channels)
        average = jnp.mean(here, axis=-1, keepdims=True)
        centred = here - average
        variance = jnp.mean(centred * centred, axis=-1, keepdims=True)
        inv_std = lax.rsqrt(variance + 1e-06)
        normed = centred * inv_std
        force = forcing[pl.ds(first, group)].reshape(size, channels).astype(f32)
        mixed = (normed * gain[...] + nbias[...] + force).astype(bf16)
        pre = jnp.dot(mixed, up[...], preferred_element_type=f32) + upb[...]
        square = pre * pre
        tanh_value = jnp.tanh(pre * (gelu_scale + gelu_scale * cubic_coef * square))
        half = 0.5 + 0.5 * tanh_value
        hidden = (pre * half).astype(bf16)
        slope = half + pre * (1.0 - tanh_value * tanh_value) * (
            0.5 * gelu_scale + 1.5 * gelu_scale * cubic_coef * square
        )
        projected = jnp.dot(hidden, down[...], preferred_element_type=f32) + downb[...]
        ocean = column(land, first, group)
        own = state[pl.ds(first, group)].reshape(size, channels).astype(f32)
        out = ocean * (own + scale[...] * projected)
        result[pl.ds(first, group)] = out.astype(bf16).reshape(group, cols, channels)
        cot = cotangent[pl.ds(first, group)].reshape(size, channels).astype(f32)
        grad_out = (ocean * scale[...] * cot).astype(bf16)
        grad_hidden = jnp.dot(grad_out, down_t[...], preferred_element_type=f32)
        grad_pre = (grad_hidden * slope).astype(bf16)
        gmix = jnp.dot(grad_pre, up_t[...], preferred_element_type=f32)
        spread[...] = column(entry_weights, step * lines, lines)
        for k in range(fan):
            weights = spread[pl.ds(k, size, stride=fan), :]
            terms[pl.ds(k * ROUND * size + place * size, size), :] = weights * gmix
        gained = gmix * gain[...]
        gconv = inv_std * (
            gained
            - jnp.mean(gained, axis=-1, keepdims=True)
            - normed * jnp.mean(gained * normed, axis=-1, keepdims=True)
        )
        grad_conv[pl.ds(first, group)] = gconv.reshape(group, cols, channels)
        contract = (((0,), (0,)), ((), ()))
        acc_up[...] += lax.dot_general(mixed, grad_pre, contract, preferred_element_type=f32)
        acc_down[...] += lax.dot_general(grad_out, hidden, contract, preferred_element_type=f32)

    unit = BATCH * BATCHES
    units = terms.shape[0] // unit

    def round_of(index, _):
        for place in range(ROUND):
            mlp_step(index * ROUND + place, place)

        @pl.when(index == 0)
        def _():
            for copy in scalar_copies:
                copy.wait()

        def add_unit(at, _):
            first_cell = at * (unit // fan)
            first_entry = index * terms.shape[0] + at * unit

            def add_batch(first, count):
                found = []
                for k in range(first, first + count):
                    place = (k % fan) * (ROUND * size) + first_cell + k // fan
                    found.append((targets[first_entry + k], terms[pl.ds(place, 1), :]))
                sums = [table[pl.ds(t, 1), :] + v for t, v in found]
                for (t, _), value in zip(found, sums):
                    table[pl.ds(t, 1), :] = value

            clashing = clash[first_entry]
            for level, count in enumerate((BATCH, SMALL, 1)):

                @pl.when(clashing == level)
                def _():
                    for first in range(0, unit, count):
                        add_batch(first, count)

            return 0

        lax.fori_loop(0, units, add_unit, 0)
        return 0

    lax.fori_loop(0, rows // (group * ROUND), round_of, 0)
    half = table.shape[0] // 2

    keep_copies = [
        pltpu.make_async_copy(table.at[pl.ds(k * (half // 4), half // 4)], keep, sems.at[2 + k])
        for k, keep in enumerate((keep_0, keep_1, keep_2, keep_3))
    ]
    for copy in keep_copies:
        copy.start()

    buffer_rows = outgoing.shape[0]
    for first in range(0, half, buffer_rows):

        def give(at):
            outgoing[at, :] = table[pl.ds(half + first + at.start, at.size), :].astype(bf16)

        in_chunks(buffer_rows, give)
        copy = pltpu.make_async_copy(outgoing, send.at[pl.ds(first, buffer_rows)], sems.at[6])
        copy.start()
        if first + buffer_rows < half:
            copy.wait()
    keep_copies.append(copy)
    blocks = up.shape[1] // channels
    for k in range(blocks):
        part = slice(k * channels, (k + 1) * channels)
        grads[k] = acc_up[:, part]
        grads[blocks + k] = acc_down[:, part].T
    for copy in keep_copies:
        copy.wait()


def find_targets(lat_count, lon_count, orders, owner, cell, targets, clash):
    lat, lon = lax.axis_index("lat"), lax.axis_index("lon")
    lon_bits = lon_count.bit_length() - 1
    half_rows = lat_count * lon_count // 2 * A_DEV
    width = A_DEV // 2
    device = owner[...]
    at_lat = (device >> lon_bits) ^ lat
    at_lon = (device & (lon_count - 1)) ^ lon
    numbers = []
    for order in orders:
        number = jnp.zeros_like(device)
        for bit in order:
            number = number * 2 + ((at_lon >> bit) & 1)
        numbers.append(number * lat_count + at_lat)
    upper = (cell[...] >= width).astype(jnp.int32)
    block = jnp.where(upper == 1, numbers[1], numbers[0])
    row = (at_lon & 1) * half_rows + upper * (half_rows // 2) + block * width
    row = row + cell[...] - upper * width
    targets[...] = row
    lane = lax.broadcasted_iota(jnp.int32, row.shape, 1)
    twice = jnp.zeros_like(row)
    for distance in range(BATCH - 1, 0, -1):
        same = row == pltpu.roll(row, distance, 1)
        twice = jnp.where(same & (lane % BATCH >= distance), jnp.maximum(twice, 1), twice)
        if distance < SMALL:
            twice = jnp.where(same & (lane % SMALL >= distance), 2, twice)
    distance = 1
    while distance < BATCH * BATCHES:
        twice = jnp.maximum(twice, pltpu.roll(twice, row.shape[1] - distance, 1))
        distance *= 2
    clash[...] = twice


def conv_grad_kernel(state, south, north, left, right, grad_conv, out, padded):
    rows, cols, channels = grad_conv.shape
    height = rows + 2 * MARGIN
    fill_rows(padded, state, south, north)
    for h in range(height):
        padded[h, PAD - MARGIN : PAD, :] = left[h].astype(f32)
        padded[h, PAD + cols : PAD + cols + MARGIN, :] = right[h].astype(f32)
    out[...] = jnp.zeros_like(out)
    unroll = 2
    for b in range(TAPS):

        def step_of(step, sums):
            sums = list(sums)
            for u in range(unroll):
                base = pl.multiple_of((step * unroll + u) * 8, 8)
                gc = [grad_conv[r, pl.ds(base, 8), :] for r in range(rows)]
                for h in range(height):
                    x = padded[h, pl.ds(base + (PAD - MARGIN + b), 8), :]
                    for a in range(TAPS):
                        if 0 <= h - a < rows:
                            k = a * 2 + (h - a) % 2
                            sums[k] = sums[k] + gc[h - a] * x
            return tuple(sums)

        zero = jnp.zeros((8, channels), f32)
        sums = lax.fori_loop(0, cols // (8 * unroll), step_of, (zero,) * (2 * TAPS))
        for a in range(TAPS):
            total = sums[2 * a] + sums[2 * a + 1]
            out[pl.ds(a * TAPS + b, 1), :] = jnp.sum(total, axis=0, keepdims=True)


def swap_bit(array, bit):
    pairs = [(i, i ^ (1 << bit)) for i in range(lax.axis_size("lon"))]
    return lax.ppermute(array, "lon", pairs)


def after(array, *others):
    return lax.optimization_barrier((array,) + others)[0]


def on_device(
    state, forcing, cotangent, land_mask, dw_weight, dw_bias, norm_gain, norm_bias,
    up_weight, up_bias, down_weight, down_bias, layer_scale, owner, atmos_cell, weight_index,
    intersection_weights,
):
    rows, cols, channels = state.shape
    cells = rows * cols
    hid = up_weight.shape[1]
    lat_count = lax.axis_size("lat")
    lon_count = lax.axis_size("lon")
    lat = lax.axis_index("lat")
    lon = lax.axis_index("lon")
    lon_bits = lon_count.bit_length() - 1
    devices = lat_count * lon_count
    entries = owner.shape[0]
    fan = entries // cells

    odd = lat % 2 == 1
    even_pairs, odd_pairs = [], []
    for l in range(lat_count):
        for j in range(lon_count):
            here = l * lon_count + j
            even_pairs.append((here, (l ^ 1) * lon_count + j))
            beyond = l + 1 if l % 2 else l - 1
            if 0 <= beyond < lat_count:
                odd_pairs.append((here, beyond * lon_count + j))
            else:
                odd_pairs.append((here, l * lon_count + lon_count - 1 - j))
    edge_rows = shape((MARGIN, cols, channels), bf16)
    for_even, for_odd = pl.pallas_call(
        functools.partial(edge_kernel, bands=lat_count),
        out_shape=(edge_rows, edge_rows),
        in_specs=[vmem()],
        out_specs=[vmem()] * 2,
        compiler_params=params(8),
        cost_estimate=cost(1),
        name="edges",
    )(state)
    got_even = lax.ppermute(for_even, ("lat", "lon"), even_pairs)
    got_odd = lax.ppermute(for_odd, ("lat", "lon"), odd_pairs)
    south = jnp.where(odd, got_even, jnp.where(lat == 0, jnp.zeros_like(got_odd), got_odd))
    north = jnp.where(odd, got_odd, got_even)

    forward = [(i, (i + 1) % lon_count) for i in range(lon_count)]
    backward = [(t, s) for s, t in forward]
    column = lambda part: jnp.concatenate([south[:, part], state[:, part], north[:, part]], axis=0)
    left = lax.ppermute(column(slice(cols - MARGIN, cols)), "lon", forward)
    right = lax.ppermute(column(slice(0, MARGIN)), "lon", backward)

    rest = list(range(1, lon_bits))
    orders = [rest, rest[::-1]]
    width = A_DEV // 2
    half_rows = devices // 2 * A_DEV
    lines = (entries // channels, channels)
    line = lambda v: v.reshape(1, -1)
    taps = dw_weight.reshape(-1, channels).astype(f32)
    conv, targets, clash = pl.pallas_call(
        functools.partial(inner_conv_kernel, lat_count, lon_count, orders),
        out_shape=(shape((rows, cols, channels), f32),) + (shape(lines, jnp.int32),) * 2,
        in_specs=[vmem()] * 5,
        out_specs=[vmem()] * 3,
        scratch_shapes=[pltpu.VMEM((rows, cols + 2 * PAD, channels), f32)],
        compiler_params=params(12),
        cost_estimate=cost(7),
        name="inner_conv",
    )(
        after(state, for_even), taps, line(dw_bias), owner.reshape(lines), atmos_cell.reshape(lines)
    )
    halo = pl.pallas_call(
        functools.partial(halo_conv_kernel, rows=rows),
        out_shape=shape((2 * MARGIN, cols, channels), f32),
        in_specs=[vmem()] * 3,
        out_specs=vmem(),
        scratch_shapes=[pltpu.VMEM((2 * MARGIN, cols + 2 * PAD, channels), f32)],
        compiler_params=params(8),
        cost_estimate=cost(2),
        name="halo_conv",
    )(south, north, taps)
    quarter = shape((half_rows // 4, channels), f32)
    result, *keep, send, grad_conv, grads = pl.pallas_call(
        block_kernel,
        out_shape=(
            shape((rows, cols, channels), bf16),
            *(quarter,) * 4,
            shape((half_rows, channels), bf16),
            shape((rows, cols, channels), f32),
            shape((2 * hid // channels, channels, channels), f32),
        ),
        in_specs=[vmem()] * 11 + [smem()] + [anywhere()] * 2 + [vmem()] * 11,
        out_specs=[vmem()] + [anywhere()] * 5 + [vmem()] * 2,
        scratch_shapes=[
            pltpu.VMEM((rows, cols, channels), f32),
            pltpu.VMEM((2, rows + 2 * MARGIN, 24, channels), f32),
            pltpu.VMEM((channels, hid), f32),
            pltpu.VMEM((channels, hid), f32),
            pltpu.VMEM((entries // channels, channels), f32),
            pltpu.VMEM((2 * fan * cols, channels), f32),
            pltpu.VMEM((ROUND * 2 * fan * cols, channels), f32),
            pltpu.VMEM((2 * half_rows, channels), f32),
            pltpu.VMEM((min(half_rows, 8192), channels), bf16),
            pltpu.SMEM((entries,), jnp.int32),
            pltpu.SMEM((entries,), jnp.int32),
            pltpu.SemaphoreType.DMA((7,)),
        ],
        compiler_params=params(min(60, 28 + (half_rows * channels * 10 >> 20))),
        cost_estimate=cost(28),
        name="block",
    )(
        state, south, north, left, right, conv, halo, forcing, cotangent, land_mask,
        weight_index.reshape(-1, channels), intersection_weights,
        targets.reshape(-1), clash.reshape(-1), taps, line(dw_bias), line(norm_gain), line(norm_bias), up_weight, line(up_bias),
        down_weight, line(down_bias), line(layer_scale), up_weight.T, down_weight.T,
    )

    got = swap_bit(send, 0)

    tap_count = dw_weight.shape[0] * dw_weight.shape[1]
    dw_rows = -(-tap_count // devices) * devices
    grad_dw = pl.pallas_call(
        conv_grad_kernel,
        out_shape=shape((dw_rows, channels), f32),
        in_specs=[vmem()] * 6,
        out_specs=vmem(),
        scratch_shapes=[pltpu.VMEM((rows + 2 * MARGIN, cols + 2 * PAD, channels), f32)],
        compiler_params=params(16),
        cost_estimate=cost(9),
        name="conv_grad",
    )(state, south, north, left, right, after(grad_conv, send))

    size = half_rows // 4
    got = after(got, grad_dw)
    slices = [(keep[k], got[k * size : (k + 1) * size]) for k in range(4)]
    add = lambda summands: functools.reduce(lambda x, y: x + y.astype(f32), summands)
    sends = [add(slices[1]).astype(bf16), add(slices[3]).astype(bf16)]
    first_sends = sends
    held = [list(slices[0]), list(slices[2])]
    for stage in range(len(rest)):
        arrived = [swap_bit(sends[q], orders[q][stage]) for q in range(2)]
        arrived = lax.optimization_barrier(tuple(arrived))
        for q in range(2):
            held[q].append(arrived[q])
        if stage + 1 < len(rest):
            size //= 2
            sends = [add([h[size : 2 * size] for h in held[q]]).astype(bf16) for q in range(2)]
            held = [[h[:size] for h in held[q]] for q in range(2)]
    def for_band(distance):
        at = slice(distance * width, (distance + 1) * width)
        return jnp.concatenate([add([h[at] for h in held[q]]) for q in range(2)], axis=0)

    forcing_grad = for_band(0)
    from_bands = []
    for distance in range(1, lat_count):
        pairs = [(i, i ^ distance) for i in range(lat_count)]
        from_bands.append(lax.ppermute(for_band(distance).astype(bf16), "lat", pairs))

    total = jnp.concatenate([grads.reshape(2 * hid, channels), grad_dw], axis=0).astype(bf16)
    total = after(total, *first_sends)
    total = total.reshape(devices, -1, channels)
    total = lax.all_to_all(total, ("lat", "lon"), split_axis=0, concat_axis=0, tiled=True)
    total = jnp.sum(total.astype(f32), axis=0, keepdims=True).astype(bf16)
    total = jnp.broadcast_to(total, (devices,) + total.shape[1:])
    total = lax.all_to_all(total, ("lat", "lon"), split_axis=0, concat_axis=0, tiled=True)
    scale = float(cells * devices) ** (-0.5)
    total = total.reshape(-1, channels).astype(f32) * scale
    grad_up = total[:hid].reshape(hid // channels, channels, channels)
    grad_up = grad_up.transpose(1, 0, 2).reshape(channels, hid)
    grad_down = total[hid : 2 * hid]
    grad_dw = total[2 * hid : 2 * hid + tap_count].reshape(dw_weight.shape)
    arrived, grad_dw, grad_up, grad_down = lax.optimization_barrier(
        (from_bands, grad_dw, grad_up, grad_down)
    )
    forcing_grad = add([forcing_grad] + list(arrived))
    return (result, grad_dw, grad_up, grad_down, forcing_grad)


def solution(mesh):
    grid = P("lat", "lon", None)
    in_specs = (grid, grid, grid, P("lat", "lon")) + (P(),) * 9
    in_specs += (P(("lat", "lon"), None), P(("lat", "lon")), P(("lat", "lon")), P())
    out_specs = (grid, P(), P(), P(), P(("lat", "lon"), None))
    return jax.shard_map(
        on_device, mesh=mesh, in_specs=in_specs, out_specs=out_specs, check_vma=False
    )
```

```python
import functools

import jax
import jax.numpy as jnp
from jax import lax
from jax.experimental import pallas as pl
from jax.experimental.pallas import tpu as pltpu
from jax.sharding import PartitionSpec as P

A_DEV = 512
PAD = 8
TAPS = 7
MARGIN = 3
BATCH = 16
BATCHES = 4
SMALL = 8
ROUND = 2
gelu_scale = 0.7978845608028654
cubic_coef = 0.044715
f32 = jnp.float32
bf16 = jnp.bfloat16
shape = jax.ShapeDtypeStruct


def params(mebibytes):
    return pltpu.CompilerParams(vmem_limit_bytes=mebibytes << 20)


def cost(microseconds):
    return pl.CostEstimate(flops=int(microseconds * 1e9), bytes_accessed=0, transcendentals=0)


def vmem():
    return pl.BlockSpec(memory_space=pltpu.VMEM)


def anywhere():
    return pl.BlockSpec(memory_space=pl.ANY)


def smem():
    return pl.BlockSpec(memory_space=pltpu.SMEM)


def in_chunks(rows, body):
    chunk = 512

    def step_of(step, _):
        body(pl.ds(pl.multiple_of(step * chunk, chunk), chunk))
        return 0

    lax.fori_loop(0, rows // chunk, step_of, 0)


def conv_sums(field, base, dw, starts, lines, rows):
    sums = dict(zip(rows, starts))
    for b in range(TAPS):
        weights = [
            jnp.broadcast_to(dw[pl.ds(a * TAPS + b, 1), :], (8, dw.shape[1])) for a in range(TAPS)
        ]
        for h in lines:
            x = field(h, base + (PAD - MARGIN + b))
            for a in range(TAPS):
                if h - a in sums:
                    sums[h - a] = sums[h - a] + weights[a] * x
    return [sums[r] for r in rows]


def edge_kernel(state, even, odd, *, bands):
    rows, cols, channels = state.shape
    lat = lax.axis_index("lat")

    @pl.when(lat % 2 == 1)
    def _():
        even[...] = state[0:MARGIN]
        odd[...] = state[rows - MARGIN : rows]

    @pl.when(lat % 2 == 0)
    def _():
        even[...] = state[rows - MARGIN : rows]
        odd[...] = state[0:MARGIN]

    @pl.when(lat == bands - 1)
    def _():
        column = lax.broadcasted_iota(jnp.int32, (cols, cols), 1)
        line = lax.broadcasted_iota(jnp.int32, (cols, cols), 0)
        reverse = jnp.where(line + column == cols - 1, 1.0, 0.0).astype(bf16)
        for m in range(MARGIN):
            turned = jnp.dot(reverse, state[rows - 1 - m], preferred_element_type=f32)
            odd[m] = turned.astype(bf16)


def inner_conv_kernel(
    lat_count, lon_count, orders, state, dw, dwb, owner, cell, conv, targets, clash, padded
):
    rows, cols, channels = state.shape
    find_targets(lat_count, lon_count, orders, owner, cell, targets, clash)
    for r in range(rows):
        padded[r, PAD : PAD + cols, :] = state[r].astype(f32)

    def step_of(step, _):
        base = pl.multiple_of(step * 8, 8)
        field = lambda h, at: padded[h - MARGIN, pl.ds(at, 8), :]
        bias = jnp.broadcast_to(dwb[...], (8, channels))
        lines = range(MARGIN, rows + MARGIN)
        sums = conv_sums(field, base, dw, [bias] * rows, lines, list(range(rows)))
        for r in range(rows):
            conv[r, pl.ds(base, 8), :] = sums[r]
        return 0

    lax.fori_loop(1, cols // 8 - 1, step_of, 0)


def halo_conv_kernel(south, north, dw, conv, padded, *, rows):
    _, cols, channels = south.shape
    padded[0:MARGIN, PAD : PAD + cols, :] = south[...].astype(f32)
    padded[MARGIN : 2 * MARGIN, PAD : PAD + cols, :] = north[...].astype(f32)

    def step_of(step, _):
        base = pl.multiple_of(step * 8, 8)
        zero = jnp.zeros((8, channels), f32)
        for side in range(2):
            first = 0 if side == 0 else rows + MARGIN
            field = lambda h, at: padded[h - first + side * MARGIN, pl.ds(at, 8), :]
            out = [k if side == 0 else rows - MARGIN + k for k in range(MARGIN)]
            lines = range(first, first + MARGIN)
            sums = conv_sums(field, base, dw, [zero] * MARGIN, lines, out)
            for k in range(MARGIN):
                conv[side * MARGIN + k, pl.ds(base, 8), :] = sums[k]
        return 0

    lax.fori_loop(1, cols // 8 - 1, step_of, 0)


def fill_rows(padded, state, south, north):
    rows, cols, _ = state.shape
    inner = slice(PAD, PAD + cols)
    padded[0:MARGIN, inner, :] = south[...].astype(f32)
    padded[rows + MARGIN : rows + 2 * MARGIN, inner, :] = north[...].astype(f32)
    for r in range(rows):
        padded[r + MARGIN, inner, :] = state[r].astype(f32)


def block_kernel(
    state, south, north, left, right, conv, halo, forcing, cotangent, land, weight_index, weight_table,
    target_list, clash_list, dw, dwb, gain, nbias, up, upb, down, downb, scale, up_t, down_t,
    result, keep_0, keep_1, keep_2, keep_3, send, grad_conv, grads,
    field, edge, acc_up, acc_down, entry_weights, spread, terms, table, outgoing, targets, clash, sems,
):
    rows, cols, channels = state.shape
    scalar_copies = [
        pltpu.make_async_copy(target_list, targets, sems.at[0]),
        pltpu.make_async_copy(clash_list, clash, sems.at[1]),
    ]
    for copy in scalar_copies:
        copy.start()
    wide = 16
    for side in range(2):
        own = slice(0, wide) if side == 0 else slice(cols - wide, cols)
        at = PAD if side == 0 else 0
        edge[side, 0:MARGIN, at : at + wide, :] = south[:, own, :].astype(f32)
        edge[side, rows + MARGIN : rows + 2 * MARGIN, at : at + wide, :] = north[:, own, :].astype(f32)
        for r in range(rows):
            edge[side, r + MARGIN, at : at + wide, :] = state[r, own, :].astype(f32)
        for h in range(rows + 2 * MARGIN):
            if side == 0:
                edge[side, h, PAD - MARGIN : PAD, :] = left[h].astype(f32)
            else:
                edge[side, h, wide : wide + MARGIN, :] = right[h].astype(f32)
        bias = jnp.broadcast_to(dwb[...], (8, channels))
        lines = range(rows + 2 * MARGIN)
        at_edge = lambda h, at: edge[side, h, pl.ds(at, 8), :]
        sums = conv_sums(at_edge, 0, dw, [bias] * rows, lines, list(range(rows)))
        out = slice(0, 8) if side == 0 else slice(cols - 8, cols)
        for r in range(rows):
            field[r, out, :] = sums[r]
    inner = slice(8, cols - 8)
    for r in range(rows):
        here = conv[r, inner, :]
        if r < MARGIN:
            here = here + halo[r, inner, :]
        if r >= rows - MARGIN:
            here = here + halo[r - rows + 2 * MARGIN, inner, :]
        field[r, inner, :] = here

    def clear(at):
        table[at, :] = jnp.zeros((at.size, channels), f32)

    in_chunks(table.shape[0], clear)
    index = weight_index[...]
    looked_up = jnp.zeros(index.shape, f32)
    for k in range(weight_table.shape[0]):
        looked_up = jnp.where(index == k, weight_table[k], looked_up)
    acc_up[...] = jnp.zeros_like(acc_up)
    acc_down[...] = jnp.zeros_like(acc_down)
    group = 2
    size = group * cols
    fan = terms.shape[0] // (ROUND * size)
    lines = fan * size // channels
    for k in range(rows // group):
        entry_weights[k] = looked_up[k * lines : (k + 1) * lines]

    def columns(step):
        first = step * group
        stacked = [entry_weights[step]]
        for k in range(group):
            mask = land[pl.ds(first + k, 1), :].astype(f32)
            stacked += [mask[:, at : at + channels] for at in range(0, cols, channels)]
        used = lines + group * cols // channels
        stacked.append(jnp.zeros((channels - used, channels), f32))
        turned = jnp.concatenate(stacked, axis=0).T
        wide = [jnp.broadcast_to(turned[:, j : j + 1], (channels, channels)) for j in range(used)]
        return jnp.concatenate(wide[:lines], axis=0), jnp.concatenate(wide[lines:], axis=0)

    def mlp_step(step, place):
        first = step * group
        here = field[pl.ds(first, group)].reshape(size, channels)
        average = jnp.mean(here, axis=-1, keepdims=True)
        centred = here - average
        variance = jnp.mean(centred * centred, axis=-1, keepdims=True)
        inv_std = lax.rsqrt(variance + 1e-06)
        normed = centred * inv_std
        force = forcing[pl.ds(first, group)].reshape(size, channels).astype(f32)
        mixed = (normed * gain[...] + nbias[...] + force).astype(bf16)
        pre = jnp.dot(mixed, up[...], preferred_element_type=f32) + upb[...]
        square = pre * pre
        tanh_value = jnp.tanh(pre * (gelu_scale + gelu_scale * cubic_coef * square))
        half = 0.5 + 0.5 * tanh_value
        hidden = (pre * half).astype(bf16)
        slope = half + pre * (1.0 - tanh_value * tanh_value) * (
            0.5 * gelu_scale + 1.5 * gelu_scale * cubic_coef * square
        )
        projected = jnp.dot(hidden, down[...], preferred_element_type=f32) + downb[...]
        spread[...], ocean = columns(step)
        own = state[pl.ds(first, group)].reshape(size, channels).astype(f32)
        out = ocean * (own + scale[...] * projected)
        result[pl.ds(first, group)] = out.astype(bf16).reshape(group, cols, channels)
        cot = cotangent[pl.ds(first, group)].reshape(size, channels).astype(f32)
        grad_out = (ocean * scale[...] * cot).astype(bf16)
        grad_hidden = jnp.dot(grad_out, down_t[...], preferred_element_type=f32)
        grad_pre = (grad_hidden * slope).astype(bf16)
        gmix = jnp.dot(grad_pre, up_t[...], preferred_element_type=f32)
        for k in range(fan):
            weights = spread[pl.ds(k, size, stride=fan), :]
            terms[pl.ds(k * ROUND * size + place * size, size), :] = weights * gmix
        gained = gmix * gain[...]
        gconv = inv_std * (
            gained
            - jnp.mean(gained, axis=-1, keepdims=True)
            - normed * jnp.mean(gained * normed, axis=-1, keepdims=True)
        )
        grad_conv[pl.ds(first, group)] = gconv.reshape(group, cols, channels)
        contract = (((0,), (0,)), ((), ()))
        acc_up[...] += lax.dot_general(mixed, grad_pre, contract, preferred_element_type=f32)
        acc_down[...] += lax.dot_general(grad_out, hidden, contract, preferred_element_type=f32)

    unit = BATCH * BATCHES
    units = terms.shape[0] // unit

    def round_of(index, _):
        for place in range(ROUND):
            mlp_step(index * ROUND + place, place)

        @pl.when(index == 0)
        def _():
            for copy in scalar_copies:
                copy.wait()

        def add_unit(at, _):
            first_cell = at * (unit // fan)
            first_entry = index * terms.shape[0] + at * unit

            def add_batch(first, count):
                found = []
                for k in range(first, first + count):
                    place = (k % fan) * (ROUND * size) + first_cell + k // fan
                    found.append((targets[first_entry + k], terms[pl.ds(place, 1), :]))
                sums = [table[pl.ds(t, 1), :] + v for t, v in found]
                for (t, _), value in zip(found, sums):
                    table[pl.ds(t, 1), :] = value

            clashing = clash[first_entry]
            for level, count in enumerate((BATCH, SMALL, 1)):

                @pl.when(clashing == level)
                def _():
                    for first in range(0, unit, count):
                        add_batch(first, count)

            return 0

        lax.fori_loop(0, units, add_unit, 0)
        return 0

    lax.fori_loop(0, rows // (group * ROUND), round_of, 0)
    half = table.shape[0] // 2

    keep_copies = [
        pltpu.make_async_copy(table.at[pl.ds(k * (half // 4), half // 4)], keep, sems.at[2 + k])
        for k, keep in enumerate((keep_0, keep_1, keep_2, keep_3))
    ]
    for copy in keep_copies:
        copy.start()

    buffer_rows = outgoing.shape[0]
    for first in range(0, half, buffer_rows):

        def give(at):
            outgoing[at, :] = table[pl.ds(half + first + at.start, at.size), :].astype(bf16)

        in_chunks(buffer_rows, give)
        copy = pltpu.make_async_copy(outgoing, send.at[pl.ds(first, buffer_rows)], sems.at[6])
        copy.start()
        if first + buffer_rows < half:
            copy.wait()
    keep_copies.append(copy)
    blocks = up.shape[1] // channels
    for k in range(blocks):
        part = slice(k * channels, (k + 1) * channels)
        grads[k] = acc_up[:, part]
        grads[blocks + k] = acc_down[:, part].T
    for copy in keep_copies:
        copy.wait()


def find_targets(lat_count, lon_count, orders, owner, cell, targets, clash):
    lat, lon = lax.axis_index("lat"), lax.axis_index("lon")
    lon_bits = lon_count.bit_length() - 1
    half_rows = lat_count * lon_count // 2 * A_DEV
    width = A_DEV // 2
    device = owner[...]
    at_lat = (device >> lon_bits) ^ lat
    at_lon = (device & (lon_count - 1)) ^ lon
    numbers = []
    for order in orders:
        number = jnp.zeros_like(device)
        for bit in order:
            number = number * 2 + ((at_lon >> bit) & 1)
        numbers.append(number * lat_count + at_lat)
    upper = (cell[...] >= width).astype(jnp.int32)
    block = jnp.where(upper == 1, numbers[1], numbers[0])
    row = (at_lon & 1) * half_rows + upper * (half_rows // 2) + block * width
    row = row + cell[...] - upper * width
    targets[...] = row
    lane = lax.broadcasted_iota(jnp.int32, row.shape, 1)
    twice = jnp.zeros_like(row)
    for distance in range(BATCH - 1, 0, -1):
        same = row == pltpu.roll(row, distance, 1)
        twice = jnp.where(same & (lane % BATCH >= distance), jnp.maximum(twice, 1), twice)
        if distance < SMALL:
            twice = jnp.where(same & (lane % SMALL >= distance), 2, twice)
    distance = 1
    while distance < BATCH * BATCHES:
        twice = jnp.maximum(twice, pltpu.roll(twice, row.shape[1] - distance, 1))
        distance *= 2
    clash[...] = twice


def conv_grad_kernel(state, south, north, left, right, grad_conv, out, padded):
    rows, cols, channels = grad_conv.shape
    height = rows + 2 * MARGIN
    fill_rows(padded, state, south, north)
    for h in range(height):
        padded[h, PAD - MARGIN : PAD, :] = left[h].astype(f32)
        padded[h, PAD + cols : PAD + cols + MARGIN, :] = right[h].astype(f32)
    out[...] = jnp.zeros_like(out)
    unroll = 2
    for b in range(TAPS):

        def step_of(step, sums):
            sums = list(sums)
            for u in range(unroll):
                base = pl.multiple_of((step * unroll + u) * 8, 8)
                gc = [grad_conv[r, pl.ds(base, 8), :] for r in range(rows)]
                for h in range(height):
                    x = padded[h, pl.ds(base + (PAD - MARGIN + b), 8), :]
                    for a in range(TAPS):
                        if 0 <= h - a < rows:
                            k = a * 2 + (h - a) % 2
                            sums[k] = sums[k] + gc[h - a] * x
            return tuple(sums)

        zero = jnp.zeros((8, channels), f32)
        sums = lax.fori_loop(0, cols // (8 * unroll), step_of, (zero,) * (2 * TAPS))
        for a in range(TAPS):
            total = sums[2 * a] + sums[2 * a + 1]
            out[pl.ds(a * TAPS + b, 1), :] = jnp.sum(total, axis=0, keepdims=True)


def swap_bit(array, bit):
    pairs = [(i, i ^ (1 << bit)) for i in range(lax.axis_size("lon"))]
    return lax.ppermute(array, "lon", pairs)


def after(array, *others):
    return lax.optimization_barrier((array,) + others)[0]


def on_device(
    state, forcing, cotangent, land_mask, dw_weight, dw_bias, norm_gain, norm_bias,
    up_weight, up_bias, down_weight, down_bias, layer_scale, owner, atmos_cell, weight_index,
    intersection_weights,
):
    rows, cols, channels = state.shape
    cells = rows * cols
    hid = up_weight.shape[1]
    lat_count = lax.axis_size("lat")
    lon_count = lax.axis_size("lon")
    lat = lax.axis_index("lat")
    lon = lax.axis_index("lon")
    lon_bits = lon_count.bit_length() - 1
    devices = lat_count * lon_count
    entries = owner.shape[0]
    fan = entries // cells

    odd = lat % 2 == 1
    even_pairs, odd_pairs = [], []
    for l in range(lat_count):
        for j in range(lon_count):
            here = l * lon_count + j
            even_pairs.append((here, (l ^ 1) * lon_count + j))
            beyond = l + 1 if l % 2 else l - 1
            if 0 <= beyond < lat_count:
                odd_pairs.append((here, beyond * lon_count + j))
            else:
                odd_pairs.append((here, l * lon_count + lon_count - 1 - j))
    edge_rows = shape((MARGIN, cols, channels), bf16)
    for_even, for_odd = pl.pallas_call(
        functools.partial(edge_kernel, bands=lat_count),
        out_shape=(edge_rows, edge_rows),
        in_specs=[vmem()],
        out_specs=[vmem()] * 2,
        compiler_params=params(8),
        cost_estimate=cost(1),
        name="edges",
    )(state)
    got_even = lax.ppermute(for_even, ("lat", "lon"), even_pairs)
    got_odd = lax.ppermute(for_odd, ("lat", "lon"), odd_pairs)
    south = jnp.where(odd, got_even, jnp.where(lat == 0, jnp.zeros_like(got_odd), got_odd))
    north = jnp.where(odd, got_odd, got_even)

    forward = [(i, (i + 1) % lon_count) for i in range(lon_count)]
    backward = [(t, s) for s, t in forward]
    column = lambda part: jnp.concatenate([south[:, part], state[:, part], north[:, part]], axis=0)
    left = lax.ppermute(column(slice(cols - MARGIN, cols)), "lon", forward)
    right = lax.ppermute(column(slice(0, MARGIN)), "lon", backward)

    rest = list(range(1, lon_bits))
    orders = [rest, rest[::-1]]
    width = A_DEV // 2
    half_rows = devices // 2 * A_DEV
    lines = (entries // channels, channels)
    line = lambda v: v.reshape(1, -1)
    taps = dw_weight.reshape(-1, channels).astype(f32)
    conv, targets, clash = pl.pallas_call(
        functools.partial(inner_conv_kernel, lat_count, lon_count, orders),
        out_shape=(shape((rows, cols, channels), f32),) + (shape(lines, jnp.int32),) * 2,
        in_specs=[vmem()] * 5,
        out_specs=[vmem()] * 3,
        scratch_shapes=[pltpu.VMEM((rows, cols + 2 * PAD, channels), f32)],
        compiler_params=params(12),
        cost_estimate=cost(7),
        name="inner_conv",
    )(
        after(state, for_even), taps, line(dw_bias), owner.reshape(lines), atmos_cell.reshape(lines)
    )
    halo = pl.pallas_call(
        functools.partial(halo_conv_kernel, rows=rows),
        out_shape=shape((2 * MARGIN, cols, channels), f32),
        in_specs=[vmem()] * 3,
        out_specs=vmem(),
        scratch_shapes=[pltpu.VMEM((2 * MARGIN, cols + 2 * PAD, channels), f32)],
        compiler_params=params(8),
        cost_estimate=cost(2),
        name="halo_conv",
    )(south, north, taps)
    quarter = shape((half_rows // 4, channels), f32)
    result, *keep, send, grad_conv, grads = pl.pallas_call(
        block_kernel,
        out_shape=(
            shape((rows, cols, channels), bf16),
            *(quarter,) * 4,
            shape((half_rows, channels), bf16),
            shape((rows, cols, channels), f32),
            shape((2 * hid // channels, channels, channels), f32),
        ),
        in_specs=[vmem()] * 11 + [smem()] + [anywhere()] * 2 + [vmem()] * 11,
        out_specs=[vmem()] + [anywhere()] * 5 + [vmem()] * 2,
        scratch_shapes=[
            pltpu.VMEM((rows, cols, channels), f32),
            pltpu.VMEM((2, rows + 2 * MARGIN, 24, channels), f32),
            pltpu.VMEM((channels, hid), f32),
            pltpu.VMEM((channels, hid), f32),
            pltpu.VMEM((rows // 2, 2 * entries // rows // channels, channels), f32),
            pltpu.VMEM((2 * fan * cols, channels), f32),
            pltpu.VMEM((ROUND * 2 * fan * cols, channels), f32),
            pltpu.VMEM((2 * half_rows, channels), f32),
            pltpu.VMEM((min(half_rows, 8192), channels), bf16),
            pltpu.SMEM((entries,), jnp.int32),
            pltpu.SMEM((entries,), jnp.int32),
            pltpu.SemaphoreType.DMA((7,)),
        ],
        compiler_params=params(min(60, 28 + (half_rows * channels * 10 >> 20))),
        cost_estimate=cost(28),
        name="block",
    )(
        state, south, north, left, right, conv, halo, forcing, cotangent, land_mask,
        weight_index.reshape(-1, channels), intersection_weights,
        targets.reshape(-1), clash.reshape(-1), taps, line(dw_bias), line(norm_gain), line(norm_bias), up_weight, line(up_bias),
        down_weight, line(down_bias), line(layer_scale), up_weight.T, down_weight.T,
    )

    got = swap_bit(send, 0)

    tap_count = dw_weight.shape[0] * dw_weight.shape[1]
    dw_rows = -(-tap_count // devices) * devices
    grad_dw = pl.pallas_call(
        conv_grad_kernel,
        out_shape=shape((dw_rows, channels), f32),
        in_specs=[vmem()] * 6,
        out_specs=vmem(),
        scratch_shapes=[pltpu.VMEM((rows + 2 * MARGIN, cols + 2 * PAD, channels), f32)],
        compiler_params=params(16),
        cost_estimate=cost(9),
        name="conv_grad",
    )(state, south, north, left, right, after(grad_conv, send))

    size = half_rows // 4
    got = after(got, grad_dw)
    slices = [(keep[k], got[k * size : (k + 1) * size]) for k in range(4)]
    add = lambda summands: functools.reduce(lambda x, y: x + y.astype(f32), summands)
    sends = [add(slices[1]).astype(bf16), add(slices[3]).astype(bf16)]
    first_sends = sends
    held = [list(slices[0]), list(slices[2])]
    for stage in range(len(rest)):
        arrived = [swap_bit(sends[q], orders[q][stage]) for q in range(2)]
        arrived = lax.optimization_barrier(tuple(arrived))
        for q in range(2):
            held[q].append(arrived[q])
        if stage + 1 < len(rest):
            size //= 2
            sends = [add([h[size : 2 * size] for h in held[q]]).astype(bf16) for q in range(2)]
            held = [[h[:size] for h in held[q]] for q in range(2)]
    def for_band(distance):
        at = slice(distance * width, (distance + 1) * width)
        return jnp.concatenate([add([h[at] for h in held[q]]) for q in range(2)], axis=0)

    forcing_grad = for_band(0)
    from_bands = []
    for distance in range(1, lat_count):
        pairs = [(i, i ^ distance) for i in range(lat_count)]
        from_bands.append(lax.ppermute(for_band(distance).astype(bf16), "lat", pairs))

    total = jnp.concatenate([grads.reshape(2 * hid, channels), grad_dw], axis=0).astype(bf16)
    total = after(total, *first_sends)
    total = total.reshape(devices, -1, channels)
    total = lax.all_to_all(total, ("lat", "lon"), split_axis=0, concat_axis=0, tiled=True)
    total = jnp.sum(total.astype(f32), axis=0, keepdims=True).astype(bf16)
    total = jnp.broadcast_to(total, (devices,) + total.shape[1:])
    total = lax.all_to_all(total, ("lat", "lon"), split_axis=0, concat_axis=0, tiled=True)
    scale = float(cells * devices) ** (-0.5)
    total = total.reshape(-1, channels).astype(f32) * scale
    grad_up = total[:hid].reshape(hid // channels, channels, channels)
    grad_up = grad_up.transpose(1, 0, 2).reshape(channels, hid)
    grad_down = total[hid : 2 * hid]
    grad_dw = total[2 * hid : 2 * hid + tap_count].reshape(dw_weight.shape)
    arrived, grad_dw, grad_up, grad_down = lax.optimization_barrier(
        (from_bands, grad_dw, grad_up, grad_down)
    )
    forcing_grad = add([forcing_grad] + list(arrived))
    return (result, grad_dw, grad_up, grad_down, forcing_grad)


def solution(mesh):
    grid = P("lat", "lon", None)
    in_specs = (grid, grid, grid, P("lat", "lon")) + (P(),) * 9
    in_specs += (P(("lat", "lon"), None), P(("lat", "lon")), P(("lat", "lon")), P())
    out_specs = (grid, P(), P(), P(), P(("lat", "lon"), None))
    return jax.shard_map(
        on_device, mesh=mesh, in_specs=in_specs, out_specs=out_specs, check_vma=False
    )
```

```python
import functools

import jax
import jax.numpy as jnp
from jax import lax
from jax.experimental import pallas as pl
from jax.experimental.pallas import tpu as pltpu
from jax.sharding import PartitionSpec as P

A_DEV = 512
PAD = 8
TAPS = 7
MARGIN = 3
BATCH = 16
BATCHES = 4
SMALL = 8
ROUND = 2
gelu_scale = 0.7978845608028654
cubic_coef = 0.044715
f32 = jnp.float32
bf16 = jnp.bfloat16
shape = jax.ShapeDtypeStruct


def params(mebibytes):
    return pltpu.CompilerParams(vmem_limit_bytes=mebibytes << 20)


def cost(microseconds):
    return pl.CostEstimate(flops=int(microseconds * 1e9), bytes_accessed=0, transcendentals=0)


def vmem():
    return pl.BlockSpec(memory_space=pltpu.VMEM)


def anywhere():
    return pl.BlockSpec(memory_space=pl.ANY)


def smem():
    return pl.BlockSpec(memory_space=pltpu.SMEM)


def in_chunks(rows, body):
    chunk = 512

    def step_of(step, _):
        body(pl.ds(pl.multiple_of(step * chunk, chunk), chunk))
        return 0

    lax.fori_loop(0, rows // chunk, step_of, 0)


def conv_sums(field, base, dw, starts, lines, rows):
    sums = dict(zip(rows, starts))
    for b in range(TAPS):
        weights = [
            jnp.broadcast_to(dw[pl.ds(a * TAPS + b, 1), :], (8, dw.shape[1])) for a in range(TAPS)
        ]
        for h in lines:
            x = field(h, base + (PAD - MARGIN + b))
            for a in range(TAPS):
                if h - a in sums:
                    sums[h - a] = sums[h - a] + weights[a] * x
    return [sums[r] for r in rows]


def edge_kernel(state, even, odd, *, bands):
    rows, cols, channels = state.shape
    lat = lax.axis_index("lat")

    @pl.when(lat % 2 == 1)
    def _():
        even[...] = state[0:MARGIN]
        odd[...] = state[rows - MARGIN : rows]

    @pl.when(lat % 2 == 0)
    def _():
        even[...] = state[rows - MARGIN : rows]
        odd[...] = state[0:MARGIN]

    @pl.when(lat == bands - 1)
    def _():
        column = lax.broadcasted_iota(jnp.int32, (cols, cols), 1)
        line = lax.broadcasted_iota(jnp.int32, (cols, cols), 0)
        reverse = jnp.where(line + column == cols - 1, 1.0, 0.0).astype(bf16)
        for m in range(MARGIN):
            turned = jnp.dot(reverse, state[rows - 1 - m], preferred_element_type=f32)
            odd[m] = turned.astype(bf16)


def inner_conv_kernel(
    lat_count, lon_count, orders, state, dw, dwb, owner, cell, conv, targets, clash, padded
):
    rows, cols, channels = state.shape
    find_targets(lat_count, lon_count, orders, owner, cell, targets, clash)
    for r in range(rows):
        padded[r, PAD : PAD + cols, :] = state[r].astype(f32)

    def step_of(step, _):
        base = pl.multiple_of(step * 8, 8)
        field = lambda h, at: padded[h - MARGIN, pl.ds(at, 8), :]
        bias = jnp.broadcast_to(dwb[...], (8, channels))
        lines = range(MARGIN, rows + MARGIN)
        sums = conv_sums(field, base, dw, [bias] * rows, lines, list(range(rows)))
        for r in range(rows):
            conv[r, pl.ds(base, 8), :] = sums[r]
        return 0

    lax.fori_loop(1, cols // 8 - 1, step_of, 0)


def halo_conv_kernel(south, north, dw, conv, padded, *, rows):
    _, cols, channels = south.shape
    padded[0:MARGIN, PAD : PAD + cols, :] = south[...].astype(f32)
    padded[MARGIN : 2 * MARGIN, PAD : PAD + cols, :] = north[...].astype(f32)

    def step_of(step, _):
        base = pl.multiple_of(step * 8, 8)
        zero = jnp.zeros((8, channels), f32)
        for side in range(2):
            first = 0 if side == 0 else rows + MARGIN
            field = lambda h, at: padded[h - first + side * MARGIN, pl.ds(at, 8), :]
            out = [k if side == 0 else rows - MARGIN + k for k in range(MARGIN)]
            lines = range(first, first + MARGIN)
            sums = conv_sums(field, base, dw, [zero] * MARGIN, lines, out)
            for k in range(MARGIN):
                conv[side * MARGIN + k, pl.ds(base, 8), :] = sums[k]
        return 0

    lax.fori_loop(1, cols // 8 - 1, step_of, 0)


def fill_rows(padded, state, south, north):
    rows, cols, _ = state.shape
    inner = slice(PAD, PAD + cols)
    padded[0:MARGIN, inner, :] = south[...].astype(f32)
    padded[rows + MARGIN : rows + 2 * MARGIN, inner, :] = north[...].astype(f32)
    for r in range(rows):
        padded[r + MARGIN, inner, :] = state[r].astype(f32)


def block_kernel(
    state, south, north, left, right, conv, halo, forcing, cotangent, land, weight_index, weight_table,
    target_list, clash_list, dw, dwb, gain, nbias, up, upb, down, downb, scale, up_t, down_t,
    result, keep_0, keep_1, keep_2, keep_3, send, grad_conv, grads,
    field, edge, acc_up, acc_down, entry_weights, spread, terms, table, outgoing, targets, clash, sems,
):
    rows, cols, channels = state.shape
    scalar_copies = [
        pltpu.make_async_copy(target_list, targets, sems.at[0]),
        pltpu.make_async_copy(clash_list, clash, sems.at[1]),
    ]
    for copy in scalar_copies:
        copy.start()
    wide = 16
    for side in range(2):
        own = slice(0, wide) if side == 0 else slice(cols - wide, cols)
        at = PAD if side == 0 else 0
        edge[side, 0:MARGIN, at : at + wide, :] = south[:, own, :].astype(f32)
        edge[side, rows + MARGIN : rows + 2 * MARGIN, at : at + wide, :] = north[:, own, :].astype(f32)
        for r in range(rows):
            edge[side, r + MARGIN, at : at + wide, :] = state[r, own, :].astype(f32)
        for h in range(rows + 2 * MARGIN):
            if side == 0:
                edge[side, h, PAD - MARGIN : PAD, :] = left[h].astype(f32)
            else:
                edge[side, h, wide : wide + MARGIN, :] = right[h].astype(f32)
        bias = jnp.broadcast_to(dwb[...], (8, channels))
        lines = range(rows + 2 * MARGIN)
        at_edge = lambda h, at: edge[side, h, pl.ds(at, 8), :]
        sums = conv_sums(at_edge, 0, dw, [bias] * rows, lines, list(range(rows)))
        out = slice(0, 8) if side == 0 else slice(cols - 8, cols)
        for r in range(rows):
            field[r, out, :] = sums[r]
    inner = slice(8, cols - 8)
    for r in range(rows):
        here = conv[r, inner, :]
        if r < MARGIN:
            here = here + halo[r, inner, :]
        if r >= rows - MARGIN:
            here = here + halo[r - rows + 2 * MARGIN, inner, :]
        field[r, inner, :] = here

    def clear(at):
        table[at, :] = jnp.zeros((at.size, channels), f32)

    in_chunks(table.shape[0], clear)
    index = weight_index[...]
    looked_up = jnp.zeros(index.shape, f32)
    for k in range(weight_table.shape[0]):
        looked_up = jnp.where(index == k, weight_table[k], looked_up)
    acc_up[...] = jnp.zeros_like(acc_up)
    acc_down[...] = jnp.zeros_like(acc_down)
    group = 2
    size = group * cols
    fan = terms.shape[0] // (ROUND * size)
    lines = fan * size // channels
    for k in range(rows // group):
        entry_weights[k] = looked_up[k * lines : (k + 1) * lines]

    def columns(step):
        first = step * group
        stacked = [entry_weights[step]]
        for k in range(group):
            mask = land[pl.ds(first + k, 1), :].astype(f32)
            stacked += [mask[:, at : at + channels] for at in range(0, cols, channels)]
        used = lines + group * cols // channels
        stacked.append(jnp.zeros((channels - used, channels), f32))
        turned = jnp.concatenate(stacked, axis=0).T
        wide = [jnp.broadcast_to(turned[:, j : j + 1], (channels, channels)) for j in range(used)]
        return jnp.concatenate(wide[:lines], axis=0), jnp.concatenate(wide[lines:], axis=0)

    share = 1.0 / channels
    mean_one = jnp.full((channels, channels), share, bf16)
    mean_both = jnp.full((2 * channels, channels), share, bf16)
    corner = [
        lax.broadcasted_iota(jnp.int32, (2 * channels, 2 * channels), d) < channels for d in range(2)
    ]
    mean_each = jnp.where(corner[0] == corner[1], share, 0.0).astype(bf16)

    def mlp_step(step, place):
        first = step * group
        here = field[pl.ds(first, group)].reshape(size, channels)
        high = here.astype(bf16)
        low = (here - high.astype(f32)).astype(bf16)
        average = jnp.dot(jnp.concatenate([high, low], axis=1), mean_both, preferred_element_type=f32)
        centred = here - average
        variance = jnp.dot((centred * centred).astype(bf16), mean_one, preferred_element_type=f32)
        inv_std = lax.rsqrt(variance + 1e-06)
        normed = centred * inv_std
        force = forcing[pl.ds(first, group)].reshape(size, channels).astype(f32)
        mixed = (normed * gain[...] + nbias[...] + force).astype(bf16)
        pre = jnp.dot(mixed, up[...], preferred_element_type=f32) + upb[...]
        square = pre * pre
        tanh_value = jnp.tanh(pre * (gelu_scale + gelu_scale * cubic_coef * square))
        half = 0.5 + 0.5 * tanh_value
        hidden = (pre * half).astype(bf16)
        slope = half + pre * (1.0 - tanh_value * tanh_value) * (
            0.5 * gelu_scale + 1.5 * gelu_scale * cubic_coef * square
        )
        projected = jnp.dot(hidden, down[...], preferred_element_type=f32) + downb[...]
        spread[...], ocean = columns(step)
        own = state[pl.ds(first, group)].reshape(size, channels).astype(f32)
        out = ocean * (own + scale[...] * projected)
        result[pl.ds(first, group)] = out.astype(bf16).reshape(group, cols, channels)
        cot = cotangent[pl.ds(first, group)].reshape(size, channels).astype(f32)
        grad_out = (ocean * scale[...] * cot).astype(bf16)
        grad_hidden = jnp.dot(grad_out, down_t[...], preferred_element_type=f32)
        grad_pre = (grad_hidden * slope).astype(bf16)
        gmix = jnp.dot(grad_pre, up_t[...], preferred_element_type=f32)
        for k in range(fan):
            weights = spread[pl.ds(k, size, stride=fan), :]
            terms[pl.ds(k * ROUND * size + place * size, size), :] = weights * gmix
        gained = gmix * gain[...]
        pair = jnp.concatenate([gained.astype(bf16), (gained * normed).astype(bf16)], axis=1)
        means = jnp.dot(pair, mean_each, preferred_element_type=f32)
        gconv = inv_std * (gained - means[:, :channels] - normed * means[:, channels:])
        grad_conv[pl.ds(first, group)] = gconv.reshape(group, cols, channels)
        contract = (((0,), (0,)), ((), ()))
        acc_up[...] += lax.dot_general(mixed, grad_pre, contract, preferred_element_type=f32)
        acc_down[...] += lax.dot_general(grad_out, hidden, contract, preferred_element_type=f32)

    unit = BATCH * BATCHES
    units = terms.shape[0] // unit

    def round_of(index, _):
        for place in range(ROUND):
            mlp_step(index * ROUND + place, place)

        @pl.when(index == 0)
        def _():
            for copy in scalar_copies:
                copy.wait()

        def add_unit(at, _):
            first_cell = at * (unit // fan)
            first_entry = index * terms.shape[0] + at * unit

            def add_batch(first, count):
                found = []
                for k in range(first, first + count):
                    place = (k % fan) * (ROUND * size) + first_cell + k // fan
                    found.append((targets[first_entry + k], terms[pl.ds(place, 1), :]))
                sums = [table[pl.ds(t, 1), :] + v for t, v in found]
                for (t, _), value in zip(found, sums):
                    table[pl.ds(t, 1), :] = value

            clashing = clash[first_entry]
            for level, count in enumerate((BATCH, SMALL, 1)):

                @pl.when(clashing == level)
                def _():
                    for first in range(0, unit, count):
                        add_batch(first, count)

            return 0

        lax.fori_loop(0, units, add_unit, 0)
        return 0

    lax.fori_loop(0, rows // (group * ROUND), round_of, 0)
    half = table.shape[0] // 2

    keep_copies = [
        pltpu.make_async_copy(table.at[pl.ds(k * (half // 4), half // 4)], keep, sems.at[2 + k])
        for k, keep in enumerate((keep_0, keep_1, keep_2, keep_3))
    ]
    for copy in keep_copies:
        copy.start()

    buffer_rows = outgoing.shape[0]
    for first in range(0, half, buffer_rows):

        def give(at):
            outgoing[at, :] = table[pl.ds(half + first + at.start, at.size), :].astype(bf16)

        in_chunks(buffer_rows, give)
        copy = pltpu.make_async_copy(outgoing, send.at[pl.ds(first, buffer_rows)], sems.at[6])
        copy.start()
        if first + buffer_rows < half:
            copy.wait()
    keep_copies.append(copy)
    blocks = up.shape[1] // channels
    for k in range(blocks):
        part = slice(k * channels, (k + 1) * channels)
        grads[k] = acc_up[:, part]
        grads[blocks + k] = acc_down[:, part].T
    for copy in keep_copies:
        copy.wait()


def find_targets(lat_count, lon_count, orders, owner, cell, targets, clash):
    lat, lon = lax.axis_index("lat"), lax.axis_index("lon")
    lon_bits = lon_count.bit_length() - 1
    half_rows = lat_count * lon_count // 2 * A_DEV
    width = A_DEV // 2
    device = owner[...]
    at_lat = (device >> lon_bits) ^ lat
    at_lon = (device & (lon_count - 1)) ^ lon
    numbers = []
    for order in orders:
        number = jnp.zeros_like(device)
        for bit in order:
            number = number * 2 + ((at_lon >> bit) & 1)
        numbers.append(number * lat_count + at_lat)
    upper = (cell[...] >= width).astype(jnp.int32)
    block = jnp.where(upper == 1, numbers[1], numbers[0])
    row = (at_lon & 1) * half_rows + upper * (half_rows // 2) + block * width
    row = row + cell[...] - upper * width
    targets[...] = row
    lane = lax.broadcasted_iota(jnp.int32, row.shape, 1)
    twice = jnp.zeros_like(row)
    for distance in range(BATCH - 1, 0, -1):
        same = row == pltpu.roll(row, distance, 1)
        twice = jnp.where(same & (lane % BATCH >= distance), jnp.maximum(twice, 1), twice)
        if distance < SMALL:
            twice = jnp.where(same & (lane % SMALL >= distance), 2, twice)
    distance = 1
    while distance < BATCH * BATCHES:
        twice = jnp.maximum(twice, pltpu.roll(twice, row.shape[1] - distance, 1))
        distance *= 2
    clash[...] = twice


def conv_grad_kernel(state, south, north, left, right, grad_conv, out, padded):
    rows, cols, channels = grad_conv.shape
    height = rows + 2 * MARGIN
    fill_rows(padded, state, south, north)
    for h in range(height):
        padded[h, PAD - MARGIN : PAD, :] = left[h].astype(f32)
        padded[h, PAD + cols : PAD + cols + MARGIN, :] = right[h].astype(f32)
    out[...] = jnp.zeros_like(out)
    unroll = 2
    for b in range(TAPS):

        def step_of(step, sums):
            sums = list(sums)
            for u in range(unroll):
                base = pl.multiple_of((step * unroll + u) * 8, 8)
                gc = [grad_conv[r, pl.ds(base, 8), :] for r in range(rows)]
                for h in range(height):
                    x = padded[h, pl.ds(base + (PAD - MARGIN + b), 8), :]
                    for a in range(TAPS):
                        if 0 <= h - a < rows:
                            k = a * 2 + (h - a) % 2
                            sums[k] = sums[k] + gc[h - a] * x
            return tuple(sums)

        zero = jnp.zeros((8, channels), f32)
        sums = lax.fori_loop(0, cols // (8 * unroll), step_of, (zero,) * (2 * TAPS))
        for a in range(TAPS):
            total = sums[2 * a] + sums[2 * a + 1]
            out[pl.ds(a * TAPS + b, 1), :] = jnp.sum(total, axis=0, keepdims=True)


def swap_bit(array, bit):
    pairs = [(i, i ^ (1 << bit)) for i in range(lax.axis_size("lon"))]
    return lax.ppermute(array, "lon", pairs)


def after(array, *others):
    return lax.optimization_barrier((array,) + others)[0]


def on_device(
    state, forcing, cotangent, land_mask, dw_weight, dw_bias, norm_gain, norm_bias,
    up_weight, up_bias, down_weight, down_bias, layer_scale, owner, atmos_cell, weight_index,
    intersection_weights,
):
    rows, cols, channels = state.shape
    cells = rows * cols
    hid = up_weight.shape[1]
    lat_count = lax.axis_size("lat")
    lon_count = lax.axis_size("lon")
    lat = lax.axis_index("lat")
    lon = lax.axis_index("lon")
    lon_bits = lon_count.bit_length() - 1
    devices = lat_count * lon_count
    entries = owner.shape[0]
    fan = entries // cells

    odd = lat % 2 == 1
    even_pairs, odd_pairs = [], []
    for l in range(lat_count):
        for j in range(lon_count):
            here = l * lon_count + j
            even_pairs.append((here, (l ^ 1) * lon_count + j))
            beyond = l + 1 if l % 2 else l - 1
            if 0 <= beyond < lat_count:
                odd_pairs.append((here, beyond * lon_count + j))
            else:
                odd_pairs.append((here, l * lon_count + lon_count - 1 - j))
    edge_rows = shape((MARGIN, cols, channels), bf16)
    for_even, for_odd = pl.pallas_call(
        functools.partial(edge_kernel, bands=lat_count),
        out_shape=(edge_rows, edge_rows),
        in_specs=[vmem()],
        out_specs=[vmem()] * 2,
        compiler_params=params(8),
        cost_estimate=cost(1),
        name="edges",
    )(state)
    got_even = lax.ppermute(for_even, ("lat", "lon"), even_pairs)
    got_odd = lax.ppermute(for_odd, ("lat", "lon"), odd_pairs)
    south = jnp.where(odd, got_even, jnp.where(lat == 0, jnp.zeros_like(got_odd), got_odd))
    north = jnp.where(odd, got_odd, got_even)

    forward = [(i, (i + 1) % lon_count) for i in range(lon_count)]
    backward = [(t, s) for s, t in forward]
    column = lambda part: jnp.concatenate([south[:, part], state[:, part], north[:, part]], axis=0)
    left = lax.ppermute(column(slice(cols - MARGIN, cols)), "lon", forward)
    right = lax.ppermute(column(slice(0, MARGIN)), "lon", backward)

    rest = list(range(1, lon_bits))
    orders = [rest, rest[::-1]]
    width = A_DEV // 2
    half_rows = devices // 2 * A_DEV
    lines = (entries // channels, channels)
    line = lambda v: v.reshape(1, -1)
    taps = dw_weight.reshape(-1, channels).astype(f32)
    conv, targets, clash = pl.pallas_call(
        functools.partial(inner_conv_kernel, lat_count, lon_count, orders),
        out_shape=(shape((rows, cols, channels), f32),) + (shape(lines, jnp.int32),) * 2,
        in_specs=[vmem()] * 5,
        out_specs=[vmem()] * 3,
        scratch_shapes=[pltpu.VMEM((rows, cols + 2 * PAD, channels), f32)],
        compiler_params=params(12),
        cost_estimate=cost(7),
        name="inner_conv",
    )(
        after(state, for_even), taps, line(dw_bias), owner.reshape(lines), atmos_cell.reshape(lines)
    )
    halo = pl.pallas_call(
        functools.partial(halo_conv_kernel, rows=rows),
        out_shape=shape((2 * MARGIN, cols, channels), f32),
        in_specs=[vmem()] * 3,
        out_specs=vmem(),
        scratch_shapes=[pltpu.VMEM((2 * MARGIN, cols + 2 * PAD, channels), f32)],
        compiler_params=params(8),
        cost_estimate=cost(2),
        name="halo_conv",
    )(south, north, taps)
    quarter = shape((half_rows // 4, channels), f32)
    result, *keep, send, grad_conv, grads = pl.pallas_call(
        block_kernel,
        out_shape=(
            shape((rows, cols, channels), bf16),
            *(quarter,) * 4,
            shape((half_rows, channels), bf16),
            shape((rows, cols, channels), f32),
            shape((2 * hid // channels, channels, channels), f32),
        ),
        in_specs=[vmem()] * 11 + [smem()] + [anywhere()] * 2 + [vmem()] * 11,
        out_specs=[vmem()] + [anywhere()] * 5 + [vmem()] * 2,
        scratch_shapes=[
            pltpu.VMEM((rows, cols, channels), f32),
            pltpu.VMEM((2, rows + 2 * MARGIN, 24, channels), f32),
            pltpu.VMEM((channels, hid), f32),
            pltpu.VMEM((channels, hid), f32),
            pltpu.VMEM((rows // 2, 2 * entries // rows // channels, channels), f32),
            pltpu.VMEM((2 * fan * cols, channels), f32),
            pltpu.VMEM((ROUND * 2 * fan * cols, channels), f32),
            pltpu.VMEM((2 * half_rows, channels), f32),
            pltpu.VMEM((min(half_rows, 8192), channels), bf16),
            pltpu.SMEM((entries,), jnp.int32),
            pltpu.SMEM((entries,), jnp.int32),
            pltpu.SemaphoreType.DMA((7,)),
        ],
        compiler_params=params(min(60, 28 + (half_rows * channels * 10 >> 20))),
        cost_estimate=cost(28),
        name="block",
    )(
        state, south, north, left, right, conv, halo, forcing, cotangent, land_mask,
        weight_index.reshape(-1, channels), intersection_weights,
        targets.reshape(-1), clash.reshape(-1), taps, line(dw_bias), line(norm_gain), line(norm_bias), up_weight, line(up_bias),
        down_weight, line(down_bias), line(layer_scale), up_weight.T, down_weight.T,
    )

    got = swap_bit(send, 0)

    tap_count = dw_weight.shape[0] * dw_weight.shape[1]
    dw_rows = -(-tap_count // devices) * devices
    grad_dw = pl.pallas_call(
        conv_grad_kernel,
        out_shape=shape((dw_rows, channels), f32),
        in_specs=[vmem()] * 6,
        out_specs=vmem(),
        scratch_shapes=[pltpu.VMEM((rows + 2 * MARGIN, cols + 2 * PAD, channels), f32)],
        compiler_params=params(16),
        cost_estimate=cost(9),
        name="conv_grad",
    )(state, south, north, left, right, after(grad_conv, send))

    size = half_rows // 4
    got = after(got, grad_dw)
    slices = [(keep[k], got[k * size : (k + 1) * size]) for k in range(4)]
    add = lambda summands: functools.reduce(lambda x, y: x + y.astype(f32), summands)
    sends = [add(slices[1]).astype(bf16), add(slices[3]).astype(bf16)]
    first_sends = sends
    held = [list(slices[0]), list(slices[2])]
    for stage in range(len(rest)):
        arrived = [swap_bit(sends[q], orders[q][stage]) for q in range(2)]
        arrived = lax.optimization_barrier(tuple(arrived))
        for q in range(2):
            held[q].append(arrived[q])
        if stage + 1 < len(rest):
            size //= 2
            sends = [add([h[size : 2 * size] for h in held[q]]).astype(bf16) for q in range(2)]
            held = [[h[:size] for h in held[q]] for q in range(2)]
    def for_band(distance):
        at = slice(distance * width, (distance + 1) * width)
        return jnp.concatenate([add([h[at] for h in held[q]]) for q in range(2)], axis=0)

    forcing_grad = for_band(0)
    from_bands = []
    for distance in range(1, lat_count):
        pairs = [(i, i ^ distance) for i in range(lat_count)]
        from_bands.append(lax.ppermute(for_band(distance).astype(bf16), "lat", pairs))

    total = jnp.concatenate([grads.reshape(2 * hid, channels), grad_dw], axis=0).astype(bf16)
    total = after(total, *first_sends)
    total = total.reshape(devices, -1, channels)
    total = lax.all_to_all(total, ("lat", "lon"), split_axis=0, concat_axis=0, tiled=True)
    total = jnp.sum(total.astype(f32), axis=0, keepdims=True).astype(bf16)
    total = jnp.broadcast_to(total, (devices,) + total.shape[1:])
    total = lax.all_to_all(total, ("lat", "lon"), split_axis=0, concat_axis=0, tiled=True)
    scale = float(cells * devices) ** (-0.5)
    total = total.reshape(-1, channels).astype(f32) * scale
    grad_up = total[:hid].reshape(hid // channels, channels, channels)
    grad_up = grad_up.transpose(1, 0, 2).reshape(channels, hid)
    grad_down = total[hid : 2 * hid]
    grad_dw = total[2 * hid : 2 * hid + tap_count].reshape(dw_weight.shape)
    arrived, grad_dw, grad_up, grad_down = lax.optimization_barrier(
        (from_bands, grad_dw, grad_up, grad_down)
    )
    forcing_grad = add([forcing_grad] + list(arrived))
    return (result, grad_dw, grad_up, grad_down, forcing_grad)


def solution(mesh):
    grid = P("lat", "lon", None)
    in_specs = (grid, grid, grid, P("lat", "lon")) + (P(),) * 9
    in_specs += (P(("lat", "lon"), None), P(("lat", "lon")), P(("lat", "lon")), P())
    out_specs = (grid, P(), P(), P(), P(("lat", "lon"), None))
    return jax.shard_map(
        on_device, mesh=mesh, in_specs=in_specs, out_specs=out_specs, check_vma=False
    )
```

```python
import functools

import jax
import jax.numpy as jnp
from jax import lax
from jax.experimental import pallas as pl
from jax.experimental.pallas import tpu as pltpu
from jax.sharding import PartitionSpec as P

A_DEV = 512
PAD = 8
TAPS = 7
MARGIN = 3
BATCH = 16
BATCHES = 4
SMALL = 8
ROUND = 2
gelu_scale = 0.7978845608028654
cubic_coef = 0.044715
f32 = jnp.float32
bf16 = jnp.bfloat16
shape = jax.ShapeDtypeStruct


def params(mebibytes):
    return pltpu.CompilerParams(vmem_limit_bytes=mebibytes << 20)


def cost(microseconds):
    return pl.CostEstimate(flops=int(microseconds * 1e9), bytes_accessed=0, transcendentals=0)


def vmem():
    return pl.BlockSpec(memory_space=pltpu.VMEM)


def anywhere():
    return pl.BlockSpec(memory_space=pl.ANY)


def smem():
    return pl.BlockSpec(memory_space=pltpu.SMEM)


def in_chunks(rows, body):
    chunk = 512

    def step_of(step, _):
        body(pl.ds(pl.multiple_of(step * chunk, chunk), chunk))
        return 0

    lax.fori_loop(0, rows // chunk, step_of, 0)


def conv_sums(field, base, dw, starts, lines, rows):
    sums = dict(zip(rows, starts))
    for b in range(TAPS):
        weights = [
            jnp.broadcast_to(dw[pl.ds(a * TAPS + b, 1), :], (8, dw.shape[1])) for a in range(TAPS)
        ]
        for h in lines:
            x = field(h, base + (PAD - MARGIN + b))
            for a in range(TAPS):
                if h - a in sums:
                    sums[h - a] = sums[h - a] + weights[a] * x
    return [sums[r] for r in rows]


def edge_kernel(state, even, odd, *, bands):
    rows, cols, channels = state.shape
    lat = lax.axis_index("lat")

    @pl.when(lat % 2 == 1)
    def _():
        even[...] = state[0:MARGIN]
        odd[...] = state[rows - MARGIN : rows]

    @pl.when(lat % 2 == 0)
    def _():
        even[...] = state[rows - MARGIN : rows]
        odd[...] = state[0:MARGIN]

    @pl.when(lat == bands - 1)
    def _():
        column = lax.broadcasted_iota(jnp.int32, (cols, cols), 1)
        line = lax.broadcasted_iota(jnp.int32, (cols, cols), 0)
        reverse = jnp.where(line + column == cols - 1, 1.0, 0.0).astype(bf16)
        for m in range(MARGIN):
            turned = jnp.dot(reverse, state[rows - 1 - m], preferred_element_type=f32)
            odd[m] = turned.astype(bf16)


def inner_conv_kernel(
    lat_count, lon_count, orders, state, dw, dwb, owner, cell, conv, targets, clash, padded
):
    rows, cols, channels = state.shape
    find_targets(lat_count, lon_count, orders, owner, cell, targets, clash)
    for r in range(rows):
        padded[r, PAD : PAD + cols, :] = state[r].astype(f32)

    def step_of(step, _):
        base = pl.multiple_of(step * 8, 8)
        field = lambda h, at: padded[h - MARGIN, pl.ds(at, 8), :]
        bias = jnp.broadcast_to(dwb[...], (8, channels))
        lines = range(MARGIN, rows + MARGIN)
        sums = conv_sums(field, base, dw, [bias] * rows, lines, list(range(rows)))
        for r in range(rows):
            conv[r, pl.ds(base, 8), :] = sums[r]
        return 0

    lax.fori_loop(1, cols // 8 - 1, step_of, 0)


def halo_conv_kernel(south, north, dw, conv, padded, *, rows):
    _, cols, channels = south.shape
    padded[0:MARGIN, PAD : PAD + cols, :] = south[...].astype(f32)
    padded[MARGIN : 2 * MARGIN, PAD : PAD + cols, :] = north[...].astype(f32)

    def step_of(step, _):
        base = pl.multiple_of(step * 8, 8)
        zero = jnp.zeros((8, channels), f32)
        for side in range(2):
            first = 0 if side == 0 else rows + MARGIN
            field = lambda h, at: padded[h - first + side * MARGIN, pl.ds(at, 8), :]
            out = [k if side == 0 else rows - MARGIN + k for k in range(MARGIN)]
            lines = range(first, first + MARGIN)
            sums = conv_sums(field, base, dw, [zero] * MARGIN, lines, out)
            for k in range(MARGIN):
                conv[side * MARGIN + k, pl.ds(base, 8), :] = sums[k]
        return 0

    lax.fori_loop(1, cols // 8 - 1, step_of, 0)


def fill_rows(padded, state, south, north):
    rows, cols, _ = state.shape
    inner = slice(PAD, PAD + cols)
    padded[0:MARGIN, inner, :] = south[...].astype(f32)
    padded[rows + MARGIN : rows + 2 * MARGIN, inner, :] = north[...].astype(f32)
    for r in range(rows):
        padded[r + MARGIN, inner, :] = state[r].astype(f32)


def block_kernel(
    state, south, north, left, right, conv, halo, forcing, cotangent, land, weight_index, weight_table,
    target_list, clash_list, dw, dwb, gain, nbias, up, upb, down, downb, scale, up_t, down_t,
    result, keep_0, keep_1, keep_2, keep_3, send, grad_conv, grads,
    field, edge, acc_up, acc_down, entry_weights, spread, terms, table, outgoing, targets, clash, sems,
):
    rows, cols, channels = state.shape
    scalar_copies = [
        pltpu.make_async_copy(target_list, targets, sems.at[0]),
        pltpu.make_async_copy(clash_list, clash, sems.at[1]),
    ]
    for copy in scalar_copies:
        copy.start()
    wide = 16
    for side in range(2):
        own = slice(0, wide) if side == 0 else slice(cols - wide, cols)
        at = PAD if side == 0 else 0
        edge[side, 0:MARGIN, at : at + wide, :] = south[:, own, :].astype(f32)
        edge[side, rows + MARGIN : rows + 2 * MARGIN, at : at + wide, :] = north[:, own, :].astype(f32)
        for r in range(rows):
            edge[side, r + MARGIN, at : at + wide, :] = state[r, own, :].astype(f32)
        for h in range(rows + 2 * MARGIN):
            if side == 0:
                edge[side, h, PAD - MARGIN : PAD, :] = left[h].astype(f32)
            else:
                edge[side, h, wide : wide + MARGIN, :] = right[h].astype(f32)
        bias = jnp.broadcast_to(dwb[...], (8, channels))
        lines = range(rows + 2 * MARGIN)
        at_edge = lambda h, at: edge[side, h, pl.ds(at, 8), :]
        sums = conv_sums(at_edge, 0, dw, [bias] * rows, lines, list(range(rows)))
        out = slice(0, 8) if side == 0 else slice(cols - 8, cols)
        for r in range(rows):
            field[r, out, :] = sums[r]
    inner = slice(8, cols - 8)
    for r in range(rows):
        here = conv[r, inner, :]
        if r < MARGIN:
            here = here + halo[r, inner, :]
        if r >= rows - MARGIN:
            here = here + halo[r - rows + 2 * MARGIN, inner, :]
        field[r, inner, :] = here

    def clear(at):
        table[at, :] = jnp.zeros((at.size, channels), f32)

    in_chunks(table.shape[0], clear)
    index = weight_index[...]
    looked_up = jnp.zeros(index.shape, f32)
    for k in range(weight_table.shape[0]):
        looked_up = jnp.where(index == k, weight_table[k], looked_up)
    acc_up[...] = jnp.zeros_like(acc_up)
    acc_down[...] = jnp.zeros_like(acc_down)
    group = 2
    size = group * cols
    fan = terms.shape[0] // (ROUND * size)
    lines = fan * size // channels
    for k in range(rows // group):
        entry_weights[k] = looked_up[k * lines : (k + 1) * lines]

    def columns(step):
        first = step * group
        stacked = [entry_weights[step]]
        for k in range(group):
            mask = land[pl.ds(first + k, 1), :].astype(f32)
            stacked += [mask[:, at : at + channels] for at in range(0, cols, channels)]
        used = lines + group * cols // channels
        stacked.append(jnp.zeros((channels - used, channels), f32))
        turned = jnp.concatenate(stacked, axis=0).T
        wide = [jnp.broadcast_to(turned[:, j : j + 1], (channels, channels)) for j in range(used)]
        return jnp.concatenate(wide[:lines], axis=0), jnp.concatenate(wide[lines:], axis=0)

    def mlp_step(step, place):
        first = step * group
        spread[...], ocean = columns(step)
        cot = cotangent[pl.ds(first, group)].reshape(size, channels).astype(f32)
        grad_out = (ocean * scale[...] * cot).astype(bf16)
        grad_hidden = jnp.dot(grad_out, down_t[...], preferred_element_type=f32)
        here = field[pl.ds(first, group)].reshape(size, channels)
        average = jnp.mean(here, axis=-1, keepdims=True)
        centred = here - average
        variance = jnp.mean(centred * centred, axis=-1, keepdims=True)
        inv_std = lax.rsqrt(variance + 1e-06)
        normed = centred * inv_std
        force = forcing[pl.ds(first, group)].reshape(size, channels).astype(f32)
        mixed = (normed * gain[...] + nbias[...] + force).astype(bf16)
        pre = jnp.dot(mixed, up[...], preferred_element_type=f32) + upb[...]
        square = pre * pre
        tanh_value = jnp.tanh(pre * (gelu_scale + gelu_scale * cubic_coef * square))
        half = 0.5 + 0.5 * tanh_value
        hidden = (pre * half).astype(bf16)
        slope = half + pre * (1.0 - tanh_value * tanh_value) * (
            0.5 * gelu_scale + 1.5 * gelu_scale * cubic_coef * square
        )
        grad_pre = (grad_hidden * slope).astype(bf16)
        gmix = jnp.dot(grad_pre, up_t[...], preferred_element_type=f32)
        for k in range(fan):
            weights = spread[pl.ds(k, size, stride=fan), :]
            terms[pl.ds(k * ROUND * size + place * size, size), :] = weights * gmix
        projected = jnp.dot(hidden, down[...], preferred_element_type=f32) + downb[...]
        own = state[pl.ds(first, group)].reshape(size, channels).astype(f32)
        out = ocean * (own + scale[...] * projected)
        result[pl.ds(first, group)] = out.astype(bf16).reshape(group, cols, channels)
        gained = gmix * gain[...]
        gconv = inv_std * (
            gained
            - jnp.mean(gained, axis=-1, keepdims=True)
            - normed * jnp.mean(gained * normed, axis=-1, keepdims=True)
        )
        grad_conv[pl.ds(first, group)] = gconv.reshape(group, cols, channels)
        contract = (((0,), (0,)), ((), ()))
        acc_up[...] += lax.dot_general(mixed, grad_pre, contract, preferred_element_type=f32)
        acc_down[...] += lax.dot_general(grad_out, hidden, contract, preferred_element_type=f32)

    unit = BATCH * BATCHES
    units = terms.shape[0] // unit

    def round_of(index, _):
        for place in range(ROUND):
            mlp_step(index * ROUND + place, place)

        @pl.when(index == 0)
        def _():
            for copy in scalar_copies:
                copy.wait()

        def add_unit(at, _):
            first_cell = at * (unit // fan)
            first_entry = index * terms.shape[0] + at * unit

            def add_batch(first, count):
                found = []
                for k in range(first, first + count):
                    place = (k % fan) * (ROUND * size) + first_cell + k // fan
                    found.append((targets[first_entry + k], terms[pl.ds(place, 1), :]))
                sums = [table[pl.ds(t, 1), :] + v for t, v in found]
                for (t, _), value in zip(found, sums):
                    table[pl.ds(t, 1), :] = value

            clashing = clash[first_entry]
            for level, count in enumerate((BATCH, SMALL, 1)):

                @pl.when(clashing == level)
                def _():
                    for first in range(0, unit, count):
                        add_batch(first, count)

            return 0

        lax.fori_loop(0, units, add_unit, 0)
        return 0

    lax.fori_loop(0, rows // (group * ROUND), round_of, 0)
    half = table.shape[0] // 2

    keep_copies = [
        pltpu.make_async_copy(table.at[pl.ds(k * (half // 4), half // 4)], keep, sems.at[2 + k])
        for k, keep in enumerate((keep_0, keep_1, keep_2, keep_3))
    ]
    for copy in keep_copies:
        copy.start()

    buffer_rows = outgoing.shape[0]
    for first in range(0, half, buffer_rows):

        def give(at):
            outgoing[at, :] = table[pl.ds(half + first + at.start, at.size), :].astype(bf16)

        in_chunks(buffer_rows, give)
        copy = pltpu.make_async_copy(outgoing, send.at[pl.ds(first, buffer_rows)], sems.at[6])
        copy.start()
        if first + buffer_rows < half:
            copy.wait()
    keep_copies.append(copy)
    blocks = up.shape[1] // channels
    for k in range(blocks):
        part = slice(k * channels, (k + 1) * channels)
        grads[k] = acc_up[:, part]
        grads[blocks + k] = acc_down[:, part].T
    for copy in keep_copies:
        copy.wait()


def find_targets(lat_count, lon_count, orders, owner, cell, targets, clash):
    lat, lon = lax.axis_index("lat"), lax.axis_index("lon")
    lon_bits = lon_count.bit_length() - 1
    half_rows = lat_count * lon_count // 2 * A_DEV
    width = A_DEV // 2
    device = owner[...]
    at_lat = (device >> lon_bits) ^ lat
    at_lon = (device & (lon_count - 1)) ^ lon
    numbers = []
    for order in orders:
        number = jnp.zeros_like(device)
        for bit in order:
            number = number * 2 + ((at_lon >> bit) & 1)
        numbers.append(number * lat_count + at_lat)
    upper = (cell[...] >= width).astype(jnp.int32)
    block = jnp.where(upper == 1, numbers[1], numbers[0])
    row = (at_lon & 1) * half_rows + upper * (half_rows // 2) + block * width
    row = row + cell[...] - upper * width
    targets[...] = row
    lane = lax.broadcasted_iota(jnp.int32, row.shape, 1)
    twice = jnp.zeros_like(row)
    for distance in range(BATCH - 1, 0, -1):
        same = row == pltpu.roll(row, distance, 1)
        twice = jnp.where(same & (lane % BATCH >= distance), jnp.maximum(twice, 1), twice)
        if distance < SMALL:
            twice = jnp.where(same & (lane % SMALL >= distance), 2, twice)
    distance = 1
    while distance < BATCH * BATCHES:
        twice = jnp.maximum(twice, pltpu.roll(twice, row.shape[1] - distance, 1))
        distance *= 2
    clash[...] = twice


def conv_grad_kernel(state, south, north, left, right, grad_conv, out, padded):
    rows, cols, channels = grad_conv.shape
    height = rows + 2 * MARGIN
    fill_rows(padded, state, south, north)
    for h in range(height):
        padded[h, PAD - MARGIN : PAD, :] = left[h].astype(f32)
        padded[h, PAD + cols : PAD + cols + MARGIN, :] = right[h].astype(f32)
    out[...] = jnp.zeros_like(out)
    unroll = 2
    for b in range(TAPS):

        def step_of(step, sums):
            sums = list(sums)
            for u in range(unroll):
                base = pl.multiple_of((step * unroll + u) * 8, 8)
                gc = [grad_conv[r, pl.ds(base, 8), :] for r in range(rows)]
                for h in range(height):
                    x = padded[h, pl.ds(base + (PAD - MARGIN + b), 8), :]
                    for a in range(TAPS):
                        if 0 <= h - a < rows:
                            k = a * 2 + (h - a) % 2
                            sums[k] = sums[k] + gc[h - a] * x
            return tuple(sums)

        zero = jnp.zeros((8, channels), f32)
        sums = lax.fori_loop(0, cols // (8 * unroll), step_of, (zero,) * (2 * TAPS))
        for a in range(TAPS):
            total = sums[2 * a] + sums[2 * a + 1]
            out[pl.ds(a * TAPS + b, 1), :] = jnp.sum(total, axis=0, keepdims=True)


def swap_bit(array, bit):
    pairs = [(i, i ^ (1 << bit)) for i in range(lax.axis_size("lon"))]
    return lax.ppermute(array, "lon", pairs)


def after(array, *others):
    return lax.optimization_barrier((array,) + others)[0]


def on_device(
    state, forcing, cotangent, land_mask, dw_weight, dw_bias, norm_gain, norm_bias,
    up_weight, up_bias, down_weight, down_bias, layer_scale, owner, atmos_cell, weight_index,
    intersection_weights,
):
    rows, cols, channels = state.shape
    cells = rows * cols
    hid = up_weight.shape[1]
    lat_count = lax.axis_size("lat")
    lon_count = lax.axis_size("lon")
    lat = lax.axis_index("lat")
    lon = lax.axis_index("lon")
    lon_bits = lon_count.bit_length() - 1
    devices = lat_count * lon_count
    entries = owner.shape[0]
    fan = entries // cells

    odd = lat % 2 == 1
    even_pairs, odd_pairs = [], []
    for l in range(lat_count):
        for j in range(lon_count):
            here = l * lon_count + j
            even_pairs.append((here, (l ^ 1) * lon_count + j))
            beyond = l + 1 if l % 2 else l - 1
            if 0 <= beyond < lat_count:
                odd_pairs.append((here, beyond * lon_count + j))
            else:
                odd_pairs.append((here, l * lon_count + lon_count - 1 - j))
    edge_rows = shape((MARGIN, cols, channels), bf16)
    for_even, for_odd = pl.pallas_call(
        functools.partial(edge_kernel, bands=lat_count),
        out_shape=(edge_rows, edge_rows),
        in_specs=[vmem()],
        out_specs=[vmem()] * 2,
        compiler_params=params(8),
        cost_estimate=cost(1),
        name="edges",
    )(state)
    got_even = lax.ppermute(for_even, ("lat", "lon"), even_pairs)
    got_odd = lax.ppermute(for_odd, ("lat", "lon"), odd_pairs)
    south = jnp.where(odd, got_even, jnp.where(lat == 0, jnp.zeros_like(got_odd), got_odd))
    north = jnp.where(odd, got_odd, got_even)

    forward = [(i, (i + 1) % lon_count) for i in range(lon_count)]
    backward = [(t, s) for s, t in forward]
    column = lambda part: jnp.concatenate([south[:, part], state[:, part], north[:, part]], axis=0)
    left = lax.ppermute(column(slice(cols - MARGIN, cols)), "lon", forward)
    right = lax.ppermute(column(slice(0, MARGIN)), "lon", backward)

    rest = list(range(1, lon_bits))
    orders = [rest, rest[::-1]]
    width = A_DEV // 2
    half_rows = devices // 2 * A_DEV
    lines = (entries // channels, channels)
    line = lambda v: v.reshape(1, -1)
    taps = dw_weight.reshape(-1, channels).astype(f32)
    conv, targets, clash = pl.pallas_call(
        functools.partial(inner_conv_kernel, lat_count, lon_count, orders),
        out_shape=(shape((rows, cols, channels), f32),) + (shape(lines, jnp.int32),) * 2,
        in_specs=[vmem()] * 5,
        out_specs=[vmem()] * 3,
        scratch_shapes=[pltpu.VMEM((rows, cols + 2 * PAD, channels), f32)],
        compiler_params=params(12),
        cost_estimate=cost(7),
        name="inner_conv",
    )(
        after(state, for_even), taps, line(dw_bias), owner.reshape(lines), atmos_cell.reshape(lines)
    )
    halo = pl.pallas_call(
        functools.partial(halo_conv_kernel, rows=rows),
        out_shape=shape((2 * MARGIN, cols, channels), f32),
        in_specs=[vmem()] * 3,
        out_specs=vmem(),
        scratch_shapes=[pltpu.VMEM((2 * MARGIN, cols + 2 * PAD, channels), f32)],
        compiler_params=params(8),
        cost_estimate=cost(2),
        name="halo_conv",
    )(south, north, taps)
    quarter = shape((half_rows // 4, channels), f32)
    result, *keep, send, grad_conv, grads = pl.pallas_call(
        block_kernel,
        out_shape=(
            shape((rows, cols, channels), bf16),
            *(quarter,) * 4,
            shape((half_rows, channels), bf16),
            shape((rows, cols, channels), f32),
            shape((2 * hid // channels, channels, channels), f32),
        ),
        in_specs=[vmem()] * 11 + [smem()] + [anywhere()] * 2 + [vmem()] * 11,
        out_specs=[vmem()] + [anywhere()] * 5 + [vmem()] * 2,
        scratch_shapes=[
            pltpu.VMEM((rows, cols, channels), f32),
            pltpu.VMEM((2, rows + 2 * MARGIN, 24, channels), f32),
            pltpu.VMEM((channels, hid), f32),
            pltpu.VMEM((channels, hid), f32),
            pltpu.VMEM((rows // 2, 2 * entries // rows // channels, channels), f32),
            pltpu.VMEM((2 * fan * cols, channels), f32),
            pltpu.VMEM((ROUND * 2 * fan * cols, channels), f32),
            pltpu.VMEM((2 * half_rows, channels), f32),
            pltpu.VMEM((min(half_rows, 8192), channels), bf16),
            pltpu.SMEM((entries,), jnp.int32),
            pltpu.SMEM((entries,), jnp.int32),
            pltpu.SemaphoreType.DMA((7,)),
        ],
        compiler_params=params(min(60, 28 + (half_rows * channels * 10 >> 20))),
        cost_estimate=cost(28),
        name="block",
    )(
        state, south, north, left, right, conv, halo, forcing, cotangent, land_mask,
        weight_index.reshape(-1, channels), intersection_weights,
        targets.reshape(-1), clash.reshape(-1), taps, line(dw_bias), line(norm_gain), line(norm_bias), up_weight, line(up_bias),
        down_weight, line(down_bias), line(layer_scale), up_weight.T, down_weight.T,
    )

    got = swap_bit(send, 0)

    tap_count = dw_weight.shape[0] * dw_weight.shape[1]
    dw_rows = -(-tap_count // devices) * devices
    grad_dw = pl.pallas_call(
        conv_grad_kernel,
        out_shape=shape((dw_rows, channels), f32),
        in_specs=[vmem()] * 6,
        out_specs=vmem(),
        scratch_shapes=[pltpu.VMEM((rows + 2 * MARGIN, cols + 2 * PAD, channels), f32)],
        compiler_params=params(16),
        cost_estimate=cost(9),
        name="conv_grad",
    )(state, south, north, left, right, after(grad_conv, send))

    size = half_rows // 4
    got = after(got, grad_dw)
    slices = [(keep[k], got[k * size : (k + 1) * size]) for k in range(4)]
    add = lambda summands: functools.reduce(lambda x, y: x + y.astype(f32), summands)
    sends = [add(slices[1]).astype(bf16), add(slices[3]).astype(bf16)]
    first_sends = sends
    held = [list(slices[0]), list(slices[2])]
    for stage in range(len(rest)):
        arrived = [swap_bit(sends[q], orders[q][stage]) for q in range(2)]
        arrived = lax.optimization_barrier(tuple(arrived))
        for q in range(2):
            held[q].append(arrived[q])
        if stage + 1 < len(rest):
            size //= 2
            sends = [add([h[size : 2 * size] for h in held[q]]).astype(bf16) for q in range(2)]
            held = [[h[:size] for h in held[q]] for q in range(2)]
    def for_band(distance):
        at = slice(distance * width, (distance + 1) * width)
        return jnp.concatenate([add([h[at] for h in held[q]]) for q in range(2)], axis=0)

    forcing_grad = for_band(0)
    from_bands = []
    for distance in range(1, lat_count):
        pairs = [(i, i ^ distance) for i in range(lat_count)]
        from_bands.append(lax.ppermute(for_band(distance).astype(bf16), "lat", pairs))

    total = jnp.concatenate([grads.reshape(2 * hid, channels), grad_dw], axis=0).astype(bf16)
    total = after(total, *first_sends)
    total = total.reshape(devices, -1, channels)
    total = lax.all_to_all(total, ("lat", "lon"), split_axis=0, concat_axis=0, tiled=True)
    total = jnp.sum(total.astype(f32), axis=0, keepdims=True).astype(bf16)
    total = jnp.broadcast_to(total, (devices,) + total.shape[1:])
    total = lax.all_to_all(total, ("lat", "lon"), split_axis=0, concat_axis=0, tiled=True)
    scale = float(cells * devices) ** (-0.5)
    total = total.reshape(-1, channels).astype(f32) * scale
    grad_up = total[:hid].reshape(hid // channels, channels, channels)
    grad_up = grad_up.transpose(1, 0, 2).reshape(channels, hid)
    grad_down = total[hid : 2 * hid]
    grad_dw = total[2 * hid : 2 * hid + tap_count].reshape(dw_weight.shape)
    arrived, grad_dw, grad_up, grad_down = lax.optimization_barrier(
        (from_bands, grad_dw, grad_up, grad_down)
    )
    forcing_grad = add([forcing_grad] + list(arrived))
    return (result, grad_dw, grad_up, grad_down, forcing_grad)


def solution(mesh):
    grid = P("lat", "lon", None)
    in_specs = (grid, grid, grid, P("lat", "lon")) + (P(),) * 9
    in_specs += (P(("lat", "lon"), None), P(("lat", "lon")), P(("lat", "lon")), P())
    out_specs = (grid, P(), P(), P(), P(("lat", "lon"), None))
    return jax.shard_map(
        on_device, mesh=mesh, in_specs=in_specs, out_specs=out_specs, check_vma=False
    )
```

```python
import functools

import jax
import jax.numpy as jnp
from jax import lax
from jax.experimental import pallas as pl
from jax.experimental.pallas import tpu as pltpu
from jax.sharding import PartitionSpec as P

A_DEV = 512
PAD = 8
TAPS = 7
MARGIN = 3
BATCH = 16
BATCHES = 4
SMALL = 8
ROUND = 2
gelu_scale = 0.7978845608028654
cubic_coef = 0.044715
f32 = jnp.float32
bf16 = jnp.bfloat16
shape = jax.ShapeDtypeStruct


def params(mebibytes):
    return pltpu.CompilerParams(vmem_limit_bytes=mebibytes << 20)


def cost(microseconds):
    return pl.CostEstimate(flops=int(microseconds * 1e9), bytes_accessed=0, transcendentals=0)


def vmem():
    return pl.BlockSpec(memory_space=pltpu.VMEM)


def anywhere():
    return pl.BlockSpec(memory_space=pl.ANY)


def smem():
    return pl.BlockSpec(memory_space=pltpu.SMEM)


def in_chunks(rows, body):
    chunk = 512

    def step_of(step, _):
        body(pl.ds(pl.multiple_of(step * chunk, chunk), chunk))
        return 0

    lax.fori_loop(0, rows // chunk, step_of, 0)


def conv_sums(field, base, dw, starts, lines, rows):
    sums = dict(zip(rows, starts))
    for b in range(TAPS):
        weights = [
            jnp.broadcast_to(dw[pl.ds(a * TAPS + b, 1), :], (8, dw.shape[1])) for a in range(TAPS)
        ]
        for h in lines:
            x = field(h, base + (PAD - MARGIN + b))
            for a in range(TAPS):
                if h - a in sums:
                    sums[h - a] = sums[h - a] + weights[a] * x
    return [sums[r] for r in rows]


def edge_kernel(state, even, odd, *, bands):
    rows, cols, channels = state.shape
    lat = lax.axis_index("lat")

    @pl.when(lat % 2 == 1)
    def _():
        even[...] = state[0:MARGIN]
        odd[...] = state[rows - MARGIN : rows]

    @pl.when(lat % 2 == 0)
    def _():
        even[...] = state[rows - MARGIN : rows]
        odd[...] = state[0:MARGIN]

    @pl.when(lat == bands - 1)
    def _():
        column = lax.broadcasted_iota(jnp.int32, (cols, cols), 1)
        line = lax.broadcasted_iota(jnp.int32, (cols, cols), 0)
        reverse = jnp.where(line + column == cols - 1, 1.0, 0.0).astype(bf16)
        for m in range(MARGIN):
            turned = jnp.dot(reverse, state[rows - 1 - m], preferred_element_type=f32)
            odd[m] = turned.astype(bf16)


def inner_conv_kernel(
    lat_count, lon_count, orders, state, dw, dwb, owner, cell, conv, targets, clash, padded
):
    rows, cols, channels = state.shape
    find_targets(lat_count, lon_count, orders, owner, cell, targets, clash)
    for r in range(rows):
        padded[r, PAD : PAD + cols, :] = state[r].astype(f32)

    def step_of(step, _):
        base = pl.multiple_of(step * 8, 8)
        field = lambda h, at: padded[h - MARGIN, pl.ds(at, 8), :]
        bias = jnp.broadcast_to(dwb[...], (8, channels))
        lines = range(MARGIN, rows + MARGIN)
        sums = conv_sums(field, base, dw, [bias] * rows, lines, list(range(rows)))
        for r in range(rows):
            conv[r, pl.ds(base, 8), :] = sums[r]
        return 0

    lax.fori_loop(1, cols // 8 - 1, step_of, 0)


def halo_conv_kernel(south, north, dw, conv, padded, *, rows):
    _, cols, channels = south.shape
    padded[0:MARGIN, PAD : PAD + cols, :] = south[...].astype(f32)
    padded[MARGIN : 2 * MARGIN, PAD : PAD + cols, :] = north[...].astype(f32)

    def step_of(step, _):
        base = pl.multiple_of(step * 8, 8)
        zero = jnp.zeros((8, channels), f32)
        for side in range(2):
            first = 0 if side == 0 else rows + MARGIN
            field = lambda h, at: padded[h - first + side * MARGIN, pl.ds(at, 8), :]
            out = [k if side == 0 else rows - MARGIN + k for k in range(MARGIN)]
            lines = range(first, first + MARGIN)
            sums = conv_sums(field, base, dw, [zero] * MARGIN, lines, out)
            for k in range(MARGIN):
                conv[side * MARGIN + k, pl.ds(base, 8), :] = sums[k]
        return 0

    lax.fori_loop(1, cols // 8 - 1, step_of, 0)


def fill_rows(padded, state, south, north):
    rows, cols, _ = state.shape
    inner = slice(PAD, PAD + cols)
    padded[0:MARGIN, inner, :] = south[...].astype(f32)
    padded[rows + MARGIN : rows + 2 * MARGIN, inner, :] = north[...].astype(f32)
    for r in range(rows):
        padded[r + MARGIN, inner, :] = state[r].astype(f32)


def block_kernel(
    state, south, north, left, right, conv, halo, forcing, cotangent, land, weight_index, weight_table,
    target_list, clash_list, dw, dwb, gain, nbias, up, upb, down, downb, scale, up_t, down_t,
    result, keep_0, keep_1, keep_2, keep_3, send, grad_conv, grads,
    field, edge, acc_up, acc_down, entry_weights, spread, terms, table, outgoing, targets, clash, sems,
):
    rows, cols, channels = state.shape
    scalar_copies = [
        pltpu.make_async_copy(target_list, targets, sems.at[0]),
        pltpu.make_async_copy(clash_list, clash, sems.at[1]),
    ]
    for copy in scalar_copies:
        copy.start()
    wide = 16
    for side in range(2):
        own = slice(0, wide) if side == 0 else slice(cols - wide, cols)
        at = PAD if side == 0 else 0
        edge[side, 0:MARGIN, at : at + wide, :] = south[:, own, :].astype(f32)
        edge[side, rows + MARGIN : rows + 2 * MARGIN, at : at + wide, :] = north[:, own, :].astype(f32)
        for r in range(rows):
            edge[side, r + MARGIN, at : at + wide, :] = state[r, own, :].astype(f32)
        for h in range(rows + 2 * MARGIN):
            if side == 0:
                edge[side, h, PAD - MARGIN : PAD, :] = left[h].astype(f32)
            else:
                edge[side, h, wide : wide + MARGIN, :] = right[h].astype(f32)
        bias = jnp.broadcast_to(dwb[...], (8, channels))
        lines = range(rows + 2 * MARGIN)
        at_edge = lambda h, at: edge[side, h, pl.ds(at, 8), :]
        sums = conv_sums(at_edge, 0, dw, [bias] * rows, lines, list(range(rows)))
        out = slice(0, 8) if side == 0 else slice(cols - 8, cols)
        for r in range(rows):
            field[r, out, :] = sums[r]
    inner = slice(8, cols - 8)
    for r in range(rows):
        here = conv[r, inner, :]
        if r < MARGIN:
            here = here + halo[r, inner, :]
        if r >= rows - MARGIN:
            here = here + halo[r - rows + 2 * MARGIN, inner, :]
        field[r, inner, :] = here

    index = weight_index[...]
    looked_up = jnp.zeros(index.shape, f32)
    for k in range(weight_table.shape[0]):
        looked_up = jnp.where(index == k, weight_table[k], looked_up)
    acc_up[...] = jnp.zeros_like(acc_up)
    acc_down[...] = jnp.zeros_like(acc_down)
    group = 2
    size = group * cols
    fan = terms.shape[0] // (ROUND * size)
    lines = fan * size // channels
    for k in range(rows // group):
        entry_weights[k] = looked_up[k * lines : (k + 1) * lines]

    def columns(step):
        first = step * group
        stacked = [entry_weights[step]]
        for k in range(group):
            mask = land[pl.ds(first + k, 1), :].astype(f32)
            stacked += [mask[:, at : at + channels] for at in range(0, cols, channels)]
        used = lines + group * cols // channels
        stacked.append(jnp.zeros((channels - used, channels), f32))
        turned = jnp.concatenate(stacked, axis=0).T
        wide = [jnp.broadcast_to(turned[:, j : j + 1], (channels, channels)) for j in range(used)]
        return jnp.concatenate(wide[:lines], axis=0), jnp.concatenate(wide[lines:], axis=0)

    def mlp_step(step, place):
        first = step * group
        here = field[pl.ds(first, group)].reshape(size, channels)
        average = jnp.mean(here, axis=-1, keepdims=True)
        centred = here - average
        variance = jnp.mean(centred * centred, axis=-1, keepdims=True)
        inv_std = lax.rsqrt(variance + 1e-06)
        normed = centred * inv_std
        force = forcing[pl.ds(first, group)].reshape(size, channels).astype(f32)
        mixed = (normed * gain[...] + nbias[...] + force).astype(bf16)
        pre = jnp.dot(mixed, up[...], preferred_element_type=f32) + upb[...]
        square = pre * pre
        tanh_value = jnp.tanh(pre * (gelu_scale + gelu_scale * cubic_coef * square))
        half = 0.5 + 0.5 * tanh_value
        hidden = (pre * half).astype(bf16)
        slope = half + pre * (1.0 - tanh_value * tanh_value) * (
            0.5 * gelu_scale + 1.5 * gelu_scale * cubic_coef * square
        )
        projected = jnp.dot(hidden, down[...], preferred_element_type=f32) + downb[...]
        spread[...], ocean = columns(step)
        own = state[pl.ds(first, group)].reshape(size, channels).astype(f32)
        out = ocean * (own + scale[...] * projected)
        result[pl.ds(first, group)] = out.astype(bf16).reshape(group, cols, channels)
        cot = cotangent[pl.ds(first, group)].reshape(size, channels).astype(f32)
        grad_out = (ocean * scale[...] * cot).astype(bf16)
        grad_hidden = jnp.dot(grad_out, down_t[...], preferred_element_type=f32)
        grad_pre = (grad_hidden * slope).astype(bf16)
        gmix = jnp.dot(grad_pre, up_t[...], preferred_element_type=f32)
        for k in range(fan):
            weights = spread[pl.ds(k, size, stride=fan), :]
            terms[pl.ds(k * ROUND * size + place * size, size), :] = weights * gmix
        gained = gmix * gain[...]
        gconv = inv_std * (
            gained
            - jnp.mean(gained, axis=-1, keepdims=True)
            - normed * jnp.mean(gained * normed, axis=-1, keepdims=True)
        )
        grad_conv[pl.ds(first, group)] = gconv.reshape(group, cols, channels)
        contract = (((0,), (0,)), ((), ()))
        acc_up[...] += lax.dot_general(mixed, grad_pre, contract, preferred_element_type=f32)
        acc_down[...] += lax.dot_general(grad_out, hidden, contract, preferred_element_type=f32)

    unit = BATCH * BATCHES
    units = terms.shape[0] // unit

    def round_of(index):
        for place in range(ROUND):
            mlp_step(index * ROUND + place, place)
            if index == 0:
                share = table.shape[0] // ROUND
                table[place * share : (place + 1) * share] = jnp.zeros((share, channels), f32)
        if index == 0:
            for copy in scalar_copies:
                copy.wait()

        def add_unit(at, _):
            first_cell = at * (unit // fan)
            first_entry = index * terms.shape[0] + at * unit

            def add_batch(first, count):
                found = []
                for k in range(first, first + count):
                    place = (k % fan) * (ROUND * size) + first_cell + k // fan
                    found.append((targets[first_entry + k], terms[pl.ds(place, 1), :]))
                sums = [table[pl.ds(t, 1), :] + v for t, v in found]
                for (t, _), value in zip(found, sums):
                    table[pl.ds(t, 1), :] = value

            clashing = clash[first_entry]
            for level, count in enumerate((BATCH, SMALL, 1)):

                @pl.when(clashing == level)
                def _():
                    for first in range(0, unit, count):
                        add_batch(first, count)

            return 0

        lax.fori_loop(0, units, add_unit, 0)

    for index in range(rows // (group * ROUND)):
        round_of(index)
    half = table.shape[0] // 2

    keep_copies = [
        pltpu.make_async_copy(table.at[pl.ds(k * (half // 4), half // 4)], keep, sems.at[2 + k])
        for k, keep in enumerate((keep_0, keep_1, keep_2, keep_3))
    ]
    for copy in keep_copies:
        copy.start()

    buffer_rows = outgoing.shape[0]
    for first in range(0, half, buffer_rows):

        def give(at):
            outgoing[at, :] = table[pl.ds(half + first + at.start, at.size), :].astype(bf16)

        in_chunks(buffer_rows, give)
        copy = pltpu.make_async_copy(outgoing, send.at[pl.ds(first, buffer_rows)], sems.at[6])
        copy.start()
        if first + buffer_rows < half:
            copy.wait()
    keep_copies.append(copy)
    blocks = up.shape[1] // channels
    for k in range(blocks):
        part = slice(k * channels, (k + 1) * channels)
        grads[k] = acc_up[:, part]
        grads[blocks + k] = acc_down[:, part].T
    for copy in keep_copies:
        copy.wait()


def find_targets(lat_count, lon_count, orders, owner, cell, targets, clash):
    lat, lon = lax.axis_index("lat"), lax.axis_index("lon")
    lon_bits = lon_count.bit_length() - 1
    half_rows = lat_count * lon_count // 2 * A_DEV
    width = A_DEV // 2
    device = owner[...]
    at_lat = (device >> lon_bits) ^ lat
    at_lon = (device & (lon_count - 1)) ^ lon
    numbers = []
    for order in orders:
        number = jnp.zeros_like(device)
        for bit in order:
            number = number * 2 + ((at_lon >> bit) & 1)
        numbers.append(number * lat_count + at_lat)
    upper = (cell[...] >= width).astype(jnp.int32)
    block = jnp.where(upper == 1, numbers[1], numbers[0])
    row = (at_lon & 1) * half_rows + upper * (half_rows // 2) + block * width
    row = row + cell[...] - upper * width
    targets[...] = row
    lane = lax.broadcasted_iota(jnp.int32, row.shape, 1)
    twice = jnp.zeros_like(row)
    for distance in range(BATCH - 1, 0, -1):
        same = row == pltpu.roll(row, distance, 1)
        twice = jnp.where(same & (lane % BATCH >= distance), jnp.maximum(twice, 1), twice)
        if distance < SMALL:
            twice = jnp.where(same & (lane % SMALL >= distance), 2, twice)
    distance = 1
    while distance < BATCH * BATCHES:
        twice = jnp.maximum(twice, pltpu.roll(twice, row.shape[1] - distance, 1))
        distance *= 2
    clash[...] = twice


def conv_grad_kernel(state, south, north, left, right, grad_conv, out, padded):
    rows, cols, channels = grad_conv.shape
    height = rows + 2 * MARGIN
    fill_rows(padded, state, south, north)
    for h in range(height):
        padded[h, PAD - MARGIN : PAD, :] = left[h].astype(f32)
        padded[h, PAD + cols : PAD + cols + MARGIN, :] = right[h].astype(f32)
    out[...] = jnp.zeros_like(out)
    unroll = 2
    for b in range(TAPS):

        def step_of(step, sums):
            sums = list(sums)
            for u in range(unroll):
                base = pl.multiple_of((step * unroll + u) * 8, 8)
                gc = [grad_conv[r, pl.ds(base, 8), :] for r in range(rows)]
                for h in range(height):
                    x = padded[h, pl.ds(base + (PAD - MARGIN + b), 8), :]
                    for a in range(TAPS):
                        if 0 <= h - a < rows:
                            k = a * 2 + (h - a) % 2
                            sums[k] = sums[k] + gc[h - a] * x
            return tuple(sums)

        zero = jnp.zeros((8, channels), f32)
        sums = lax.fori_loop(0, cols // (8 * unroll), step_of, (zero,) * (2 * TAPS))
        for a in range(TAPS):
            total = sums[2 * a] + sums[2 * a + 1]
            out[pl.ds(a * TAPS + b, 1), :] = jnp.sum(total, axis=0, keepdims=True)


def swap_bit(array, bit):
    pairs = [(i, i ^ (1 << bit)) for i in range(lax.axis_size("lon"))]
    return lax.ppermute(array, "lon", pairs)


def after(array, *others):
    return lax.optimization_barrier((array,) + others)[0]


def on_device(
    state, forcing, cotangent, land_mask, dw_weight, dw_bias, norm_gain, norm_bias,
    up_weight, up_bias, down_weight, down_bias, layer_scale, owner, atmos_cell, weight_index,
    intersection_weights,
):
    rows, cols, channels = state.shape
    cells = rows * cols
    hid = up_weight.shape[1]
    lat_count = lax.axis_size("lat")
    lon_count = lax.axis_size("lon")
    lat = lax.axis_index("lat")
    lon = lax.axis_index("lon")
    lon_bits = lon_count.bit_length() - 1
    devices = lat_count * lon_count
    entries = owner.shape[0]
    fan = entries // cells

    odd = lat % 2 == 1
    even_pairs, odd_pairs = [], []
    for l in range(lat_count):
        for j in range(lon_count):
            here = l * lon_count + j
            even_pairs.append((here, (l ^ 1) * lon_count + j))
            beyond = l + 1 if l % 2 else l - 1
            if 0 <= beyond < lat_count:
                odd_pairs.append((here, beyond * lon_count + j))
            else:
                odd_pairs.append((here, l * lon_count + lon_count - 1 - j))
    edge_rows = shape((MARGIN, cols, channels), bf16)
    for_even, for_odd = pl.pallas_call(
        functools.partial(edge_kernel, bands=lat_count),
        out_shape=(edge_rows, edge_rows),
        in_specs=[vmem()],
        out_specs=[vmem()] * 2,
        compiler_params=params(8),
        cost_estimate=cost(1),
        name="edges",
    )(state)
    got_even = lax.ppermute(for_even, ("lat", "lon"), even_pairs)
    got_odd = lax.ppermute(for_odd, ("lat", "lon"), odd_pairs)
    south = jnp.where(odd, got_even, jnp.where(lat == 0, jnp.zeros_like(got_odd), got_odd))
    north = jnp.where(odd, got_odd, got_even)

    forward = [(i, (i + 1) % lon_count) for i in range(lon_count)]
    backward = [(t, s) for s, t in forward]
    column = lambda part: jnp.concatenate([south[:, part], state[:, part], north[:, part]], axis=0)
    left = lax.ppermute(column(slice(cols - MARGIN, cols)), "lon", forward)
    right = lax.ppermute(column(slice(0, MARGIN)), "lon", backward)

    rest = list(range(1, lon_bits))
    orders = [rest, rest[::-1]]
    width = A_DEV // 2
    half_rows = devices // 2 * A_DEV
    lines = (entries // channels, channels)
    line = lambda v: v.reshape(1, -1)
    taps = dw_weight.reshape(-1, channels).astype(f32)
    conv, targets, clash = pl.pallas_call(
        functools.partial(inner_conv_kernel, lat_count, lon_count, orders),
        out_shape=(shape((rows, cols, channels), f32),) + (shape(lines, jnp.int32),) * 2,
        in_specs=[vmem()] * 5,
        out_specs=[vmem()] * 3,
        scratch_shapes=[pltpu.VMEM((rows, cols + 2 * PAD, channels), f32)],
        compiler_params=params(12),
        cost_estimate=cost(7),
        name="inner_conv",
    )(
        after(state, for_even), taps, line(dw_bias), owner.reshape(lines), atmos_cell.reshape(lines)
    )
    halo = pl.pallas_call(
        functools.partial(halo_conv_kernel, rows=rows),
        out_shape=shape((2 * MARGIN, cols, channels), f32),
        in_specs=[vmem()] * 3,
        out_specs=vmem(),
        scratch_shapes=[pltpu.VMEM((2 * MARGIN, cols + 2 * PAD, channels), f32)],
        compiler_params=params(8),
        cost_estimate=cost(2),
        name="halo_conv",
    )(south, north, taps)
    quarter = shape((half_rows // 4, channels), f32)
    result, *keep, send, grad_conv, grads = pl.pallas_call(
        block_kernel,
        out_shape=(
            shape((rows, cols, channels), bf16),
            *(quarter,) * 4,
            shape((half_rows, channels), bf16),
            shape((rows, cols, channels), f32),
            shape((2 * hid // channels, channels, channels), f32),
        ),
        in_specs=[vmem()] * 11 + [smem()] + [anywhere()] * 2 + [vmem()] * 11,
        out_specs=[vmem()] + [anywhere()] * 5 + [vmem()] * 2,
        scratch_shapes=[
            pltpu.VMEM((rows, cols, channels), f32),
            pltpu.VMEM((2, rows + 2 * MARGIN, 24, channels), f32),
            pltpu.VMEM((channels, hid), f32),
            pltpu.VMEM((channels, hid), f32),
            pltpu.VMEM((rows // 2, 2 * entries // rows // channels, channels), f32),
            pltpu.VMEM((2 * fan * cols, channels), f32),
            pltpu.VMEM((ROUND * 2 * fan * cols, channels), f32),
            pltpu.VMEM((2 * half_rows, channels), f32),
            pltpu.VMEM((min(half_rows, 8192), channels), bf16),
            pltpu.SMEM((entries,), jnp.int32),
            pltpu.SMEM((entries,), jnp.int32),
            pltpu.SemaphoreType.DMA((7,)),
        ],
        compiler_params=params(min(60, 28 + (half_rows * channels * 10 >> 20))),
        cost_estimate=cost(28),
        name="block",
    )(
        state, south, north, left, right, conv, halo, forcing, cotangent, land_mask,
        weight_index.reshape(-1, channels), intersection_weights,
        targets.reshape(-1), clash.reshape(-1), taps, line(dw_bias), line(norm_gain), line(norm_bias), up_weight, line(up_bias),
        down_weight, line(down_bias), line(layer_scale), up_weight.T, down_weight.T,
    )

    got = swap_bit(send, 0)

    tap_count = dw_weight.shape[0] * dw_weight.shape[1]
    dw_rows = -(-tap_count // devices) * devices
    grad_dw = pl.pallas_call(
        conv_grad_kernel,
        out_shape=shape((dw_rows, channels), f32),
        in_specs=[vmem()] * 6,
        out_specs=vmem(),
        scratch_shapes=[pltpu.VMEM((rows + 2 * MARGIN, cols + 2 * PAD, channels), f32)],
        compiler_params=params(16),
        cost_estimate=cost(9),
        name="conv_grad",
    )(state, south, north, left, right, after(grad_conv, send))

    size = half_rows // 4
    got = after(got, grad_dw)
    slices = [(keep[k], got[k * size : (k + 1) * size]) for k in range(4)]
    add = lambda summands: functools.reduce(lambda x, y: x + y.astype(f32), summands)
    sends = [add(slices[1]).astype(bf16), add(slices[3]).astype(bf16)]
    first_sends = sends
    held = [list(slices[0]), list(slices[2])]
    for stage in range(len(rest)):
        arrived = [swap_bit(sends[q], orders[q][stage]) for q in range(2)]
        arrived = lax.optimization_barrier(tuple(arrived))
        for q in range(2):
            held[q].append(arrived[q])
        if stage + 1 < len(rest):
            size //= 2
            sends = [add([h[size : 2 * size] for h in held[q]]).astype(bf16) for q in range(2)]
            held = [[h[:size] for h in held[q]] for q in range(2)]
    def for_band(distance):
        at = slice(distance * width, (distance + 1) * width)
        return jnp.concatenate([add([h[at] for h in held[q]]) for q in range(2)], axis=0)

    sends = [for_band(distance).astype(bf16) for distance in range(1, lat_count)]
    from_bands = []
    for distance in range(1, lat_count):
        pairs = [(i, i ^ distance) for i in range(lat_count)]
        from_bands.append(lax.ppermute(sends[distance - 1], "lat", pairs))
    held, _ = lax.optimization_barrier((held, sends))
    forcing_grad = for_band(0)

    total = jnp.concatenate([grads.reshape(2 * hid, channels), grad_dw], axis=0).astype(bf16)
    total = after(total, *first_sends)
    total = total.reshape(devices, -1, channels)
    total = lax.all_to_all(total, ("lat", "lon"), split_axis=0, concat_axis=0, tiled=True)
    total = jnp.sum(total.astype(f32), axis=0, keepdims=True).astype(bf16)
    total = jnp.broadcast_to(total, (devices,) + total.shape[1:])
    total = lax.all_to_all(total, ("lat", "lon"), split_axis=0, concat_axis=0, tiled=True)
    scale = float(cells * devices) ** (-0.5)
    total = total.reshape(-1, channels).astype(f32) * scale
    grad_up = total[:hid].reshape(hid // channels, channels, channels)
    grad_up = grad_up.transpose(1, 0, 2).reshape(channels, hid)
    grad_down = total[hid : 2 * hid]
    grad_dw = total[2 * hid : 2 * hid + tap_count].reshape(dw_weight.shape)
    arrived, grad_dw, grad_up, grad_down = lax.optimization_barrier(
        (from_bands, grad_dw, grad_up, grad_down)
    )
    forcing_grad = add([forcing_grad] + list(arrived))
    return (result, grad_dw, grad_up, grad_down, forcing_grad)


def solution(mesh):
    grid = P("lat", "lon", None)
    in_specs = (grid, grid, grid, P("lat", "lon")) + (P(),) * 9
    in_specs += (P(("lat", "lon"), None), P(("lat", "lon")), P(("lat", "lon")), P())
    out_specs = (grid, P(), P(), P(), P(("lat", "lon"), None))
    return jax.shard_map(
        on_device, mesh=mesh, in_specs=in_specs, out_specs=out_specs, check_vma=False
    )
```
